32 devices in a mesh: task: 4 (over y, x), dp: 8 (over z, core).
Axes of the slice: x: 2, y: 2, z: 4, core: 2. Of those that a mesh axis runs over, the one named last changes fastest.
Arguments:
- images: bfloat16 [64, 16, 18, 2048], P(('task', 'dp')), may hold values from -6 to 6
- sizes: int32 [64, 2], P(('task', 'dp')), may hold values from 5 to 18, as said below
- thresholds: bfloat16 [64, 16, 18, 2048], P(('task', 'dp')), may hold values from 0 to 1
- head_grad: bfloat16 [64, 16, 18, 768], P(('task', 'dp')), may hold values from -6 to 6
- w_reduce: bfloat16 [2048, 512], replicated, may hold values from -0.125 to 0.125
- w_spatial: bfloat16 [3, 3, 512, 512], replicated, may hold values from -0.09375 to 0.09375
- w_expand: bfloat16 [512, 2048], replicated, may hold values from -0.25 to 0.25
- w_heads: bfloat16 [2048, 768], replicated, may hold values from -0.125 to 0.125
- gain_a: float32 [512], replicated, may hold values from 0.5 to 1.5
- shift_a: float32 [512], replicated, may hold values from -2 to 2
- gain_b: float32 [512], replicated, may hold values from 0.5 to 1.5
- shift_b: float32 [512], replicated, may hold values from -2 to 2
- gain_c: float32 [2048], replicated, may hold values from 0.5 to 1.5
- shift_c: float32 [2048], replicated, may hold values from -2 to 2
Outputs:
- head_out: bfloat16 [64, 16, 18, 768], P(('task', 'dp'))
- grad_images: bfloat16 [64, 16, 18, 2048], P(('task', 'dp'))
- grad_reduce: float32 [2048, 512], replicated
- grad_spatial: float32 [3, 3, 512, 512], replicated
- grad_expand: float32 [512, 2048], replicated
- grad_heads: float32 [2048, 768], replicated
- grad_gain_a: float32 [512], replicated
- grad_shift_a: float32 [512], replicated
- grad_gain_b: float32 [512], replicated
- grad_shift_b: float32 [512], replicated
- grad_gain_c: float32 [2048], replicated
- grad_shift_c: float32 [2048], replicated
The draws below stay inside these ranges and needn't reach their ends.
Inputs may be any that keep to these rules, and one draw needn't show every extreme that they name: `sizes`: each image's valid height is at most 16 and width at most 18; the last image is full and the first has height 16 // 3.
All inputs are finite; a program needn't handle non-finite values.
Results may differ from the reference program's by a relative error of at most 0.0095.
Values may be sent and summed in bfloat16 or wider, within the bound.
A program may use at most 192 MiB of HBM per device.

```python
import jax
import jax.numpy as jnp
from jax import lax

WIDE = 2048
MID = 512
HEAD = 256
TASKS = 3
HP = 16
WP = 18
IMAGES = 64


def draw_sizes(key, part):
    key = jax.random.fold_in(key, 7)
    row_key, col_key = jax.random.split(key)
    index = jnp.arange(IMAGES, dtype=jnp.int32)
    low_rows = HP // 3 + index * (HP - HP // 3) // IMAGES
    low_cols = WP // 3 + index * (WP - WP // 3) // IMAGES
    heights = jax.random.randint(row_key, (IMAGES,), 0, 1048576) % (HP - low_rows + 1) + low_rows
    widths = jax.random.randint(col_key, (IMAGES,), 0, 1048576) % (WP - low_cols + 1) + low_cols
    heights = heights.at[0].set(HP // 3).at[IMAGES - 1].set(HP)
    widths = widths.at[IMAGES - 1].set(WP)
    return jnp.stack([heights, widths], axis=1).astype(jnp.int32)


def shard_levels(rng, dims, cuts, least, high):
    def one(axis_at, shards_of):
        steps = jax.random.uniform(jax.random.fold_in(jax.random.fold_in(rng, 6), axis_at), (shards_of,), jnp.float32, least / len(cuts), high / len(cuts))
        return jnp.repeat(jnp.exp(steps), dims[axis_at] // shards_of).reshape((-1,) + (1,) * (len(dims) - axis_at - 1))

    factor_of = one(*cuts[0])
    for cut in cuts[1:]:
        factor_of = factor_of * one(*cut)
    return factor_of


def scatter_about(key, shape, scale, bound, shards=(), held_as=jnp.bfloat16):
    array = jax.random.normal(key, shape, jnp.float32) * scale
    if len(shards) > 0:
        array = shard_levels(key, shape, shards, -0.22, 0.18) * array
    return jnp.clip(array, min=-bound, max=bound).astype(held_as)


def setup_inputs(seed: int = 0) -> dict:
    keys = jax.random.split(jax.random.key(seed), 15)
    images = scatter_about(keys[0], (IMAGES, HP, WP, WIDE), 1.0, 6.0, ((0, 32),))
    sizes = draw_sizes(jax.random.fold_in(keys[14], 71), 0)
    thresholds = jnp.clip(1.0 * jax.random.uniform(keys[2], (IMAGES, HP, WP, WIDE), jnp.float32) ** shard_levels(keys[2], (IMAGES, HP, WP, WIDE), ((0, 32),), -0.2, 0.2), 0.0, 1.0).astype(jnp.bfloat16)
    head_grad = scatter_about(keys[3], (IMAGES, HP, WP, TASKS * HEAD), 1.0, 6.0, ((0, 32),))
    w_reduce = scatter_about(keys[4], (WIDE, MID), WIDE ** -0.5, 0.125)
    w_spatial = scatter_about(keys[5], (3, 3, MID, MID), (9 * MID) ** -0.5, 0.09375)
    w_expand = scatter_about(keys[6], (MID, WIDE), MID ** -0.5, 0.25)
    w_heads = scatter_about(keys[7], (WIDE, TASKS * HEAD), WIDE ** -0.5, 0.125)
    gain_a = jnp.clip(1.0 + 0.1 * jax.random.normal(keys[8], (MID,), jnp.float32), 0.5, 1.5)
    shift_a = scatter_about(keys[9], (MID,), 0.3, 2.0, (), jnp.float32)
    gain_b = jnp.clip(1.0 + 0.1 * jax.random.normal(keys[10], (MID,), jnp.float32), 0.5, 1.5)
    shift_b = scatter_about(keys[11], (MID,), 0.3, 2.0, (), jnp.float32)
    gain_c = jnp.clip(1.0 + 0.1 * jax.random.normal(keys[12], (WIDE,), jnp.float32), 0.5, 1.5)
    shift_c = scatter_about(keys[13], (WIDE,), 0.3, 2.0, (), jnp.float32)
    return dict(images=images, sizes=sizes, thresholds=thresholds, head_grad=head_grad, w_reduce=w_reduce, w_spatial=w_spatial, w_expand=w_expand, w_heads=w_heads, gain_a=gain_a, shift_a=shift_a, gain_b=gain_b, shift_b=shift_b, gain_c=gain_c, shift_c=shift_c)


@jax.custom_vjp
def low(v):
    return lax.optimization_barrier(v.astype(jnp.bfloat16)).astype(jnp.float32)

@jax.custom_vjp
def low_back(v):
    return v

def low_keep(v):
    return (low(v), None)

def low_pass(kept, grad):
    return (grad,)

def back_keep(v):
    return (v, None)

def back_low(kept, grad):
    return (low(grad),)
low.defvjp(low_keep, low_pass)
low_back.defvjp(back_keep, back_low)
EPS = 1e-05
SOFT = 0.01
TEMP = 0.1
HIGH = lax.Precision.HIGHEST

def grid_mask(sizes):
    row_index = jnp.arange(HP, dtype=jnp.int32)[None, :, None]
    col_index = jnp.arange(WP, dtype=jnp.int32)[None, None, :]
    inside = (row_index < sizes[:, 0, None, None]) & (col_index < sizes[:, 1, None, None])
    return inside.astype(jnp.float32)

def normalize(values, gain, shift, valid, count):
    summed = lax.optimization_barrier(jnp.sum(values * valid, axis=(0, 1, 2)))
    square = lax.optimization_barrier(jnp.sum(values * values * valid, axis=(0, 1, 2)))
    center = summed / count
    inverse = lax.rsqrt(square / count - center * center + EPS)
    return (values - center) * inverse * gain + shift

def graddrop(task_grads, limits):
    signed = lax.optimization_barrier(jnp.sum(task_grads, axis=0))
    magnitude = lax.optimization_barrier(jnp.sum(jnp.sqrt(task_grads * task_grads + SOFT), axis=0))
    purity = 0.5 * (1.0 + signed / magnitude)
    keep = jax.nn.sigmoid((purity - limits) / TEMP) * jax.nn.sigmoid(task_grads / TEMP) + jax.nn.sigmoid((limits - purity) / TEMP) * jax.nn.sigmoid(-task_grads / TEMP)
    return lax.optimization_barrier(jnp.sum(keep * task_grads, axis=0))

def reference(images, sizes, thresholds, head_grad, w_reduce, w_spatial, w_expand, w_heads, gain_a, shift_a, gain_b, shift_b, gain_c, shift_c):
    valid = grid_mask(sizes)[..., None]
    count = jnp.sum(valid)

    def trunk(inputs, reduce_w, spatial_w, expand_w, ga, sa, gb, sb, gc, sc):
        masked = inputs * valid
        first = low_back(jnp.einsum('ihwc,cd->ihwd', low(masked), reduce_w, precision=HIGH))
        hidden_a = jax.nn.silu(normalize(first, ga, sa, valid, count)) * valid
        second = low_back(lax.conv_general_dilated(low(hidden_a), spatial_w, (1, 1), 'SAME', dimension_numbers=('NHWC', 'HWIO', 'NHWC'), precision=HIGH))
        hidden_b = jax.nn.silu(normalize(second, gb, sb, valid, count)) * valid
        third = low_back(jnp.einsum('ihwc,cd->ihwd', low(hidden_b), expand_w, precision=HIGH))
        return jax.nn.silu(normalize(third, gc, sc, valid, count) + masked) * valid
    floats = (images.astype(jnp.float32), w_reduce.astype(jnp.float32), w_spatial.astype(jnp.float32), w_expand.astype(jnp.float32), gain_a, shift_a, gain_b, shift_b, gain_c, shift_c)
    trunk_out, trunk_back = jax.vjp(trunk, *floats)
    heads_f = w_heads.astype(jnp.float32)
    grad_f = head_grad.astype(jnp.float32)

    def head(features, matrix):
        return jnp.einsum('ihwc,cd->ihwd', low(features), matrix, precision=HIGH)
    outputs = []
    task_grads = []
    head_parts = []
    for task in range(TASKS):
        columns = heads_f[:, task * HEAD:(task + 1) * HEAD]
        value, head_back = jax.vjp(head, trunk_out, columns)
        grad_feat, grad_cols = head_back(grad_f[..., task * HEAD:(task + 1) * HEAD])
        outputs.append(value)
        task_grads.append(low(grad_feat))
        head_parts.append(grad_cols)
    head_out = jnp.concatenate(outputs, axis=-1).astype(jnp.bfloat16)
    merged = graddrop(jnp.stack(task_grads), thresholds.astype(jnp.float32))
    grads = trunk_back(merged)
    return (head_out, grads[0].astype(jnp.bfloat16), grads[1], grads[2], grads[3], jnp.concatenate(head_parts, axis=1), grads[4], grads[5], grads[6], grads[7], grads[8], grads[9])
```

```python
import functools

import jax
import jax.numpy as jnp
from jax import lax
from jax.experimental import pallas as pl
from jax.experimental.pallas import tpu as pltpu
from jax.sharding import PartitionSpec as P

TASKS = 3
EPS = 1e-05
SOFT = 0.01
MESH = pl.DeviceIdType.MESH
F32 = jnp.float32
LOW = jnp.bfloat16
NT = (((1,), (1,)), ((), ()))
TN = (((0,), (0,)), ((), ()))
SEGMENTS = ("heads", "expand", "spatial", "reduce")


class Plan:
    def __init__(self, mesh, images, w_reduce, w_heads):
        self.tasks = mesh.shape["task"]
        self.dp = mesh.shape["dp"]
        self.line = self.dp // 2
        self.devices = self.tasks * self.dp
        assert self.tasks == 4 and self.dp % 2 == 0
        self.count, self.height, self.span, self.wide = images.shape
        assert self.height & (self.height - 1) == 0 and self.height % 16 == 0
        self.mid = w_reduce.shape[1]
        self.heads = w_heads.shape[1]
        self.image = self.height * self.span
        self.cells = self.count * self.image
        self.step = self.image + self.height
        self.rows = self.count * self.step - self.height
        self.both = 2 * self.count * self.step - self.height
        self.half = self.wide // 2
        unit = self.tasks * self.line * 16
        real = {
            "heads": self.heads // 256 * self.half,
            "expand": self.half // 256 * self.mid,
            "spatial": 9 * self.mid,
            "reduce": self.mid // 256 * self.half,
        }
        self.real = real
        self.size = {k: -(-real[k] // unit) * unit for k in SEGMENTS}
        self.base, at = {}, 0
        for k in SEGMENTS:
            self.base[k] = at
            at += self.size[k]
        self.total = at


def chunk_of(rows):
    for size in (128, 96, 64, 48, 32, 16):
        if rows % size == 0:
            return size
    raise ValueError(rows)


def column_sum(values):
    return jnp.sum(values.reshape(values.shape[0] // 8, 8, values.shape[1]), axis=0)


def fold(part):
    return jnp.sum(part, axis=0, keepdims=True)


def logistic(values):
    return 0.5 + 0.5 * jnp.tanh(0.5 * values)


def lanes(block, width=128):
    return pl.ds(pl.multiple_of(block * width, width), width)


def span16(start, size):
    return pl.ds(pl.multiple_of(start, 16), size)


def repeat(count, body):
    def step(i, carry):
        body(i)
        return carry

    lax.fori_loop(0, count, step, 0)


def block_kernel(
    plan,
    images,
    sizes,
    limits,
    head_grad,
    w_reduce,
    w_spatial,
    w_expand,
    w_heads,
    gain_a,
    shift_a,
    gain_b,
    shift_b,
    gain_c,
    shift_c,
    head_out,
    grad_images,
    gathered,
    gain_a_grad,
    shift_a_grad,
    gain_b_grad,
    shift_b_grad,
    gain_c_grad,
    shift_c_grad,
    *scratch,
):
    (
        img,
        wr,
        ws,
        we,
        wh,
        hg,
        trunk,
        sib_one,
        sib_two,
        img_t,
        merged,
        third,
        first,
        second,
        back,
        hid_a,
        hid_b,
        hid_b_t,
        low_b,
        low_b_all,
        low_a,
        gsc,
        stage,
        mask,
        coef,
        msg,
        slots,
        wide_msg,
        wide_slots,
        total,
        terms,
        recv_one,
        recv_two,
        recv_three,
        load_sem,
        out_sem,
        sum_send,
        sum_recv,
        sib_send,
        sib_recv,
        ring_send,
        ring_recv,
        keep_sem,
    ) = scratch
    p = plan
    n_img, height, image, step = p.count, p.height, p.image, p.step
    cells, rows, mid, wide, half = p.cells, p.rows, p.mid, p.wide, p.half
    mid_blocks, wide_blocks = mid // 128, wide // 128
    task = lax.axis_index("task")
    dp = lax.axis_index("dp")
    core = lax.rem(dp, 2)
    level = dp // 2
    me = task * p.dp + dp
    sibling = {"task": task, "dp": dp + 1 - 2 * core}

    def remote(src, dst, send, recv, device):
        return pltpu.make_async_remote_copy(
            src_ref=src, dst_ref=dst, send_sem=send, recv_sem=recv, device_id=device, device_id_type=MESH
        )

    def take(ref, sem):
        pltpu.make_async_copy(ref, ref, sem).wait()

    barrier = pltpu.get_barrier_semaphore()

    def greet(i):
        other = lax.rem(me + 1 + i, p.devices)
        pl.semaphore_signal(
            barrier,
            inc=1,
            device_id={"task": other // p.dp, "dp": lax.rem(other, p.dp)},
            device_id_type=MESH,
        )

    repeat(p.devices - 1, greet)

    loads = {
        "images": (images, img),
        "reduce": (w_reduce, wr),
        "grad": (head_grad, hg.at[pl.ds(0, cells)]),
        "heads": (w_heads, wh),
        "limits": (limits, trunk),
        "expand": (w_expand, we),
    }
    order = list(loads)
    for i, key in enumerate(order):
        pltpu.make_async_copy(*loads[key], load_sem.at[i]).start()
    for row_tap in range(3):
        for col_tap in range(3):
            pltpu.make_async_copy(
                w_spatial.at[row_tap * 3 + col_tap],
                ws.at[col_tap, pl.ds(row_tap * mid, mid)],
                load_sem.at[len(order)],
            ).start()

    def loaded(key):
        pltpu.make_async_copy(*loads[key], load_sem.at[order.index(key)]).wait()

    mask[...] = jnp.zeros_like(mask)
    for k in range(n_img):
        at = lax.broadcasted_iota(jnp.int32, (image, 128), 0)
        inside = ((at & (height - 1)) < sizes[k, 0]) & ((at // height) < sizes[k, 1])
        mask[pl.ds(k * step, image)] = jnp.where(inside, 1.0, 0.0)
    zero_rows = jnp.zeros((height, 3 * mid), LOW)
    for k in range(2 * n_img + 1):
        hid_a[pl.ds(k * step, height)] = zero_rows
    for k in range(n_img + 1):
        low_b[pl.ds(k * step, height)] = zero_rows
    low_b_all[pl.ds(rows, height)] = jnp.zeros((height, mid // 2), LOW)

    def sum_start(k, slot):
        slots[slot, me] = msg[k]

        def send(i):
            other = lax.rem(me + 1 + i, p.devices)
            remote(
                msg.at[k],
                slots.at[slot, me],
                sum_send.at[k],
                sum_recv.at[k],
                {"task": other // p.dp, "dp": lax.rem(other, p.dp)},
            ).start()

        repeat(p.devices - 1, send)

    def sum_finish(k, slot):
        some = slots.at[slot, pl.ds(0, p.devices - 1)]
        take(some, sum_recv.at[k])
        take(some, sum_send.at[k])
        total[pl.ds(0, 2 * mid_blocks)] = jnp.sum(slots[slot], axis=0)

    plane = 2 * p.tasks
    spot = task * 2 + core

    def wide_start(k):
        wide_slots[k, spot] = wide_msg[k, 0]
        for i in range(1, plane):
            other = lax.rem(spot + i, plane)
            remote(
                wide_msg.at[k, 0],
                wide_slots.at[k, spot],
                sum_send.at[5 + 2 * k],
                sum_recv.at[5 + 2 * k],
                {"task": other // 2, "dp": level * 2 + lax.rem(other, 2)},
            ).start()

    def wide_turn(k):
        some = wide_slots.at[k, pl.ds(0, plane - 1)]
        take(some, sum_recv.at[5 + 2 * k])
        take(some, sum_send.at[5 + 2 * k])
        partial = jnp.sum(wide_slots[k, pl.ds(0, plane)], axis=0)
        wide_msg[k, 1] = partial
        wide_slots[k, plane + level] = partial
        for i in range(1, p.line):
            other = lax.rem(level + i, p.line)
            remote(
                wide_msg.at[k, 1],
                wide_slots.at[k, plane + level],
                sum_send.at[6 + 2 * k],
                sum_recv.at[6 + 2 * k],
                {"task": task, "dp": other * 2 + core},
            ).start()

    def wide_finish(k):
        some = wide_slots.at[k, pl.ds(plane, p.line - 1)]
        take(some, sum_recv.at[6 + 2 * k])
        take(some, sum_send.at[6 + 2 * k])
        total[...] = jnp.sum(wide_slots[k, pl.ds(plane, p.line)], axis=0)

    low_bit, high_bit = lax.rem(task, 2), task // 2
    near = {"task": task + 1 - 2 * low_bit, "dp": dp}
    far = {"task": task + 2 - 4 * high_bit, "dp": dp}
    routes = ((low_bit, high_bit, near, far), (high_bit, low_bit, far, near))

    def ring(name, stage_at, part):
        s = SEGMENTS.index(name)
        return ring_send.at[s, stage_at, part], ring_recv.at[s, stage_at, part]

    def put(name, row, values):
        low = values.astype(LOW)
        at = span16(p.base[name] + row, low.shape[0])
        terms[0, at, :] = low[:, :128]
        terms[1, at, :] = low[:, 128:]

    def add(part, to, others, count):
        size = chunk_of(count)

        def one(i):
            at = span16(to + i * size, size)
            acc = terms[part, at, :].astype(F32)
            for read in others:
                acc = acc + read(i * size, size)
            terms[part, at, :] = acc.astype(LOW)

        repeat(count // size, one)

    def from_one(name, part, start):
        return lambda i, size: recv_one[part, span16(p.base[name] // 2 + start + i, size), :].astype(F32)

    def from_two(name, part):
        return lambda i, size: recv_two[part, span16(p.base[name] // 4 + i, size), :].astype(F32)

    def from_three(name, part, k):
        return lambda i, size: recv_three[
            part, k, span16(p.base[name] // (4 * p.line) + i, size), :
        ].astype(F32)

    def send_one(name):
        size = p.size[name] // 2
        for part, (mine, _, partner, _) in enumerate(routes):
            send, recv = ring(name, 0, part)
            remote(
                terms.at[part, span16(p.base[name] + (1 - mine) * size, size)],
                recv_one.at[part, pl.ds(p.base[name] // 2, size)],
                send,
                recv,
                partner,
            ).start()

    def send_two(name):
        size = p.size[name] // 4
        for part, (mine, then, _, partner) in enumerate(routes):
            send, recv = ring(name, 0, part)
            some = recv_one.at[part, pl.ds(p.base[name] // 2, 2 * size)]
            take(some, recv)
            take(some, send)
            at = p.base[name] + mine * 2 * size + (1 - then) * size
            add(part, at, [from_one(name, part, (1 - then) * size)], size)
            send, recv = ring(name, 1, part)
            remote(
                terms.at[part, span16(at, size)],
                recv_two.at[part, pl.ds(p.base[name] // 4, size)],
                send,
                recv,
                partner,
            ).start()

    def quarter(name, part):
        mine, then, _, _ = routes[part]
        return p.base[name] + (mine * 2 + then) * (p.size[name] // 4)

    def send_three(name):
        size = p.size[name] // 4
        piece = size // p.line
        for part, (mine, then, _, _) in enumerate(routes):
            send, recv = ring(name, 1, part)
            some = recv_two.at[part, pl.ds(p.base[name] // 4, size)]
            take(some, recv)
            take(some, send)
            at = quarter(name, part)
            add(part, at, [from_one(name, part, then * size), from_two(name, part)], size)
            send, recv = ring(name, 2, part)
            for i in range(1, p.line):
                other = lax.rem(level + i, p.line)
                remote(
                    terms.at[part, span16(at + other * piece, piece)],
                    recv_three.at[part, i - 1, pl.ds(p.base[name] // (4 * p.line), piece)],
                    send,
                    recv,
                    {"task": task, "dp": other * 2 + core},
                ).start()

    def home(name, part, start, size):
        return gathered.at[core, part, span16(start, size)]

    def gather_one(name):
        s = SEGMENTS.index(name)
        piece = p.size[name] // 4 // p.line
        for part in range(2):
            send, recv = ring(name, 2, part)
            some = recv_three.at[part, pl.ds(0, p.line - 1), pl.ds(p.base[name] // (4 * p.line), piece)]
            take(some, recv)
            take(some, send)
            at = quarter(name, part) + level * piece
            add(part, at, [from_three(name, part, k) for k in range(p.line - 1)], piece)
            send, recv = ring(name, 3, part)
            mine = terms.at[part, span16(at, piece)]
            for i in range(1, p.line):
                other = lax.rem(level + i, p.line)
                target = {"task": task, "dp": other * 2 + core}
                remote(mine, home(name, part, at, piece), send, recv, target).start()
            pltpu.make_async_copy(mine, home(name, part, at, piece), keep_sem.at[s, part]).start()

    def gather_two(name):
        s = SEGMENTS.index(name)
        size = p.size[name] // 4
        piece = size // p.line
        for part, (_, _, _, partner) in enumerate(routes):
            send, recv = ring(name, 3, part)
            some = recv_three.at[part, pl.ds(0, p.line - 1), pl.ds(p.base[name] // (4 * p.line), piece)]
            take(some, recv)
            take(some, send)
            at = quarter(name, part)
            take(terms.at[part, span16(at, piece)], keep_sem.at[s, part])
            mine = home(name, part, at, size)
            send, recv = ring(name, 4, part)
            remote(mine, mine, send, recv, partner).start()

    def gather_three(name):
        size = p.size[name] // 2
        for part, (mine, _, partner, _) in enumerate(routes):
            send, recv = ring(name, 4, part)
            some = recv_two.at[part, pl.ds(p.base[name] // 4, size // 2)]
            take(some, recv)
            take(some, send)
            ours = home(name, part, p.base[name] + mine * size, size)
            send, recv = ring(name, 5, part)
            remote(ours, ours, send, recv, partner).start()

    def gather_four(name):
        for part in range(2):
            send, recv = ring(name, 5, part)
            some = recv_one.at[part, pl.ds(p.base[name] // 2, p.size[name] // 2)]
            take(some, recv)
            take(some, send)
            send, recv = ring(name, 6, part)
            ours = home(name, part, p.base[name], p.size[name])
            remote(ours, ours, send, recv, sibling).start()

    def gather_end(name):
        for part in range(2):
            send, recv = ring(name, 6, part)
            some = terms.at[part, pl.ds(p.base[name], p.size[name])]
            take(some, send)
            take(some, recv)

    other_half = pl.ds(pl.multiple_of((1 - core) * half, 128), half)
    other_quarter = pl.ds(pl.multiple_of(mid + (1 - core) * (mid // 2), 128), mid // 2)
    swaps = (
        (images.at[:, other_half], sib_one),
        (head_grad, hg.at[pl.ds(cells, cells)]),
        (hid_a.at[pl.ds(height, rows)], hid_a.at[pl.ds(n_img * step + height, rows)]),
        (hid_b.at[pl.ds(0, cells)], hid_b.at[pl.ds(cells, cells)]),
        (trunk.at[:, other_half], sib_two),
        (trunk.at[:, other_half], sib_one),
        (low_b.at[pl.ds(height, rows), other_quarter], low_b_all.at[pl.ds(rows + height, rows)]),
        (low_a.at[pl.ds(0, cells)], low_a.at[pl.ds(cells, cells)]),
    )

    def swap(k):
        src, dst = swaps[k]
        return remote(src, dst, sib_send.at[k], sib_recv.at[k], sibling)

    msg[0] = jnp.broadcast_to(fold(column_sum(mask[...])), (2 * mid_blocks, 128))
    pl.semaphore_wait(barrier, p.devices - 1)
    sum_start(0, 0)
    swap(0).start()
    swap(1).start()

    def put_stats(ref, at, blocks, block, one, two):
        ref[(*at, pl.ds(block, 1))] = fold(one)
        ref[(*at, pl.ds(blocks + block, 1))] = fold(two)

    loaded("images")
    loaded("reduce")

    def first_layer(nb):
        values = jnp.dot(img[...], wr[:, lanes(nb, 256)], preferred_element_type=F32)
        for h in range(2):
            one = two = jnp.zeros((8, 128), F32)
            for k in range(n_img):
                at = pl.ds(k * image, image)
                part = values[k * image : (k + 1) * image, h * 128 : h * 128 + 128]
                part = part * mask[pl.ds(k * step, image)]
                first[at, lanes(2 * nb + h)] = part
                one = one + column_sum(part)
                two = two + column_sum(part * part)
            put_stats(msg, (1,), mid_blocks, 2 * nb + h, one, two)

    repeat(mid // 256, first_layer)
    sum_finish(0, 0)
    count = total[pl.ds(0, 1)]
    sum_start(1, 1)

    loaded("grad")
    loaded("heads")
    loaded("limits")
    head = p.heads // TASKS

    def merge(nb):
        at_wide = pl.ds(pl.multiple_of(nb * 256, 256), 256)
        for t in range(TASKS):
            at_head = pl.ds(t * head, head)
            values = lax.dot_general(
                hg[pl.ds(0, cells), at_head], wh[at_wide, at_head], NT, preferred_element_type=F32
            )
            gsc[t] = values.astype(LOW)

        def drop(i):
            at = span16(i * 64, 64)
            for h in range(2):
                grads = [gsc[t, at, pl.ds(h * 128, 128)].astype(F32) for t in range(TASKS)]
                signed, size, kept = 0.0, 0.0, 0.0
                for g in grads:
                    square = g * g + SOFT
                    signed = signed + g
                    size = size + square * lax.rsqrt(square)
                    kept = kept + jnp.tanh(g * 5.0) * g
                limit = trunk[at, lanes(2 * nb + h)].astype(F32)
                lean = jnp.tanh(2.5 + 2.5 * (signed / size) - 5.0 * limit)
                merged[at, lanes(2 * nb + h)] = 0.5 * (signed + lean * kept)

        repeat(cells // 64, drop)

    repeat(wide // 256, merge)
    swap(0).wait_recv()

    def turn_images(j):
        own = img[:, pl.ds(pl.multiple_of(core * half + j * 128, 128), 128)]
        both = jnp.concatenate([own, sib_one[:, lanes(j)]], axis=0)
        img_t[lanes(j), :] = both.T

    def center(blocks):
        mean = total[pl.ds(0, blocks)] / count
        spread = total[pl.ds(blocks, blocks)] / count - mean * mean + EPS
        coef[0, pl.ds(0, blocks)] = mean
        coef[1, pl.ds(0, blocks)] = lax.rsqrt(spread)

    def row(k, block):
        return coef[k, pl.ds(block, 1)]

    def edges():
        at = lax.broadcasted_iota(jnp.int32, (image, 128), 0) & (height - 1)
        return at != 0, at != height - 1

    def put_shifted(ref, start, block, values, above, below):
        at = pl.ds(start, image)
        up = jnp.where(above, pltpu.roll(values, 1, 0), 0.0)
        down = jnp.where(below, pltpu.roll(values, image - 1, 0), 0.0)
        for h, part in enumerate((up, values, down)):
            ref[at, pl.ds(pl.multiple_of(h * mid + block * 128, 128), 128)] = part.astype(LOW)

    sum_finish(1, 1)
    center(mid_blocks)
    coef[2, pl.ds(0, mid_blocks)] = coef[1, pl.ds(0, mid_blocks)]

    def normalize_a(cb):
        above, below = edges()
        gain, shift = gain_a[pl.ds(cb, 1)], shift_a[pl.ds(cb, 1)]
        for k in range(n_img):
            at = pl.ds(k * image, image)
            hat = (first[at, lanes(cb)] - row(0, cb)) * row(1, cb)
            first[at, lanes(cb)] = hat
            pre = hat * gain + shift
            hidden = pre * logistic(pre) * mask[pl.ds(k * step, image)]
            put_shifted(hid_a, height + k * step, cb, hidden, above, below)

    repeat(mid_blocks, normalize_a)
    swap(2).start()

    take(ws, load_sem.at[len(order)])

    def second_layer(nb):
        values = None
        for j in range(3):
            term = jnp.dot(
                hid_a[pl.ds(j * height, rows)], ws[j, :, lanes(nb, 256)], preferred_element_type=F32
            )
            values = term if values is None else values + term
        for h in range(2):
            part = values[:, h * 128 : h * 128 + 128] * mask[...]
            second[:, lanes(2 * nb + h)] = part
            put_stats(msg, (2,), mid_blocks, 2 * nb + h, column_sum(part), column_sum(part * part))

    repeat(mid // 256, second_layer)
    sum_start(2, 0)
    repeat(half // 128, turn_images)
    sum_finish(2, 0)
    center(mid_blocks)
    coef[3, pl.ds(0, mid_blocks)] = coef[1, pl.ds(0, mid_blocks)]

    def normalize_b(cb):
        gain, shift = gain_b[pl.ds(cb, 1)], shift_b[pl.ds(cb, 1)]
        for k in range(n_img):
            at = pl.ds(k * step, image)
            hat = (second[at, lanes(cb)] - row(0, cb)) * row(1, cb)
            second[at, lanes(cb)] = hat
            pre = hat * gain + shift
            hidden = pre * logistic(pre) * mask[at]
            hid_b[pl.ds(k * image, image), lanes(cb)] = hidden.astype(LOW)

    repeat(mid_blocks, normalize_b)
    swap(3).start()

    loaded("expand")

    def third_layer(nb):
        values = jnp.dot(hid_b[pl.ds(0, cells)], we[:, lanes(nb, 256)], preferred_element_type=F32)
        third[:, lanes(nb, 256)] = values
        for h in range(2):
            part = values[:, h * 128 : h * 128 + 128]
            put_stats(
                wide_msg, (0, 0), wide_blocks, 2 * nb + h, column_sum(part), column_sum(part * part)
            )

    repeat(wide // 256, third_layer)
    wide_start(0)
    swap(3).wait_recv()
    wide_turn(0)

    def turn_hidden(j):
        hid_b_t[lanes(j), :] = hid_b[:, lanes(j)].T

    repeat(mid_blocks, turn_hidden)
    wide_finish(0)
    center(wide_blocks)

    chunk = chunk_of(image)

    def normalize_c(cb):
        gain, shift = gain_c[pl.ds(cb, 1)], shift_c[pl.ds(cb, 1)]
        one = two = jnp.zeros((8, 128), F32)
        for k in range(n_img):
            for r in range(image // chunk):
                at = pl.ds(k * image + r * chunk, chunk)
                valid = mask[pl.ds(k * step + r * chunk, chunk)]
                hat = (third[at, lanes(cb)] - row(0, cb)) * row(1, cb)
                third[at, lanes(cb)] = hat
                pre = hat * gain + shift + img[at, lanes(cb)].astype(F32)
                gate = logistic(pre)
                trunk[at, lanes(cb)] = (pre * gate * valid).astype(LOW)
                up = merged[at, lanes(cb)] * (gate * (1.0 + pre * (1.0 - gate))) * valid
                merged[at, lanes(cb)] = up
                one = one + column_sum(up)
                two = two + column_sum(up * hat)
        put_stats(wide_msg, (1, 0), wide_blocks, cb, one, two)

    repeat(wide_blocks, normalize_c)
    wide_start(1)
    swap(4).start()

    def head_layer(nb):
        values = jnp.dot(trunk[...], wh[:, lanes(nb, 256)], preferred_element_type=F32)
        stage[:, lanes(nb, 256)] = values.astype(LOW)

    repeat(p.heads // 256, head_layer)
    pltpu.make_async_copy(stage, head_out, out_sem.at[0]).start()
    wide_turn(1)
    swap(1).wait_recv()
    swap(4).wait_recv()

    def heads_gradient(j):
        own = trunk[:, pl.ds(pl.multiple_of(core * half + j * 256, 128), 256)]
        both = jnp.concatenate([own, sib_two[:, lanes(j, 256)]], axis=0)
        values = lax.dot_general(both, hg[...], TN, preferred_element_type=F32)
        for b in range(p.heads // 256):
            put("heads", b * half + j * 256, values[:, b * 256 : b * 256 + 256])

    repeat(half // 256, heads_gradient)
    send_one("heads")
    swap(4).wait_send()
    wide_finish(1)

    def backward(blocks, gain, inverse):
        scale = gain * inverse
        coef[4, pl.ds(0, blocks)] = scale
        coef[5, pl.ds(0, blocks)] = -scale * total[pl.ds(0, blocks)] / count
        coef[6, pl.ds(0, blocks)] = -scale * total[pl.ds(blocks, blocks)] / count

    shift_c_grad[...] = total[pl.ds(0, wide_blocks)]
    gain_c_grad[...] = total[pl.ds(wide_blocks, wide_blocks)]
    backward(wide_blocks, gain_c[...], coef[1])

    def third_gradient(cb):
        for k in range(n_img):
            for r in range(image // chunk):
                at = pl.ds(k * image + r * chunk, chunk)
                valid = mask[pl.ds(k * step + r * chunk, chunk)]
                down = merged[at, lanes(cb)] * row(4, cb) + row(5, cb) + third[at, lanes(cb)] * row(6, cb)
                trunk[at, lanes(cb)] = (down * valid).astype(LOW)

    repeat(wide_blocks, third_gradient)
    swap(5).start()

    def slope_of(pre):
        gate = logistic(pre)
        return gate * (1.0 + pre * (1.0 - gate))

    def third_back(nb):
        values = lax.dot_general(trunk[...], we[lanes(nb, 256), :], NT, preferred_element_type=F32)
        for h in range(2):
            cb = 2 * nb + h
            one = two = jnp.zeros((8, 128), F32)
            for k in range(n_img):
                at = pl.ds(k * image, image)
                hat = second[pl.ds(k * step, image), lanes(cb)]
                pre = hat * gain_b[pl.ds(cb, 1)] + shift_b[pl.ds(cb, 1)]
                up = values[k * image : (k + 1) * image, h * 128 : h * 128 + 128]
                up = up * slope_of(pre) * mask[pl.ds(k * step, image)]
                back[at, lanes(cb)] = up
                one = one + column_sum(up)
                two = two + column_sum(up * hat)
            put_stats(msg, (3,), mid_blocks, cb, one, two)

    repeat(mid // 256, third_back)
    sum_start(3, 1)
    send_two("heads")
    swap(5).wait_recv()

    def expand_gradient(j):
        own = trunk[:, pl.ds(pl.multiple_of(core * half + j * 256, 128), 256)]
        both = jnp.concatenate([own, sib_one[:, lanes(j, 256)]], axis=0)
        put("expand", j * mid, jnp.dot(hid_b_t[...], both, preferred_element_type=F32))

    repeat(half // 256, expand_gradient)
    send_one("expand")
    sum_finish(3, 1)
    shift_b_grad[...] = total[pl.ds(0, mid_blocks)]
    gain_b_grad[...] = total[pl.ds(mid_blocks, mid_blocks)]
    backward(mid_blocks, gain_b[...], coef[3, pl.ds(0, mid_blocks)])

    def second_gradient(cb):
        above, below = edges()
        for k in range(n_img):
            at = pl.ds(k * step, image)
            down = back[pl.ds(k * image, image), lanes(cb)] * row(4, cb) + row(5, cb)
            down = (down + second[at, lanes(cb)] * row(6, cb)) * mask[at]
            put_shifted(low_b, height + k * step, cb, down, above, below)

    repeat(mid_blocks, second_gradient)
    swap(6).start()
    own_quarter = pl.ds(pl.multiple_of(mid + core * (mid // 2), 128), mid // 2)
    low_b_all[pl.ds(0, rows)] = low_b[pl.ds(height, rows), own_quarter]

    def second_back(nb):
        values = None
        for i in range(3):
            for j in range(3):
                term = lax.dot_general(
                    low_b[pl.ds((2 - j) * height, rows), pl.ds((2 - i) * mid, mid)],
                    ws[j, pl.ds(pl.multiple_of(i * mid + nb * 256, 256), 256), :],
                    NT,
                    preferred_element_type=F32,
                )
                values = term if values is None else values + term
        for h in range(2):
            cb = 2 * nb + h
            one = two = jnp.zeros((8, 128), F32)
            for k in range(n_img):
                at = pl.ds(k * image, image)
                hat = first[at, lanes(cb)]
                pre = hat * gain_a[pl.ds(cb, 1)] + shift_a[pl.ds(cb, 1)]
                up = values[k * step : k * step + image, h * 128 : h * 128 + 128]
                up = up * slope_of(pre) * mask[pl.ds(k * step, image)]
                back[at, lanes(cb)] = up
                one = one + column_sum(up)
                two = two + column_sum(up * hat)
            put_stats(msg, (4,), mid_blocks, cb, one, two)

    repeat(mid // 256, second_back)
    sum_start(4, 0)
    send_three("heads")
    send_two("expand")
    swap(2).wait_recv()
    swap(6).wait_recv()

    def spatial_gradient(i):
        per = 3 * mid // 256
        j, k = i // per, lax.rem(i, per)
        row_tap, sub = k // (mid // 256), lax.rem(k, mid // 256)
        values = lax.dot_general(
            hid_a[span16(j * height, p.both), lanes(k, 256)],
            low_b_all[...],
            TN,
            preferred_element_type=F32,
        )
        put("spatial", (row_tap * 3 + j) * mid + sub * 256, values)

    repeat(9 * mid // 256, spatial_gradient)
    send_one("spatial")
    sum_finish(4, 0)
    shift_a_grad[...] = total[pl.ds(0, mid_blocks)]
    gain_a_grad[...] = total[pl.ds(mid_blocks, mid_blocks)]
    backward(mid_blocks, gain_a[...], coef[2, pl.ds(0, mid_blocks)])

    def first_gradient(cb):
        for k in range(n_img):
            at = pl.ds(k * image, image)
            down = back[at, lanes(cb)] * row(4, cb) + row(5, cb) + first[at, lanes(cb)] * row(6, cb)
            low_a[at, lanes(cb)] = (down * mask[pl.ds(k * step, image)]).astype(LOW)

    repeat(mid_blocks, first_gradient)
    swap(7).start()
    gather_one("heads")
    send_three("expand")
    swap(7).wait_recv()

    def reduce_gradient(i):
        j, b = i // (mid // 256), lax.rem(i, mid // 256)
        values = jnp.dot(img_t[lanes(j, 256), :], low_a[:, lanes(b, 256)], preferred_element_type=F32)
        put("reduce", b * half + j * 256, values)

    repeat(half // 256 * (mid // 256), reduce_gradient)
    send_one("reduce")
    send_two("spatial")

    def first_back(nb):
        values = lax.dot_general(low_a[pl.ds(0, cells)], wr[lanes(nb, 256), :], NT, preferred_element_type=F32)
        for h in range(2):
            for k in range(n_img):
                at = pl.ds(k * image, image)
                part = values[k * image : (k + 1) * image, h * 128 : h * 128 + 128]
                part = (part + merged[at, lanes(2 * nb + h)]) * mask[pl.ds(k * step, image)]
                img[at, lanes(2 * nb + h)] = part.astype(LOW)

    repeat(wide // 256, first_back)
    pltpu.make_async_copy(img, grad_images, out_sem.at[1]).start()

    gather_two("heads")
    gather_one("expand")
    send_two("reduce")
    gather_three("heads")
    gather_two("expand")
    send_three("spatial")
    gather_four("heads")
    send_three("reduce")
    gather_three("expand")
    gather_one("spatial")
    gather_four("expand")
    gather_one("reduce")
    gather_two("spatial")
    gather_two("reduce")
    gather_three("spatial")
    gather_three("reduce")
    gather_four("spatial")
    gather_four("reduce")
    for name in SEGMENTS:
        gather_end(name)
    pltpu.make_async_copy(stage, head_out, out_sem.at[0]).wait()
    pltpu.make_async_copy(img, grad_images, out_sem.at[1]).wait()
    for k in (0, 1, 2, 3, 5, 6, 7):
        swap(k).wait_send()


def run_block(plan, *arrays):
    p = plan
    cells, rows, mid, wide, half = p.cells, p.rows, p.mid, p.wide, p.half
    mid_blocks, wide_blocks = mid // 128, wide // 128
    anywhere = pl.BlockSpec(memory_space=pl.ANY)
    vmem = pl.BlockSpec(memory_space=pltpu.VMEM)
    smem = pl.BlockSpec(memory_space=pltpu.SMEM)
    shape = jax.ShapeDtypeStruct
    scratch = [
        pltpu.VMEM((cells, wide), LOW),
        pltpu.VMEM((wide, mid), LOW),
        pltpu.VMEM((3, 3 * mid, mid), LOW),
        pltpu.VMEM((mid, wide), LOW),
        pltpu.VMEM((wide, p.heads), LOW),
        pltpu.VMEM((2 * cells, p.heads), LOW),
        pltpu.VMEM((cells, wide), LOW),
        pltpu.VMEM((cells, half), LOW),
        pltpu.VMEM((cells, half), LOW),
        pltpu.VMEM((half, 2 * cells), LOW),
        pltpu.VMEM((cells, wide), F32),
        pltpu.VMEM((cells, wide), F32),
        pltpu.VMEM((cells, mid), F32),
        pltpu.VMEM((rows, mid), F32),
        pltpu.VMEM((cells, mid), F32),
        pltpu.VMEM((p.both + 2 * p.height, 3 * mid), LOW),
        pltpu.VMEM((2 * cells, mid), LOW),
        pltpu.VMEM((mid, 2 * cells), LOW),
        pltpu.VMEM((rows + 2 * p.height, 3 * mid), LOW),
        pltpu.VMEM((p.both, mid // 2), LOW),
        pltpu.VMEM((2 * cells, mid), LOW),
        pltpu.VMEM((TASKS, cells, 256), LOW),
        pltpu.VMEM((cells, p.heads), LOW),
        pltpu.VMEM((rows, 128), F32),
        pltpu.VMEM((7, wide_blocks, 128), F32),
        pltpu.VMEM((5, 2 * mid_blocks, 128), F32),
        pltpu.VMEM((2, p.devices, 2 * mid_blocks, 128), F32),
        pltpu.VMEM((2, 2, 2 * wide_blocks, 128), F32),
        pltpu.VMEM((2, 2 * p.tasks + p.line, 2 * wide_blocks, 128), F32),
        pltpu.VMEM((2 * wide_blocks, 128), F32),
        pltpu.VMEM((2, p.total, 128), LOW),
        pltpu.VMEM((2, p.total // 2, 128), LOW),
        pltpu.VMEM((2, p.total // 4, 128), LOW),
        pltpu.VMEM((2, p.line - 1, p.total // (4 * p.line), 128), LOW),
        pltpu.SemaphoreType.DMA((7,)),
        pltpu.SemaphoreType.DMA((2,)),
        pltpu.SemaphoreType.DMA((9,)),
        pltpu.SemaphoreType.DMA((9,)),
        pltpu.SemaphoreType.DMA((8,)),
        pltpu.SemaphoreType.DMA((8,)),
        pltpu.SemaphoreType.DMA((4, 7, 2)),
        pltpu.SemaphoreType.DMA((4, 7, 2)),
        pltpu.SemaphoreType.DMA((4, 2)),
    ]
    return pl.pallas_call(
        functools.partial(block_kernel, plan),
        out_shape=(
            shape((cells, p.heads), LOW),
            shape((cells, wide), LOW),
            shape((2, 2, p.total, 128), LOW),
            shape((mid_blocks, 128), F32),
            shape((mid_blocks, 128), F32),
            shape((mid_blocks, 128), F32),
            shape((mid_blocks, 128), F32),
            shape((wide_blocks, 128), F32),
            shape((wide_blocks, 128), F32),
        ),
        in_specs=[anywhere, smem] + [anywhere] * 6 + [vmem] * 6,
        out_specs=[anywhere] * 3 + [vmem] * 6,
        scratch_shapes=scratch,
        compiler_params=pltpu.CompilerParams(
            collective_id=0, has_side_effects=True, vmem_limit_bytes=63 * 2**20
        ),
        name="block",
    )(*arrays)


def widen_kernel(plan, *refs):
    p = plan
    gathered, heads_in, images_in = refs[:3]
    small_in = refs[3:9]
    heads_out, images_out, out_reduce, out_spatial, out_expand, out_heads = refs[9:15]
    small_out = refs[15:21]
    low, reduce, spatial, expand, heads, heads_low, images_low, load_sem, out_sem, pass_sem = refs[21:]
    fetches = (
        pltpu.make_async_copy(heads_in, heads_low, pass_sem.at[0, 0]),
        pltpu.make_async_copy(images_in, images_low, pass_sem.at[1, 0]),
    )
    passes = (
        pltpu.make_async_copy(heads_low, heads_out, pass_sem.at[0, 1]),
        pltpu.make_async_copy(images_low, images_out, pass_sem.at[1, 1]),
    )
    for one in fetches:
        one.start()
    loads = []
    for s, name in enumerate(SEGMENTS):
        for core in range(2):
            at = (core, slice(None), pl.ds(p.base[name], p.real[name]))
            load = pltpu.make_async_copy(gathered.at[at], low.at[at], load_sem.at[s, core])
            load.start()
            loads.append(load)
    for fetch, one in zip(fetches, passes):
        fetch.wait()
        one.start()
    for src, dst in zip(small_in, small_out):
        dst[...] = src[...]
    where = {
        "heads": (heads, out_heads, p.half, p.heads, True),
        "expand": (expand, out_expand, p.mid, p.half, False),
        "spatial": (spatial, out_spatial, 9 * p.mid, p.mid // 2, False),
        "reduce": (reduce, out_reduce, p.half, p.mid, True),
    }
    copies = []
    for s, name in enumerate(SEGMENTS):
        wide, out, height, width, by_rows = where[name]
        for core in range(2):
            loads[2 * s + core].wait()
            size = 256
            row_at = core * height if by_rows else 0
            col_at = 0 if by_rows else core * width

            def one(i, name=name, wide=wide, out=out, row_at=row_at, col_at=col_at, s=s, core=core):
                rows = pl.ds(pl.multiple_of(row_at + i * size, size), size)
                for b in range(width // 256):
                    src = pl.ds(pl.multiple_of(p.base[name] + b * height + i * size, size), size)
                    for part in range(2):
                        cols = pl.ds(col_at + b * 256 + part * 128, 128)
                        wide[rows, cols] = low[core, part, src, :].astype(F32)
                at = (rows, pl.ds(col_at, width))
                pltpu.make_async_copy(wide.at[at], out.at[at], out_sem.at[s, core]).start()

            repeat(height // size, one)
            at = (pl.ds(row_at, height), pl.ds(col_at, width))
            copies.append(pltpu.make_async_copy(wide.at[at], out.at[at], out_sem.at[s, core]))
    for one in copies + list(passes):
        one.wait()


def widen(plan, head_out, grad_images, gathered, *small):
    p = plan
    anywhere = pl.BlockSpec(memory_space=pl.ANY)
    vmem = pl.BlockSpec(memory_space=pltpu.VMEM)
    shape = jax.ShapeDtypeStruct
    full = ((p.wide, p.mid), (9 * p.mid, p.mid), (p.mid, p.wide), (p.wide, p.heads))
    return pl.pallas_call(
        functools.partial(widen_kernel, plan),
        out_shape=(
            shape(head_out.shape, LOW),
            shape(grad_images.shape, LOW),
            *(shape(one, F32) for one in full),
            *(shape(one.shape, F32) for one in small),
        ),
        in_specs=[anywhere] * 3 + [vmem] * 6,
        out_specs=[anywhere] * 6 + [vmem] * 6,
        scratch_shapes=[
            pltpu.VMEM(gathered.shape, LOW),
            *(pltpu.VMEM(one, F32) for one in full),
            pltpu.VMEM(head_out.shape, LOW),
            pltpu.VMEM(grad_images.shape, LOW),
            pltpu.SemaphoreType.DMA((4, 2)),
            pltpu.SemaphoreType.DMA((4, 2)),
            pltpu.SemaphoreType.DMA((2, 2)),
        ],
        compiler_params=pltpu.CompilerParams(vmem_limit_bytes=56 * 2**20),
        name="widen",
    )(gathered, head_out, grad_images, *small)


def solution(mesh):
    cells_spec = P(("task", "dp"), None, None, None)

    def body(
        images,
        sizes,
        limits,
        head_grad,
        w_reduce,
        w_spatial,
        w_expand,
        w_heads,
        gain_a,
        shift_a,
        gain_b,
        shift_b,
        gain_c,
        shift_c,
    ):
        plan = Plan(mesh, images, w_reduce, w_heads)

        def flat(array):
            return array.transpose(0, 2, 1, 3).reshape(plan.cells, array.shape[3])

        def unflat(array):
            full = (plan.count, plan.span, plan.height, array.shape[1])
            return array.reshape(full).transpose(0, 2, 1, 3)

        outs = run_block(
            plan,
            flat(images),
            sizes,
            flat(limits),
            flat(head_grad),
            w_reduce,
            w_spatial.reshape(9, plan.mid, plan.mid),
            w_expand,
            w_heads,
            *(v.reshape(-1, 128) for v in (gain_a, shift_a, gain_b, shift_b, gain_c, shift_c)),
        )
        outs = widen(plan, *outs)
        return (
            unflat(outs[0]),
            unflat(outs[1]),
            outs[2],
            outs[3].reshape(w_spatial.shape),
            outs[4],
            outs[5],
            *(v.reshape(-1) for v in outs[6:]),
        )

    return jax.shard_map(
        body,
        mesh=mesh,
        in_specs=(cells_spec, P(("task", "dp"), None), cells_spec, cells_spec) + (P(),) * 10,
        out_specs=(cells_spec, cells_spec) + (P(),) * 10,
        check_vma=False,
    )
```

```python
import functools

import jax
import jax.numpy as jnp
from jax import lax
from jax.experimental import pallas as pl
from jax.experimental.pallas import tpu as pltpu
from jax.sharding import PartitionSpec as P

TASKS = 3
EPS = 1e-05
SOFT = 0.01
MESH = pl.DeviceIdType.MESH
F32 = jnp.float32
LOW = jnp.bfloat16
NT = (((1,), (1,)), ((), ()))
TN = (((0,), (0,)), ((), ()))
HEADS, EXPAND, SPATIAL, REDUCE = range(4)
PARTS = (4, 2, 6, 4)
ROUTES = (3, 0, 0, 0, 0, 4, 0, 5, 0, 0, 0, 3, 0, 3, 5, 0)
(
    AFTER_HEADS,
    AFTER_THIRD,
    AFTER_BACK_B,
    AFTER_EXPAND,
    AFTER_BACK_A,
    AFTER_FIRST,
    AFTER_REDUCE,
    AFTER_SPATIAL,
    AFTER_HALF,
    LAST,
) = range(100, 110)
AGENDA = {
    0: (0,),
    1: (10,),
    2: (20,),
    3: (30,),
    AFTER_THIRD: (1,),
    AFTER_BACK_B: (11, 21,),
    4: (40,),
    5: (50, 31,),
    AFTER_EXPAND: (2,),
    AFTER_BACK_A: (22, 41, 12,),
    6: (60, 32, 3,),
    7: (70, 51,),
    8: (80,),
    9: (90, 42, 23, 13,),
    AFTER_FIRST: (33,),
    12: (120, 4, 61,),
    13: (130, 52,),
    14: (140,),
    15: (150, 81, 71,),
    10: (100, 43, 91,),
    11: (110, 121, 34, 5,),
    AFTER_SPATIAL: (24, 14, 62,),
    AFTER_HALF: (131,),
    LAST: (
        44, 82, 72, 35, 53, 101, 151, 25, 63, 15, 92, 141, 132, 111, 83, 45, 122, 6, 36, 73, 54, 26, 102, 64,
        152, 16, 142, 133, 93, 37, 55, 112, 27, 84, 17, 143, 46, 123, 38, 113, 7, 74, 103, 28, 65, 153, 134, 18,
        94, 47, 56, 85, 144, 124, 8, 114, 75, 104, 66, 154, 135, 48, 95, 86, 57, 145, 125, 76, 115, 105, 67, 155,
        136, 96, 87, 146, 77, 116, 68, 97, 58, 126, 106, 88, 156, 147, 137, 98, 127, 107, 157, 78, 138, 128, 117, 108,
        148, 158, 118,
    ),
}


class Plan:
    def __init__(self, mesh, images, w_reduce, w_heads):
        self.tasks = mesh.shape["task"]
        self.dp = mesh.shape["dp"]
        self.line = self.dp // 2
        self.devices = self.tasks * self.dp
        assert self.tasks == 4 and self.dp % 2 == 0
        self.count, self.height, self.span, self.wide = images.shape
        assert self.height & (self.height - 1) == 0 and self.height % 16 == 0
        self.mid = w_reduce.shape[1]
        self.heads = w_heads.shape[1]
        self.image = self.height * self.span
        self.cells = self.count * self.image
        self.step = self.image + self.height
        self.rows = self.count * self.step - self.height
        self.both = 2 * self.count * self.step - self.height
        self.half = self.wide // 2
        assert self.line & (self.line - 1) == 0
        self.levels = self.line.bit_length() - 1
        self.steps = 2 + self.levels
        unit = 16 << self.steps
        self.real = (
            self.heads // 256 * self.half,
            self.half // 256 * self.mid,
            9 * self.mid,
            self.mid // 256 * self.half,
        )
        tuned = self.steps == 4 and all(real % (n * unit) == 0 for real, n in zip(self.real, PARTS))
        self.parts = PARTS if tuned else (1, 1, 1, 1)
        self.base, self.first, self.segments, at = [], [], [], 0
        for real, n in zip(self.real, self.parts):
            self.base.append(at)
            self.first.append(len(self.segments))
            size = -(-real // (n * unit)) * unit
            for _ in range(n):
                index = len(self.segments)
                self.segments.append((index, at, size, ROUTES[index] if tuned else 0))
                at += size
        self.total = at
        self.agenda = AGENDA
        if not tuned:
            self.stride = 2 * self.steps + 1
            self.agenda = {i: (self.stride * i,) for i in range(4)}
            self.agenda[LAST] = [self.stride * i + k for k in range(1, self.stride) for i in range(4)]
        else:
            self.stride = 10


def chunk_of(rows):
    for size in (128, 96, 64, 48, 32, 16):
        if rows % size == 0:
            return size
    raise ValueError(rows)


def column_sum(values):
    return jnp.sum(values.reshape(values.shape[0] // 8, 8, values.shape[1]), axis=0)


def fold(part):
    return jnp.sum(part, axis=0, keepdims=True)


def logistic(values):
    return 0.5 + 0.5 * jnp.tanh(0.5 * values)


def lanes(block, width=128):
    return pl.ds(pl.multiple_of(block * width, width), width)


def span16(start, size):
    return pl.ds(pl.multiple_of(start, 16), size)


def repeat(count, body):
    def step(i, carry):
        body(i)
        return carry

    lax.fori_loop(0, count, step, 0)


def block_kernel(
    plan,
    images,
    sizes,
    limits,
    head_grad,
    w_reduce,
    w_spatial,
    w_expand,
    w_heads,
    gain_a,
    shift_a,
    gain_b,
    shift_b,
    gain_c,
    shift_c,
    head_out,
    grad_images,
    gathered,
    gain_a_grad,
    shift_a_grad,
    gain_b_grad,
    shift_b_grad,
    gain_c_grad,
    shift_c_grad,
    *scratch,
):
    (
        img,
        wr,
        ws,
        we,
        wh,
        hg,
        trunk,
        sib_one,
        sib_two,
        img_t,
        merged,
        third,
        first,
        second,
        back,
        hid_a,
        hid_b,
        hid_b_t,
        low_b,
        low_b_all,
        low_a,
        gsc,
        stage,
        mask,
        coef,
        msg,
        slots,
        count_msg,
        count_slots,
        wide_msg,
        wide_slots,
        total,
        terms,
        received,
        load_sem,
        out_sem,
        sum_send,
        sum_recv,
        sib_send,
        sib_recv,
        ring_send,
        ring_recv,
    ) = scratch
    p = plan
    n_img, height, image, step = p.count, p.height, p.image, p.step
    cells, rows, mid, wide, half = p.cells, p.rows, p.mid, p.wide, p.half
    mid_blocks, wide_blocks = mid // 128, wide // 128
    task = lax.axis_index("task")
    dp = lax.axis_index("dp")
    core = lax.rem(dp, 2)
    level = dp // 2
    me = task * p.dp + dp

    def place(at_task, at_dp):
        return {"task": at_task, "dp": at_dp}

    sibling = place(task, dp + 1 - 2 * core)

    def remote(src, dst, send, recv, device):
        return pltpu.make_async_remote_copy(
            src_ref=src, dst_ref=dst, send_sem=send, recv_sem=recv, device_id=device, device_id_type=MESH
        )

    def take(ref, sem):
        pltpu.make_async_copy(ref, ref, sem).wait()

    barrier = pltpu.get_barrier_semaphore()

    def greet(i):
        other = lax.rem(me + 1 + i, p.devices)
        pl.semaphore_signal(
            barrier,
            inc=1,
            device_id=place(other // p.dp, lax.rem(other, p.dp)),
            device_id_type=MESH,
        )

    loads = {
        "images": (images, img),
        "reduce": (w_reduce, wr),
        "grad": (head_grad, hg.at[pl.ds(0, cells)]),
        "heads": (w_heads, wh),
        "limits": (limits, trunk),
        "expand": (w_expand, we),
    }
    order = list(loads)

    def load(key):
        pltpu.make_async_copy(*loads[key], load_sem.at[order.index(key)]).start()

    load("images")
    load("reduce")
    repeat(p.devices - 1, greet)
    for key in order[2:]:
        load(key)
    for row_tap in range(3):
        for col_tap in range(3):
            pltpu.make_async_copy(
                w_spatial.at[row_tap * 3 + col_tap],
                ws.at[col_tap, pl.ds(row_tap * mid, mid)],
                load_sem.at[len(order)],
            ).start()

    def loaded(key):
        pltpu.make_async_copy(*loads[key], load_sem.at[order.index(key)]).wait()

    mask[...] = jnp.zeros_like(mask)
    for k in range(n_img):
        at = lax.broadcasted_iota(jnp.int32, (image, 128), 0)
        inside = ((at & (height - 1)) < sizes[k, 0]) & ((at // height) < sizes[k, 1])
        mask[pl.ds(k * step, image)] = jnp.where(inside, 1.0, 0.0)
    zero_rows = jnp.zeros((height, 3 * mid), LOW)
    for k in range(2 * n_img + 1):
        hid_a[pl.ds(k * step, height)] = zero_rows
    for k in range(n_img + 1):
        low_b[pl.ds(k * step, height)] = zero_rows
    low_b_all[pl.ds(rows, height)] = jnp.zeros((height, mid // 2), LOW)

    def to_all(k, src, dst):
        def send(i):
            other = lax.rem(me + 1 + i, p.devices)
            device = place(other // p.dp, lax.rem(other, p.dp))
            remote(src, dst.at[me], sum_send.at[k], sum_recv.at[k], device).start()

        repeat(p.devices - 1, send)

    def from_all(k, dst):
        some = dst.at[pl.ds(0, p.devices - 1)]
        take(some, sum_recv.at[k])
        take(some, sum_send.at[k])

    def sum_start(k, slot):
        slots[slot, me] = msg[k]
        to_all(k, msg.at[k], slots.at[slot])

    def sum_finish(k, slot):
        from_all(k, slots.at[slot])
        total[pl.ds(0, 2 * mid_blocks)] = jnp.sum(slots[slot], axis=0)

    plane = 2 * p.tasks
    spot = task * 2 + core

    def wide_start(k):
        wide_slots[k, spot] = wide_msg[k, 0]
        for i in range(1, plane):
            other = lax.rem(spot + i, plane)
            remote(
                wide_msg.at[k, 0],
                wide_slots.at[k, spot],
                sum_send.at[5 + 2 * k],
                sum_recv.at[5 + 2 * k],
                place(other // 2, level * 2 + lax.rem(other, 2)),
            ).start()

    def wide_turn(k):
        some = wide_slots.at[k, pl.ds(0, plane - 1)]
        take(some, sum_recv.at[5 + 2 * k])
        take(some, sum_send.at[5 + 2 * k])
        partial = jnp.sum(wide_slots[k, pl.ds(0, plane)], axis=0)
        wide_msg[k, 1] = partial
        wide_slots[k, plane + level] = partial
        for i in range(1, p.line):
            other = lax.rem(level + i, p.line)
            remote(
                wide_msg.at[k, 1],
                wide_slots.at[k, plane + level],
                sum_send.at[6 + 2 * k],
                sum_recv.at[6 + 2 * k],
                place(task, other * 2 + core),
            ).start()

    def wide_finish(k):
        some = wide_slots.at[k, pl.ds(plane, p.line - 1)]
        take(some, sum_recv.at[6 + 2 * k])
        take(some, sum_send.at[6 + 2 * k])
        total[...] = jnp.sum(wide_slots[k, pl.ds(plane, p.line)], axis=0)

    low_bit, high_bit = lax.rem(task, 2), task // 2
    along_x = (low_bit, place(task + 1 - 2 * low_bit, dp))
    along_y = (high_bit, place(task + 2 - 4 * high_bit, dp))
    along_z = []
    for k in range(p.levels):
        bit = lax.rem(level // 2**k, 2)
        along_z.append((bit, place(task, dp + 2 ** (k + 1) - 2 ** (k + 2) * bit)))

    def route(kind, part):
        one, two = (along_x, along_y) if part == 0 else (along_y, along_x)
        return (
            [one, two, *along_z],
            [one, *along_z, two],
            [*along_z, one, two],
            [one, *along_z[:1], two, *along_z[1:]],
            [*along_z[:1], one, *along_z[1:], two],
            [*along_z[:1], one, two, *along_z[1:]],
        )[kind]

    def held(segment, part, k):
        _, at, size, kind = segment
        for j, (bit, _) in enumerate(route(kind, part)[:k]):
            at = at + bit * (size >> (j + 1))
        return at

    def inbox(segment, k):
        _, at, size, _ = segment
        return at + size - (size >> k)

    def put(family, row, values):
        low = values.astype(LOW)
        at = span16(p.base[family] + row, low.shape[0])
        terms[0, at, :] = low[:, :128]
        terms[1, at, :] = low[:, 128:]

    def add_received(segment, part, at, rows_here, k):
        starts = [inbox(segment, j) + at - held(segment, part, j + 1) for j in range(k)]
        size = chunk_of(rows_here)

        def one(i):
            here = span16(at + i * size, size)
            acc = terms[part, here, :].astype(F32)
            for start in starts:
                acc = acc + received[part, span16(start + i * size, size), :].astype(F32)
            terms[part, here, :] = acc.astype(LOW)

        repeat(rows_here // size, one)

    def some_of(segment, rows_here):
        return received.at[:, pl.ds(segment[1], rows_here)]

    def settle(segment, k, arrived, sent):
        take(some_of(segment, arrived), ring_recv.at[segment[0], k])
        take(some_of(segment, sent), ring_send.at[segment[0], 0])

    def ring(segment, k):
        return ring_send.at[segment[0], 0], ring_recv.at[segment[0], k]

    def beside(segment):
        return ring_send.at[segment[0], 1], ring_recv.at[segment[0], 2 * p.steps]

    def home(part, start, rows_here):
        return gathered.at[core, part, span16(start, rows_here)]

    def scatter(segment, k):
        _, _, size, kind = segment
        here = size >> (k + 1)
        if k:
            settle(segment, k - 1, 2 * here, 2 * here)
        for part in range(2):
            bit, partner = route(kind, part)[k]
            at = held(segment, part, k) + (1 - bit) * here
            if k:
                add_received(segment, part, at, here, k)
            remote(
                terms.at[part, span16(at, here)],
                received.at[part, pl.ds(inbox(segment, k), here)],
                *ring(segment, k),
                partner,
            ).start()

    def gather(segment, k):
        _, _, size, kind = segment
        here = size >> (k + 1)
        if k == p.steps - 1:
            settle(segment, k, here, here)
        else:
            settle(segment, p.steps + k + 1, here // 2, here if k == p.steps - 2 else here // 2)
        for part in range(2):
            partner = route(kind, part)[k][1]
            at = held(segment, part, k + 1)
            mine = ours = home(part, at, here)
            if k == p.steps - 1:
                add_received(segment, part, at, here, p.steps)
                mine = terms.at[part, span16(at, here)]
                pltpu.make_async_copy(mine, ours, ring_send.at[segment[0], 0]).start()
            remote(mine, ours, *ring(segment, p.steps + k), partner).start()
            if k == 0:
                remote(ours, ours, *beside(segment), sibling).start()

    def share(segment):
        _, at, size, kind = segment
        settle(segment, p.steps, size // 2, size // 2)
        take(some_of(segment, size // 2), ring_send.at[segment[0], 1])
        for part in range(2):
            bit = route(kind, part)[0][0]
            ours = home(part, at + (1 - bit) * (size // 2), size // 2)
            remote(ours, ours, *beside(segment), sibling).start()

    def travel(point):
        for todo in p.agenda.get(point, ()):
            segment, k = p.segments[todo // p.stride], todo % p.stride
            if k < p.steps:
                scatter(segment, k)
            elif k < 2 * p.steps:
                gather(segment, 2 * p.steps - 1 - k)
            else:
                share(segment)

    other_half = pl.ds(pl.multiple_of((1 - core) * half, 128), half)
    other_quarter = pl.ds(pl.multiple_of(mid + (1 - core) * (mid // 2), 128), mid // 2)
    swaps = (
        (images.at[:, other_half], sib_one),
        (head_grad, hg.at[pl.ds(cells, cells)]),
        (hid_a.at[pl.ds(height, rows)], hid_a.at[pl.ds(n_img * step + height, rows)]),
        (hid_b.at[pl.ds(0, cells)], hid_b.at[pl.ds(cells, cells)]),
        (trunk.at[:, other_half], sib_two),
        (trunk.at[:, other_half], sib_one),
        (low_b.at[pl.ds(height, rows), other_quarter], low_b_all.at[pl.ds(rows + height, rows)]),
        (low_a.at[pl.ds(0, cells)], low_a.at[pl.ds(cells, cells)]),
    )

    def swap(k):
        src, dst = swaps[k]
        return remote(src, dst, sib_send.at[k], sib_recv.at[k], sibling)

    def put_stats(ref, at, blocks, block, one, two):
        ref[(*at, pl.ds(block, 1))] = fold(one)
        ref[(*at, pl.ds(blocks + block, 1))] = fold(two)

    count_msg[...] = fold(column_sum(mask[...]))
    count_slots[me] = count_msg[...]
    loaded("images")
    loaded("reduce")

    def first_layer(nb):
        values = jnp.dot(img[...], wr[:, lanes(nb, 256)], preferred_element_type=F32)
        for h in range(2):
            one = two = jnp.zeros((8, 128), F32)
            for k in range(n_img):
                at = pl.ds(k * image, image)
                part = values[k * image : (k + 1) * image, h * 128 : h * 128 + 128]
                part = part * mask[pl.ds(k * step, image)]
                first[at, lanes(2 * nb + h)] = part
                one = one + column_sum(part)
                two = two + column_sum(part * part)
            put_stats(msg, (1,), mid_blocks, 2 * nb + h, one, two)

    repeat(mid // 256, first_layer)

    loaded("grad")
    loaded("heads")
    loaded("limits")
    head = p.heads // TASKS

    def merge(nb):
        at_wide = pl.ds(pl.multiple_of(nb * 256, 256), 256)
        for t in range(TASKS):
            at_head = pl.ds(t * head, head)
            values = lax.dot_general(
                hg[pl.ds(0, cells), at_head], wh[at_wide, at_head], NT, preferred_element_type=F32
            )
            gsc[t] = values.astype(LOW)

        def drop(i):
            at = span16(i * 64, 64)
            for h in range(2):
                grads = [gsc[t, at, pl.ds(h * 128, 128)].astype(F32) for t in range(TASKS)]
                signed, size, kept = 0.0, 0.0, 0.0
                for g in grads:
                    square = g * g + SOFT
                    signed = signed + g
                    size = size + square * lax.rsqrt(square)
                    kept = kept + jnp.tanh(g * 5.0) * g
                limit = trunk[at, lanes(2 * nb + h)].astype(F32)
                lean = jnp.tanh(2.5 + 2.5 * (signed / size) - 5.0 * limit)
                merged[at, lanes(2 * nb + h)] = 0.5 * (signed + lean * kept)

        repeat(cells // 64, drop)

    blocks = wide // 256
    cuts = [0, blocks // 4, blocks * 5 // 8, blocks * 6 // 8, blocks]

    def merge_some(k):
        lax.fori_loop(cuts[k], cuts[k + 1], lambda i, carry: (merge(i), carry)[1], 0)

    merge_some(0)
    pl.semaphore_wait(barrier, p.devices - 1)
    to_all(0, count_msg, count_slots)
    sum_start(1, 1)
    swap(0).start()
    swap(1).start()
    merge_some(1)

    def turn_images(j):
        own = img[:, pl.ds(pl.multiple_of(core * half + j * 128, 128), 128)]
        both = jnp.concatenate([own, sib_one[:, lanes(j)]], axis=0)
        img_t[lanes(j), :] = both.T

    def center(blocks):
        mean = total[pl.ds(0, blocks)] / count
        spread = total[pl.ds(blocks, blocks)] / count - mean * mean + EPS
        coef[0, pl.ds(0, blocks)] = mean
        coef[1, pl.ds(0, blocks)] = lax.rsqrt(spread)

    def row(k, block):
        return coef[k, pl.ds(block, 1)]

    def edges():
        at = lax.broadcasted_iota(jnp.int32, (image, 128), 0) & (height - 1)
        return at != 0, at != height - 1

    def put_shifted(ref, start, block, values, above, below):
        at = pl.ds(start, image)
        up = jnp.where(above, pltpu.roll(values, 1, 0), 0.0)
        down = jnp.where(below, pltpu.roll(values, image - 1, 0), 0.0)
        for h, part in enumerate((up, values, down)):
            ref[at, pl.ds(pl.multiple_of(h * mid + block * 128, 128), 128)] = part.astype(LOW)

    from_all(0, count_slots)
    count = jnp.sum(count_slots[...], axis=0)
    sum_finish(1, 1)
    center(mid_blocks)
    coef[2, pl.ds(0, mid_blocks)] = coef[1, pl.ds(0, mid_blocks)]

    def normalize_a(cb):
        above, below = edges()
        gain, shift = gain_a[pl.ds(cb, 1)], shift_a[pl.ds(cb, 1)]
        for k in range(n_img):
            at = pl.ds(k * image, image)
            hat = (first[at, lanes(cb)] - row(0, cb)) * row(1, cb)
            first[at, lanes(cb)] = hat
            pre = hat * gain + shift
            hidden = pre * logistic(pre) * mask[pl.ds(k * step, image)]
            put_shifted(hid_a, height + k * step, cb, hidden, above, below)

    repeat(mid_blocks, normalize_a)
    swap(2).start()

    take(ws, load_sem.at[len(order)])

    def second_layer(nb):
        values = None
        for j in range(3):
            term = jnp.dot(
                hid_a[pl.ds(j * height, rows)], ws[j, :, lanes(nb, 256)], preferred_element_type=F32
            )
            values = term if values is None else values + term
        for h in range(2):
            part = values[:, h * 128 : h * 128 + 128] * mask[...]
            second[:, lanes(2 * nb + h)] = part
            put_stats(msg, (2,), mid_blocks, 2 * nb + h, column_sum(part), column_sum(part * part))

    repeat(mid // 256, second_layer)
    sum_start(2, 0)
    merge_some(2)
    swap(0).wait_recv()
    repeat(half // 128, turn_images)
    sum_finish(2, 0)
    center(mid_blocks)
    coef[3, pl.ds(0, mid_blocks)] = coef[1, pl.ds(0, mid_blocks)]

    def normalize_b(cb):
        gain, shift = gain_b[pl.ds(cb, 1)], shift_b[pl.ds(cb, 1)]
        for k in range(n_img):
            at = pl.ds(k * step, image)
            hat = (second[at, lanes(cb)] - row(0, cb)) * row(1, cb)
            second[at, lanes(cb)] = hat
            pre = hat * gain + shift
            hidden = pre * logistic(pre) * mask[at]
            hid_b[pl.ds(k * image, image), lanes(cb)] = hidden.astype(LOW)

    repeat(mid_blocks, normalize_b)
    swap(3).start()

    loaded("expand")

    def third_layer(nb):
        values = jnp.dot(hid_b[pl.ds(0, cells)], we[:, lanes(nb, 256)], preferred_element_type=F32)
        third[:, lanes(nb, 256)] = values
        for h in range(2):
            part = values[:, h * 128 : h * 128 + 128]
            put_stats(
                wide_msg, (0, 0), wide_blocks, 2 * nb + h, column_sum(part), column_sum(part * part)
            )

    repeat(wide // 256, third_layer)
    wide_start(0)
    merge_some(3)
    swap(3).wait_recv()
    wide_turn(0)

    def turn_hidden(j):
        hid_b_t[lanes(j), :] = hid_b[:, lanes(j)].T

    repeat(mid_blocks, turn_hidden)
    wide_finish(0)
    center(wide_blocks)

    chunk = chunk_of(image)

    def normalize_c(i):
        cb = lax.rem(i + (1 - core) * (wide_blocks // 2), wide_blocks)
        gain, shift = gain_c[pl.ds(cb, 1)], shift_c[pl.ds(cb, 1)]
        one = two = jnp.zeros((8, 128), F32)
        for k in range(n_img):
            for r in range(image // chunk):
                at = pl.ds(k * image + r * chunk, chunk)
                valid = mask[pl.ds(k * step + r * chunk, chunk)]
                hat = (third[at, lanes(cb)] - row(0, cb)) * row(1, cb)
                third[at, lanes(cb)] = hat
                pre = hat * gain + shift + img[at, lanes(cb)].astype(F32)
                gate = logistic(pre)
                trunk[at, lanes(cb)] = (pre * gate * valid).astype(LOW)
                up = merged[at, lanes(cb)] * (gate * (1.0 + pre * (1.0 - gate))) * valid
                merged[at, lanes(cb)] = up
                one = one + column_sum(up)
                two = two + column_sum(up * hat)
        put_stats(wide_msg, (1, 0), wide_blocks, cb, one, two)

    def both_halves(body, k):
        repeat(wide_blocks // 2, body)
        swap(k).start()
        repeat(wide_blocks // 2, lambda i: body(i + wide_blocks // 2))

    both_halves(normalize_c, 4)
    wide_start(1)

    swap(1).wait_recv()
    swap(4).wait_recv()

    def heads_gradient(j):
        own = trunk[:, pl.ds(pl.multiple_of(core * half + j * 256, 128), 256)]
        both = jnp.concatenate([own, sib_two[:, lanes(j, 256)]], axis=0)
        values = lax.dot_general(both, hg[...], TN, preferred_element_type=F32)
        for b in range(p.heads // 256):
            put(HEADS, j * p.heads + b * 256, values[:, b * 256 : b * 256 + 256])

    def each(family, total, body):
        n = p.parts[family]
        per = total // n
        for i in range(n):
            repeat(per, lambda j, i=i: body(i * per + j))
            travel(p.first[family] + i)

    each(HEADS, half // 256, heads_gradient)
    wide_turn(1)

    def head_layer(nb):
        values = jnp.dot(trunk[...], wh[:, lanes(nb, 256)], preferred_element_type=F32)
        stage[:, lanes(nb, 256)] = values.astype(LOW)

    repeat(p.heads // 256, head_layer)
    pltpu.make_async_copy(stage, head_out, out_sem.at[0]).start()
    travel(AFTER_HEADS)
    swap(4).wait_send()
    wide_finish(1)

    def backward(blocks, gain, inverse):
        scale = gain * inverse
        coef[4, pl.ds(0, blocks)] = scale
        coef[5, pl.ds(0, blocks)] = -scale * total[pl.ds(0, blocks)] / count
        coef[6, pl.ds(0, blocks)] = -scale * total[pl.ds(blocks, blocks)] / count

    shift_c_grad[...] = total[pl.ds(0, wide_blocks)]
    gain_c_grad[...] = total[pl.ds(wide_blocks, wide_blocks)]
    backward(wide_blocks, gain_c[...], coef[1])

    def third_gradient(i):
        cb = lax.rem(i + (1 - core) * (wide_blocks // 2), wide_blocks)
        for k in range(n_img):
            for r in range(image // chunk):
                at = pl.ds(k * image + r * chunk, chunk)
                valid = mask[pl.ds(k * step + r * chunk, chunk)]
                down = merged[at, lanes(cb)] * row(4, cb) + row(5, cb) + third[at, lanes(cb)] * row(6, cb)
                trunk[at, lanes(cb)] = (down * valid).astype(LOW)

    both_halves(third_gradient, 5)
    travel(AFTER_THIRD)

    def slope_of(pre):
        gate = logistic(pre)
        return gate * (1.0 + pre * (1.0 - gate))

    def third_back(nb):
        values = lax.dot_general(trunk[...], we[lanes(nb, 256), :], NT, preferred_element_type=F32)
        for h in range(2):
            cb = 2 * nb + h
            one = two = jnp.zeros((8, 128), F32)
            for k in range(n_img):
                at = pl.ds(k * image, image)
                hat = second[pl.ds(k * step, image), lanes(cb)]
                pre = hat * gain_b[pl.ds(cb, 1)] + shift_b[pl.ds(cb, 1)]
                up = values[k * image : (k + 1) * image, h * 128 : h * 128 + 128]
                up = up * slope_of(pre) * mask[pl.ds(k * step, image)]
                back[at, lanes(cb)] = up
                one = one + column_sum(up)
                two = two + column_sum(up * hat)
            put_stats(msg, (3,), mid_blocks, cb, one, two)

    repeat(mid // 256, third_back)
    sum_start(3, 1)
    travel(AFTER_BACK_B)
    swap(5).wait_recv()

    def expand_gradient(j):
        own = trunk[:, pl.ds(pl.multiple_of(core * half + j * 256, 128), 256)]
        both = jnp.concatenate([own, sib_one[:, lanes(j, 256)]], axis=0)
        put(EXPAND, j * mid, jnp.dot(hid_b_t[...], both, preferred_element_type=F32))

    each(EXPAND, half // 256, expand_gradient)
    travel(AFTER_EXPAND)
    sum_finish(3, 1)
    shift_b_grad[...] = total[pl.ds(0, mid_blocks)]
    gain_b_grad[...] = total[pl.ds(mid_blocks, mid_blocks)]
    backward(mid_blocks, gain_b[...], coef[3, pl.ds(0, mid_blocks)])

    def second_gradient(cb):
        above, below = edges()
        for k in range(n_img):
            at = pl.ds(k * step, image)
            down = back[pl.ds(k * image, image), lanes(cb)] * row(4, cb) + row(5, cb)
            down = (down + second[at, lanes(cb)] * row(6, cb)) * mask[at]
            put_shifted(low_b, height + k * step, cb, down, above, below)

    repeat(mid_blocks, second_gradient)
    swap(6).start()
    own_quarter = pl.ds(pl.multiple_of(mid + core * (mid // 2), 128), mid // 2)
    low_b_all[pl.ds(0, rows)] = low_b[pl.ds(height, rows), own_quarter]

    def second_back(nb):
        values = None
        for i in range(3):
            for j in range(3):
                term = lax.dot_general(
                    low_b[pl.ds((2 - j) * height, rows), pl.ds((2 - i) * mid, mid)],
                    ws[j, pl.ds(pl.multiple_of(i * mid + nb * 256, 256), 256), :],
                    NT,
                    preferred_element_type=F32,
                )
                values = term if values is None else values + term
        for h in range(2):
            cb = 2 * nb + h
            one = two = jnp.zeros((8, 128), F32)
            for k in range(n_img):
                at = pl.ds(k * image, image)
                hat = first[at, lanes(cb)]
                pre = hat * gain_a[pl.ds(cb, 1)] + shift_a[pl.ds(cb, 1)]
                up = values[k * step : k * step + image, h * 128 : h * 128 + 128]
                up = up * slope_of(pre) * mask[pl.ds(k * step, image)]
                back[at, lanes(cb)] = up
                one = one + column_sum(up)
                two = two + column_sum(up * hat)
            put_stats(msg, (4,), mid_blocks, cb, one, two)

    repeat(mid // 256, second_back)
    sum_start(4, 0)
    travel(AFTER_BACK_A)
    swap(2).wait_recv()
    swap(6).wait_recv()
    per_tap = 3 * mid // 256

    def spatial_gradient(i):
        j, k = i // per_tap, lax.rem(i, per_tap)
        values = lax.dot_general(
            hid_a[span16(j * height, p.both), lanes(k, 256)],
            low_b_all[...],
            TN,
            preferred_element_type=F32,
        )
        put(SPATIAL, i * 256, values)

    def spatial_some(first_part, last_part):
        n = p.parts[SPATIAL]
        per = 3 * per_tap // n
        for i in range(first_part, last_part):
            repeat(per, lambda j, i=i: spatial_gradient(i * per + j))
            travel(p.first[SPATIAL] + i)

    early = p.parts[SPATIAL] * 2 // 3
    spatial_some(0, early)
    sum_finish(4, 0)
    shift_a_grad[...] = total[pl.ds(0, mid_blocks)]
    gain_a_grad[...] = total[pl.ds(mid_blocks, mid_blocks)]
    backward(mid_blocks, gain_a[...], coef[2, pl.ds(0, mid_blocks)])

    def first_gradient(cb):
        for k in range(n_img):
            at = pl.ds(k * image, image)
            down = back[at, lanes(cb)] * row(4, cb) + row(5, cb) + first[at, lanes(cb)] * row(6, cb)
            low_a[at, lanes(cb)] = (down * mask[pl.ds(k * step, image)]).astype(LOW)

    repeat(mid_blocks, first_gradient)
    swap(7).start()
    travel(AFTER_FIRST)
    swap(7).wait_recv()

    def reduce_gradient(j):
        def one(b):
            values = jnp.dot(img_t[lanes(j, 256), :], low_a[:, lanes(b, 256)], preferred_element_type=F32)
            put(REDUCE, j * mid + b * 256, values)

        repeat(mid // 256, one)

    each(REDUCE, half // 256, reduce_gradient)
    travel(AFTER_REDUCE)
    spatial_some(early, p.parts[SPATIAL])
    travel(AFTER_SPATIAL)

    def first_back(nb):
        values = lax.dot_general(low_a[pl.ds(0, cells)], wr[lanes(nb, 256), :], NT, preferred_element_type=F32)
        for h in range(2):
            for k in range(n_img):
                at = pl.ds(k * image, image)
                part = values[k * image : (k + 1) * image, h * 128 : h * 128 + 128]
                part = (part + merged[at, lanes(2 * nb + h)]) * mask[pl.ds(k * step, image)]
                img[at, lanes(2 * nb + h)] = part.astype(LOW)

    repeat(wide // 512, first_back)
    travel(AFTER_HALF)
    repeat(wide // 512, lambda i: first_back(i + wide // 512))
    pltpu.make_async_copy(img, grad_images, out_sem.at[1]).start()

    travel(LAST)
    for segment in p.segments:
        send, recv = beside(segment)
        take(some_of(segment, segment[2]), recv)
        take(some_of(segment, segment[2] // 2), send)
    pltpu.make_async_copy(stage, head_out, out_sem.at[0]).wait()
    pltpu.make_async_copy(img, grad_images, out_sem.at[1]).wait()
    for k in (0, 1, 2, 3, 5, 6, 7):
        swap(k).wait_send()


def run_block(plan, *arrays):
    p = plan
    cells, rows, mid, wide, half = p.cells, p.rows, p.mid, p.wide, p.half
    mid_blocks, wide_blocks = mid // 128, wide // 128
    anywhere = pl.BlockSpec(memory_space=pl.ANY)
    vmem = pl.BlockSpec(memory_space=pltpu.VMEM)
    smem = pl.BlockSpec(memory_space=pltpu.SMEM)
    shape = jax.ShapeDtypeStruct
    scratch = [
        pltpu.VMEM((cells, wide), LOW),
        pltpu.VMEM((wide, mid), LOW),
        pltpu.VMEM((3, 3 * mid, mid), LOW),
        pltpu.VMEM((mid, wide), LOW),
        pltpu.VMEM((wide, p.heads), LOW),
        pltpu.VMEM((2 * cells, p.heads), LOW),
        pltpu.VMEM((cells, wide), LOW),
        pltpu.VMEM((cells, half), LOW),
        pltpu.VMEM((cells, half), LOW),
        pltpu.VMEM((half, 2 * cells), LOW),
        pltpu.VMEM((cells, wide), F32),
        pltpu.VMEM((cells, wide), F32),
        pltpu.VMEM((cells, mid), F32),
        pltpu.VMEM((rows, mid), F32),
        pltpu.VMEM((cells, mid), F32),
        pltpu.VMEM((p.both + 2 * p.height, 3 * mid), LOW),
        pltpu.VMEM((2 * cells, mid), LOW),
        pltpu.VMEM((mid, 2 * cells), LOW),
        pltpu.VMEM((rows + 2 * p.height, 3 * mid), LOW),
        pltpu.VMEM((p.both, mid // 2), LOW),
        pltpu.VMEM((2 * cells, mid), LOW),
        pltpu.VMEM((TASKS, cells, 256), LOW),
        pltpu.VMEM((cells, p.heads), LOW),
        pltpu.VMEM((rows, 128), F32),
        pltpu.VMEM((7, wide_blocks, 128), F32),
        pltpu.VMEM((5, 2 * mid_blocks, 128), F32),
        pltpu.VMEM((2, p.devices, 2 * mid_blocks, 128), F32),
        pltpu.VMEM((1, 128), F32),
        pltpu.VMEM((p.devices, 1, 128), F32),
        pltpu.VMEM((2, 2, 2 * wide_blocks, 128), F32),
        pltpu.VMEM((2, 2 * p.tasks + p.line, 2 * wide_blocks, 128), F32),
        pltpu.VMEM((2 * wide_blocks, 128), F32),
        pltpu.VMEM((2, p.total, 128), LOW),
        pltpu.VMEM((2, p.total, 128), LOW),
        pltpu.SemaphoreType.DMA((7,)),
        pltpu.SemaphoreType.DMA((2,)),
        pltpu.SemaphoreType.DMA((9,)),
        pltpu.SemaphoreType.DMA((9,)),
        pltpu.SemaphoreType.DMA((8,)),
        pltpu.SemaphoreType.DMA((8,)),
        pltpu.SemaphoreType.DMA((len(p.segments), 2)),
        pltpu.SemaphoreType.DMA((len(p.segments), 2 * p.steps + 1)),
    ]
    return pl.pallas_call(
        functools.partial(block_kernel, plan),
        out_shape=(
            shape((cells, p.heads), LOW),
            shape((cells, wide), LOW),
            shape((2, 2, p.total, 128), LOW),
            shape((mid_blocks, 128), F32),
            shape((mid_blocks, 128), F32),
            shape((mid_blocks, 128), F32),
            shape((mid_blocks, 128), F32),
            shape((wide_blocks, 128), F32),
            shape((wide_blocks, 128), F32),
        ),
        in_specs=[anywhere, smem] + [anywhere] * 6 + [vmem] * 6,
        out_specs=[anywhere] * 3 + [vmem] * 6,
        scratch_shapes=scratch,
        compiler_params=pltpu.CompilerParams(
            collective_id=0, has_side_effects=True, vmem_limit_bytes=63 * 2**20
        ),
        name="block",
    )(*arrays)


def widen_kernel(plan, *refs):
    p = plan
    gathered, heads_in, images_in = refs[:3]
    small_in = refs[3:9]
    heads_out, images_out, out_reduce, out_spatial, out_expand, out_heads = refs[9:15]
    small_out = refs[15:21]
    low, reduce, spatial, expand, heads, heads_low, images_low, load_sem, out_sem, pass_sem = refs[21:]
    fetches = (
        pltpu.make_async_copy(heads_in, heads_low, pass_sem.at[0, 0]),
        pltpu.make_async_copy(images_in, images_low, pass_sem.at[1, 0]),
    )
    passes = (
        pltpu.make_async_copy(heads_low, heads_out, pass_sem.at[0, 1]),
        pltpu.make_async_copy(images_low, images_out, pass_sem.at[1, 1]),
    )
    for one in fetches:
        one.start()
    loads = []
    for s in range(4):
        for core in range(2):
            at = (core, slice(None), pl.ds(p.base[s], p.real[s]))
            load = pltpu.make_async_copy(gathered.at[at], low.at[at], load_sem.at[s, core])
            load.start()
            loads.append(load)
    for fetch, one in zip(fetches, passes):
        fetch.wait()
        one.start()
    for src, dst in zip(small_in, small_out):
        dst[...] = src[...]
    where = (
        (heads, out_heads, p.half, p.heads, True),
        (expand, out_expand, p.mid, p.half, False),
        (spatial, out_spatial, 9 * p.mid, p.mid // 2, False),
        (reduce, out_reduce, p.half, p.mid, True),
    )
    copies = []
    per_tap = p.mid // 256
    for s, (wide, out, height, width, by_rows) in enumerate(where):
        for core in range(2):
            loads[2 * s + core].wait()
            size = 256
            row_at = core * height if by_rows else 0
            col_at = 0 if by_rows else core * width

            def one(i, s=s, wide=wide, out=out, row_at=row_at, col_at=col_at, core=core):
                rows = pl.ds(pl.multiple_of(row_at + i * size, size), size)
                for b in range(width // 256):
                    if s == EXPAND:
                        start = b * height + i * size
                    elif s == SPATIAL:
                        tap, sub = i // per_tap, lax.rem(i, per_tap)
                        start = (lax.rem(tap, 3) * 3 + tap // 3) * p.mid + sub * size
                    else:
                        start = i * width + b * size
                    src = pl.ds(pl.multiple_of(p.base[s] + start, size), size)
                    for part in range(2):
                        cols = pl.ds(col_at + b * 256 + part * 128, 128)
                        wide[rows, cols] = low[core, part, src, :].astype(F32)
                at = (rows, pl.ds(col_at, width))
                pltpu.make_async_copy(wide.at[at], out.at[at], out_sem.at[s, core]).start()

            repeat(height // size, one)
            at = (pl.ds(row_at, height), pl.ds(col_at, width))
            copies.append(pltpu.make_async_copy(wide.at[at], out.at[at], out_sem.at[s, core]))
    for one in copies + list(passes):
        one.wait()


def widen(plan, head_out, grad_images, gathered, *small):
    p = plan
    anywhere = pl.BlockSpec(memory_space=pl.ANY)
    vmem = pl.BlockSpec(memory_space=pltpu.VMEM)
    shape = jax.ShapeDtypeStruct
    full = ((p.wide, p.mid), (9 * p.mid, p.mid), (p.mid, p.wide), (p.wide, p.heads))
    return pl.pallas_call(
        functools.partial(widen_kernel, plan),
        out_shape=(
            shape(head_out.shape, LOW),
            shape(grad_images.shape, LOW),
            *(shape(one, F32) for one in full),
            *(shape(one.shape, F32) for one in small),
        ),
        in_specs=[anywhere] * 3 + [vmem] * 6,
        out_specs=[anywhere] * 6 + [vmem] * 6,
        scratch_shapes=[
            pltpu.VMEM(gathered.shape, LOW),
            *(pltpu.VMEM(one, F32) for one in full),
            pltpu.VMEM(head_out.shape, LOW),
            pltpu.VMEM(grad_images.shape, LOW),
            pltpu.SemaphoreType.DMA((4, 2)),
            pltpu.SemaphoreType.DMA((4, 2)),
            pltpu.SemaphoreType.DMA((2, 2)),
        ],
        compiler_params=pltpu.CompilerParams(vmem_limit_bytes=56 * 2**20),
        name="widen",
    )(gathered, head_out, grad_images, *small)


def solution(mesh):
    cells_spec = P(("task", "dp"), None, None, None)

    def body(
        images,
        sizes,
        limits,
        head_grad,
        w_reduce,
        w_spatial,
        w_expand,
        w_heads,
        gain_a,
        shift_a,
        gain_b,
        shift_b,
        gain_c,
        shift_c,
    ):
        plan = Plan(mesh, images, w_reduce, w_heads)

        def flat(array):
            return array.transpose(0, 2, 1, 3).reshape(plan.cells, array.shape[3])

        def unflat(array):
            full = (plan.count, plan.span, plan.height, array.shape[1])
            return array.reshape(full).transpose(0, 2, 1, 3)

        outs = run_block(
            plan,
            flat(images),
            sizes,
            flat(limits),
            flat(head_grad),
            w_reduce,
            w_spatial.reshape(9, plan.mid, plan.mid),
            w_expand,
            w_heads,
            *(v.reshape(-1, 128) for v in (gain_a, shift_a, gain_b, shift_b, gain_c, shift_c)),
        )
        outs = widen(plan, *outs)
        return (
            unflat(outs[0]),
            unflat(outs[1]),
            outs[2],
            outs[3].reshape(w_spatial.shape),
            outs[4],
            outs[5],
            *(v.reshape(-1) for v in outs[6:]),
        )

    return jax.shard_map(
        body,
        mesh=mesh,
        in_specs=(cells_spec, P(("task", "dp"), None), cells_spec, cells_spec) + (P(),) * 10,
        out_specs=(cells_spec, cells_spec) + (P(),) * 10,
        check_vma=False,
    )
```

```python
import functools

import jax
import jax.numpy as jnp
from jax import lax
from jax.experimental import pallas as pl
from jax.experimental.pallas import tpu as pltpu
from jax.sharding import PartitionSpec as P

TASKS = 3
EPS = 1e-05
SOFT = 0.01
MESH = pl.DeviceIdType.MESH
F32 = jnp.float32
LOW = jnp.bfloat16
NT = (((1,), (1,)), ((), ()))
TN = (((0,), (0,)), ((), ()))
HEADS, EXPAND, SPATIAL, REDUCE = range(4)
PARTS = (4, 2, 6, 4)
ROUTES = (0, 0, 0, 0, 5, 0, 5, 0, 0, 0, 0, 3, 5, 4, 0, 3)
(
    AFTER_HEADS_0,
    AFTER_HEADS_1,
    AFTER_HEADS_2,
    AFTER_THIRD_0,
    AFTER_THIRD_1,
    AFTER_BACK_B_1,
    AFTER_EXPAND_END,
    AFTER_SECOND,
    AFTER_BACK_A_1,
    AFTER_FIRST,
    AFTER_REDUCE_END,
    AFTER_SPATIAL_END,
    AFTER_LAST_0,
    AFTER_LAST_1,
    AFTER_LAST_2,
    LAST,
) = range(100, 116)
AGENDA = {
    0: (0,),
    1: (10,),
    2: (20,),
    3: (30,),
    AFTER_THIRD_0: (1,),
    AFTER_BACK_B_1: (11, 21,),
    4: (40,),
    5: (50, 31,),
    AFTER_EXPAND_END: (2, 12,),
    AFTER_BACK_A_1: (22, 51, 32,),
    6: (60, 41,),
    7: (70, 3, 13,),
    8: (80,),
    9: (90, 23, 52,),
    10: (100, 33, 42,),
    12: (120, 71,),
    13: (130,),
    14: (140, 61,),
    15: (150, 4, 81,),
    11: (110, 24, 14,),
    AFTER_LAST_0: (91, 53,),
    AFTER_LAST_1: (34,),
    AFTER_LAST_2: (101,),
    LAST: (
        72, 43, 121, 141, 131, 62, 5, 25, 151, 15, 54, 82, 35, 73, 111, 44, 6, 92, 26, 102, 122, 152, 142, 16,
        132, 63, 55, 7, 83, 27, 36, 123, 153, 74, 17, 112, 8, 45, 93, 103, 28, 143, 37, 133, 64, 56, 18, 113,
        84, 124, 46, 154, 75, 94, 104, 38, 134, 144, 65, 114, 57, 85, 76, 135, 47, 125, 155, 66, 95, 105, 86, 145,
        58, 115, 77, 126, 156, 136, 67, 87, 116, 48, 96, 78, 127, 106, 137, 146, 157, 88, 97, 107, 147, 68, 158, 117,
        98, 108, 128, 148, 138, 118,
    ),
}


class Plan:
    def __init__(self, mesh, images, w_reduce, w_heads):
        self.tasks = mesh.shape["task"]
        self.dp = mesh.shape["dp"]
        self.line = self.dp // 2
        self.devices = self.tasks * self.dp
        assert self.tasks == 4 and self.dp % 2 == 0
        assert self.devices & (self.devices - 1) == 0
        self.count, self.height, self.span, self.wide = images.shape
        assert self.height & (self.height - 1) == 0 and self.height % 16 == 0
        self.mid = w_reduce.shape[1]
        self.heads = w_heads.shape[1]
        assert self.mid == 512 and self.heads == 768 and self.wide == 2048
        self.image = self.height * self.span
        self.cells = self.count * self.image
        self.step = self.image + self.height
        self.rows = self.count * self.step - self.height
        self.both = 2 * self.count * self.step - self.height
        self.half = self.wide // 2
        self.depth = -(-self.both // 256) * 256
        assert self.line & (self.line - 1) == 0
        self.levels = self.line.bit_length() - 1
        self.steps = 2 + self.levels
        unit = 16 << self.steps
        self.real = (
            self.heads // 256 * self.half,
            self.half // 256 * self.mid,
            9 * self.mid,
            self.mid // 256 * self.half,
        )
        tuned = self.steps == 4 and all(real % (n * unit) == 0 for real, n in zip(self.real, PARTS))
        self.parts = PARTS if tuned else (1, 1, 1, 1)
        self.base, self.first, self.segments, at = [], [], [], 0
        for real, n in zip(self.real, self.parts):
            self.base.append(at)
            self.first.append(len(self.segments))
            size = -(-real // (n * unit)) * unit
            for _ in range(n):
                index = len(self.segments)
                self.segments.append((index, at, size, ROUTES[index] if tuned else 0))
                at += size
        self.total = at
        self.agenda = AGENDA
        if not tuned:
            self.stride = 2 * self.steps + 1
            self.agenda = {i: (self.stride * i,) for i in range(4)}
            self.agenda[LAST] = [self.stride * i + k for k in range(1, self.stride) for i in range(4)]
        else:
            self.stride = 10


def chunk_of(rows):
    for size in (128, 96, 64, 48, 32, 16):
        if rows % size == 0:
            return size
    raise ValueError(rows)


def column_sum(values):
    return jnp.sum(values.reshape(values.shape[0] // 8, 8, values.shape[1]), axis=0)


def fold(part):
    return jnp.sum(part, axis=0, keepdims=True)


def logistic(values):
    return 0.5 + 0.5 * jnp.tanh(0.5 * values)


def lanes(block, width=128):
    return pl.ds(pl.multiple_of(block * width, width), width)


def span16(start, size):
    return pl.ds(pl.multiple_of(start, 16), size)


def repeat(count, body):
    def step(i, carry):
        body(i)
        return carry

    lax.fori_loop(0, count, step, 0)


def block_kernel(
    plan,
    images,
    sizes,
    limits,
    head_grad,
    w_reduce,
    w_spatial,
    w_expand,
    w_heads,
    gain_a,
    shift_a,
    gain_b,
    shift_b,
    gain_c,
    shift_c,
    head_out,
    grad_images,
    gathered,
    gain_a_grad,
    shift_a_grad,
    gain_b_grad,
    shift_b_grad,
    gain_c_grad,
    shift_c_grad,
    *scratch,
):
    (
        wr,
        ws,
        we,
        wh,
        hg,
        trunk,
        sib_one,
        sib_two,
        img_t,
        merged,
        third,
        first,
        second,
        back,
        hid_a,
        hid_b,
        hid_b_t,
        low_b,
        low_b_all,
        gsc,
        mask,
        coef,
        msg,
        slots,
        count_msg,
        count_slots,
        wide_msg,
        wide_slots,
        total,
        terms,
        received,
        load_sem,
        sum_send,
        sum_recv,
        sib_send,
        sib_recv,
        ring_send,
        ring_recv,
    ) = scratch
    img, stage, low_a = grad_images, head_out, hid_b
    p = plan
    n_img, height, image, step = p.count, p.height, p.image, p.step
    cells, rows, mid, wide, half = p.cells, p.rows, p.mid, p.wide, p.half
    mid_blocks, wide_blocks = mid // 128, wide // 128
    chunk = chunk_of(image)
    task = lax.axis_index("task")
    dp = lax.axis_index("dp")
    core = lax.rem(dp, 2)
    level = dp // 2
    me = task * p.dp + dp
    none = dp // p.dp

    def place(at_task, at_dp):
        return {"task": at_task, "dp": at_dp}

    sibling = place(task, dp + 1 - 2 * core)

    def remote(src, dst, send, recv, device):
        return pltpu.make_async_remote_copy(
            src_ref=src, dst_ref=dst, send_sem=send, recv_sem=recv, device_id=device, device_id_type=MESH
        )

    def take(ref, sem):
        pltpu.make_async_copy(ref, ref, sem).wait()

    barrier = pltpu.get_barrier_semaphore()

    def greet(i):
        other = me ^ (p.devices - 1 - i)
        pl.semaphore_signal(
            barrier,
            inc=1,
            device_id=place(other // p.dp, lax.rem(other, p.dp)),
            device_id_type=MESH,
        )

    loads = {
        "images": (images, img),
        "reduce": (w_reduce, wr),
        "grad": (head_grad, hg.at[pl.ds(0, cells)]),
        "heads": (w_heads, wh),
        "limits": (limits, trunk),
        "expand": (w_expand, we),
    }
    order = list(loads)

    def load(key):
        pltpu.make_async_copy(*loads[key], load_sem.at[order.index(key)]).start()

    load("images")
    load("reduce")
    repeat(p.devices - 1, greet)
    for key in order[2:]:
        load(key)
    for row_tap in range(3):
        for col_tap in range(3):
            pltpu.make_async_copy(
                w_spatial.at[row_tap * 3 + col_tap],
                ws.at[col_tap, pl.ds(row_tap * mid, mid)],
                load_sem.at[len(order)],
            ).start()

    def loaded(key):
        pltpu.make_async_copy(*loads[key], load_sem.at[order.index(key)]).wait()

    mask[...] = jnp.zeros_like(mask)
    for k in range(n_img):
        at = lax.broadcasted_iota(jnp.int32, (image, 128), 0)
        inside = ((at & (height - 1)) < sizes[k, 0]) & ((at // height) < sizes[k, 1])
        mask[pl.ds(k * step, image)] = jnp.where(inside, 1.0, 0.0)
    zero_rows = jnp.zeros((height, 3 * mid), LOW)
    for k in range(2 * n_img + 1):
        hid_a[pl.ds(k * step, height)] = zero_rows
    beyond = p.depth - p.both
    hid_a[pl.ds(p.both + 2 * height, beyond)] = jnp.zeros((beyond, 3 * mid), LOW)
    low_b_all[pl.ds(p.both, beyond)] = jnp.zeros((beyond, mid // 2), LOW)
    for k in range(n_img + 1):
        low_b[pl.ds(k * step, height)] = zero_rows
    low_b_all[pl.ds(rows, height)] = jnp.zeros((height, mid // 2), LOW)

    def to_all(k, src, dst):
        def send(i):
            other = me ^ (p.devices - 1 - i)
            device = place(other // p.dp, lax.rem(other, p.dp))
            remote(src, dst.at[me], sum_send.at[k], sum_recv.at[k], device).start()

        repeat(p.devices - 1, send)

    def from_all(k, dst):
        some = dst.at[pl.ds(0, p.devices - 1)]
        take(some, sum_recv.at[k])
        take(some, sum_send.at[k])

    def sum_start(k, slot):
        slots[slot, me] = msg[k]
        to_all(k, msg.at[k], slots.at[slot])

    def sum_finish(k, slot):
        from_all(k, slots.at[slot])
        total[pl.ds(0, 2 * mid_blocks)] = jnp.sum(slots[slot], axis=0)

    plane = 2 * p.tasks
    spot = task * 2 + core

    def wide_start(k):
        wide_slots[k, spot] = wide_msg[k, 0]
        for i in range(plane - 1, 0, -1):
            other = spot ^ i
            remote(
                wide_msg.at[k, 0],
                wide_slots.at[k, spot],
                sum_send.at[5 + 2 * k],
                sum_recv.at[5 + 2 * k],
                place(other // 2, level * 2 + lax.rem(other, 2)),
            ).start()

    def wide_turn(k):
        some = wide_slots.at[k, pl.ds(0, plane - 1)]
        take(some, sum_recv.at[5 + 2 * k])
        take(some, sum_send.at[5 + 2 * k])
        partial = jnp.sum(wide_slots[k, pl.ds(0, plane)], axis=0)
        wide_msg[k, 1] = partial
        wide_slots[k, plane + level] = partial
        for i in range(p.line - 1, 0, -1):
            other = level ^ i
            remote(
                wide_msg.at[k, 1],
                wide_slots.at[k, plane + level],
                sum_send.at[6 + 2 * k],
                sum_recv.at[6 + 2 * k],
                place(task, other * 2 + core),
            ).start()

    def wide_finish(k):
        some = wide_slots.at[k, pl.ds(plane, p.line - 1)]
        take(some, sum_recv.at[6 + 2 * k])
        take(some, sum_send.at[6 + 2 * k])
        total[...] = jnp.sum(wide_slots[k, pl.ds(plane, p.line)], axis=0)

    low_bit, high_bit = lax.rem(task, 2), task // 2
    along_x = (low_bit, place(task + 1 - 2 * low_bit, dp))
    along_y = (high_bit, place(task + 2 - 4 * high_bit, dp))
    along_z = []
    for k in range(p.levels):
        bit = lax.rem(level // 2**k, 2)
        along_z.append((bit, place(task, dp + 2 ** (k + 1) - 2 ** (k + 2) * bit)))

    def route(kind, part):
        one, two = (along_x, along_y) if part == 0 else (along_y, along_x)
        return (
            [one, two, *along_z],
            [one, *along_z, two],
            [*along_z, one, two],
            [one, *along_z[:1], two, *along_z[1:]],
            [*along_z[:1], one, *along_z[1:], two],
            [*along_z[:1], one, two, *along_z[1:]],
        )[kind]

    def held(segment, part, k):
        _, at, size, kind = segment
        for j, (bit, _) in enumerate(route(kind, part)[:k]):
            at = at + bit * (size >> (j + 1))
        return at

    def inbox(segment, k):
        _, at, size, _ = segment
        return at + size - (size >> k)

    def put(family, row, values):
        low = values.astype(LOW)
        at = span16(p.base[family] + row, low.shape[0])
        terms[0, at, :] = low[:, :128]
        terms[1, at, :] = low[:, 128:]

    def add_received(segment, part, at, rows_here, k):
        starts = [inbox(segment, j) + at - held(segment, part, j + 1) for j in range(k)]
        size = chunk_of(rows_here)

        def one(i):
            here = span16(at + i * size, size)
            acc = terms[part, here, :].astype(F32)
            for start in starts:
                acc = acc + received[part, span16(start + i * size, size), :].astype(F32)
            terms[part, here, :] = acc.astype(LOW)

        repeat(rows_here // size, one)

    def some_of(segment, rows_here):
        return received.at[:, pl.ds(segment[1], rows_here)]

    def ring(segment, k):
        at = k - p.steps - 1 if k > p.steps else k
        return ring_send.at[segment[0], 0], ring_recv.at[segment[0], at]

    def settle(segment, k, arrived, sent):
        send, recv = ring(segment, k)
        take(some_of(segment, arrived), recv)
        take(some_of(segment, sent), send)

    def beside(segment):
        return ring_send.at[segment[0], 1], ring_recv.at[segment[0], p.steps + 1]

    def home(part, start, rows_here):
        return gathered.at[core, part, span16(start, rows_here)]

    def scatter(segment, k):
        _, _, size, kind = segment
        here = size >> (k + 1)
        if k:
            settle(segment, k - 1, 2 * here, 2 * here)
        for part in range(2):
            bit, partner = route(kind, part)[k]
            at = held(segment, part, k) + (1 - bit) * here
            if k:
                add_received(segment, part, at, here, k)
            remote(
                terms.at[part, span16(at, here)],
                received.at[part, pl.ds(inbox(segment, k), here)],
                *ring(segment, k),
                partner,
            ).start()

    def gather(segment, k):
        _, _, size, kind = segment
        here = size >> (k + 1)
        if k == p.steps - 1:
            settle(segment, k, here, here)
        else:
            settle(segment, p.steps + k + 1, here // 2, here if k == p.steps - 2 else here // 2)
        for part in range(2):
            partner = route(kind, part)[k][1]
            at = held(segment, part, k + 1)
            mine = ours = home(part, at, here)
            if k == p.steps - 1:
                add_received(segment, part, at, here, p.steps)
                mine = terms.at[part, span16(at, here)]
                pltpu.make_async_copy(mine, ours, ring_send.at[segment[0], 0]).start()
            remote(mine, ours, *ring(segment, p.steps + k), partner).start()
            if k == 0:
                remote(ours, ours, *beside(segment), sibling).start()

    def share(segment):
        _, at, size, kind = segment
        settle(segment, p.steps, size // 2, size // 2)
        take(some_of(segment, size // 2), ring_send.at[segment[0], 1])
        for part in range(2):
            bit = route(kind, part)[0][0]
            ours = home(part, at + (1 - bit) * (size // 2), size // 2)
            remote(ours, ours, *beside(segment), sibling).start()

    def travel(point):
        for todo in p.agenda.get(point, ()):
            segment, k = p.segments[todo // p.stride], todo % p.stride
            if k < p.steps:
                scatter(segment, k)
            elif k < 2 * p.steps:
                gather(segment, 2 * p.steps - 1 - k)
            else:
                share(segment)

    other_half = pl.ds(pl.multiple_of((1 - core) * half, 128), half)
    other_quarter = pl.ds(pl.multiple_of(mid + (1 - core) * (mid // 2), 128), mid // 2)
    swaps = (
        (images.at[:, other_half], sib_one),
        (head_grad, hg.at[pl.ds(cells, cells)]),
        (hid_a.at[pl.ds(height, rows)], hid_a.at[pl.ds(n_img * step + height, rows)]),
        (hid_b.at[pl.ds(0, cells)], hid_b.at[pl.ds(cells, cells)]),
        (trunk.at[:, other_half], sib_two),
        (trunk.at[:, other_half], sib_one),
        (low_b.at[pl.ds(height, rows), other_quarter], low_b_all.at[pl.ds(rows + height, rows)]),
        (low_a.at[pl.ds(0, cells)], low_a.at[pl.ds(cells, cells)]),
    )

    def swap(k):
        src, dst = swaps[k]
        return remote(src, dst, sib_send.at[k], sib_recv.at[k], sibling)

    def put_stats(ref, at, blocks, block, one, two):
        ref[(*at, pl.ds(block, 1))] = fold(one)
        ref[(*at, pl.ds(blocks + block, 1))] = fold(two)

    count_msg[...] = fold(column_sum(mask[...]))
    count_slots[me] = count_msg[...]
    loaded("images")
    loaded("reduce")

    def first_layer(nb):
        values = jnp.dot(img[...], wr[:, lanes(nb, 512)], preferred_element_type=F32)
        for h in range(4):
            one = two = jnp.zeros((8, 128), F32)
            for k in range(n_img):
                at = pl.ds(k * image, image)
                part = values[k * image : (k + 1) * image, h * 128 : h * 128 + 128]
                part = part * mask[pl.ds(k * step, image)]
                first[at, lanes(4 * nb + h)] = part
                one = one + column_sum(part)
                two = two + column_sum(part * part)
            put_stats(msg, (1,), mid_blocks, 4 * nb + h, one, two)

    first_layer(none)

    loaded("grad")
    loaded("heads")
    loaded("limits")
    head = p.heads // TASKS

    def merge(nb):
        at_wide = pl.ds(pl.multiple_of(nb * 256, 256), 256)
        for t in range(TASKS):
            at_head = pl.ds(t * head, head)
            values = lax.dot_general(
                hg[pl.ds(0, cells), at_head], wh[at_wide, at_head], NT, preferred_element_type=F32
            )
            gsc[t] = values.astype(LOW)

        def drop(i):
            at = span16(i * chunk, chunk)
            per = image // chunk
            valid = mask[span16(i // per * step + lax.rem(i, per) * chunk, chunk)]
            for h in range(2):
                grads = [gsc[t, at, pl.ds(h * 128, 128)].astype(F32) for t in range(TASKS)]
                signed, size, kept = 0.0, 0.0, 0.0
                for g in grads:
                    square = g * g + SOFT
                    signed = signed + g
                    size = size + square * lax.rsqrt(square)
                    kept = kept + jnp.tanh(g * 5.0) * g
                limit = trunk[at, lanes(2 * nb + h)].astype(F32)
                lean = jnp.tanh(2.5 + 2.5 * (signed / size) - 5.0 * limit)
                merged[at, lanes(2 * nb + h)] = (0.25 * valid) * (signed + lean * kept)

        repeat(cells // chunk, drop)

    blocks = wide // 256
    cuts = [0, blocks // 4, blocks * 5 // 8, blocks * 6 // 8, blocks]

    def merge_some(k):
        lax.fori_loop(cuts[k], cuts[k + 1], lambda i, carry: (merge(i), carry)[1], 0)

    merge_some(0)
    pl.semaphore_wait(barrier, p.devices - 1)
    to_all(0, count_msg, count_slots)
    sum_start(1, 1)
    swap(0).start()
    swap(1).start()
    merge_some(1)

    def turn_images(j):
        own = img[:, pl.ds(pl.multiple_of(core * half + j * 128, 128), 128)]
        both = jnp.concatenate([own, sib_one[:, lanes(j)]], axis=0)
        img_t[lanes(j), :] = both.T

    def center(blocks):
        mean = total[pl.ds(0, blocks)] / count
        spread = total[pl.ds(blocks, blocks)] / count - mean * mean + EPS
        coef[0, pl.ds(0, blocks)] = mean
        coef[1, pl.ds(0, blocks)] = lax.rsqrt(spread)

    def row(k, block):
        return coef[k, pl.ds(block, 1)]

    def edges():
        at = lax.broadcasted_iota(jnp.int32, (image, 128), 0) & (height - 1)
        return at != 0, at != height - 1

    def put_shifted(ref, start, block, values, above, below):
        at = pl.ds(start, image)
        up = jnp.where(above, pltpu.roll(values, 1, 0), 0.0)
        down = jnp.where(below, pltpu.roll(values, image - 1, 0), 0.0)
        for h, part in enumerate((up, values, down)):
            ref[at, pl.ds(pl.multiple_of(h * mid + block * 128, 128), 128)] = part.astype(LOW)

    from_all(0, count_slots)
    count = jnp.sum(count_slots[...], axis=0)
    sum_finish(1, 1)
    center(mid_blocks)
    coef[2, pl.ds(0, mid_blocks)] = coef[1, pl.ds(0, mid_blocks)]

    def normalize_a(cb):
        above, below = edges()
        gain, shift = gain_a[pl.ds(cb, 1)], shift_a[pl.ds(cb, 1)]
        for k in range(n_img):
            at = pl.ds(k * image, image)
            hat = (first[at, lanes(cb)] - row(0, cb)) * row(1, cb)
            first[at, lanes(cb)] = hat
            pre = hat * gain + shift
            hidden = pre * logistic(pre) * mask[pl.ds(k * step, image)]
            put_shifted(hid_a, height + k * step, cb, hidden, above, below)

    repeat(mid_blocks, normalize_a)
    swap(2).start()

    take(ws, load_sem.at[len(order)])

    def second_layer(nb):
        values = None
        for j in range(3):
            term = jnp.dot(
                hid_a[pl.ds(j * height, rows)], ws[j, :, lanes(nb, 512)], preferred_element_type=F32
            )
            values = term if values is None else values + term
        for h in range(4):
            part = values[:, h * 128 : h * 128 + 128] * mask[...]
            second[:, lanes(4 * nb + h)] = part
            put_stats(msg, (2,), mid_blocks, 4 * nb + h, column_sum(part), column_sum(part * part))

    second_layer(none)
    sum_start(2, 0)
    merge_some(2)
    swap(0).wait_recv()
    repeat(half // 128, turn_images)
    sum_finish(2, 0)
    center(mid_blocks)
    coef[3, pl.ds(0, mid_blocks)] = coef[1, pl.ds(0, mid_blocks)]

    def normalize_b(cb):
        gain, shift = gain_b[pl.ds(cb, 1)], shift_b[pl.ds(cb, 1)]
        for k in range(n_img):
            at = pl.ds(k * step, image)
            hat = (second[at, lanes(cb)] - row(0, cb)) * row(1, cb)
            second[at, lanes(cb)] = hat
            pre = hat * gain + shift
            hidden = pre * logistic(pre) * mask[at]
            hid_b[pl.ds(k * image, image), lanes(cb)] = hidden.astype(LOW)

    repeat(mid_blocks, normalize_b)
    swap(3).start()

    loaded("expand")

    def third_layer(nb):
        values = jnp.dot(hid_b[pl.ds(0, cells)], we[:, lanes(nb, 512)], preferred_element_type=F32)
        third[:, lanes(nb, 512)] = values
        for h in range(4):
            part = values[:, h * 128 : h * 128 + 128]
            put_stats(
                wide_msg, (0, 0), wide_blocks, 4 * nb + h, column_sum(part), column_sum(part * part)
            )

    repeat(wide // 512, third_layer)
    wide_start(0)
    merge_some(3)
    swap(3).wait()
    wide_turn(0)

    def turn_hidden(j):
        hid_b_t[lanes(j), :] = hid_b[:, lanes(j)].T

    repeat(mid_blocks, turn_hidden)
    wide_finish(0)
    center(wide_blocks)

    scale_c = gain_c[...] * coef[1]
    coef[7] = scale_c
    coef[8] = shift_c[...] - coef[0] * scale_c

    def normalize_c(i):
        cb = lax.rem(i + (1 - core) * (wide_blocks // 2), wide_blocks)
        one = two = jnp.zeros((8, 128), F32)
        for k in range(n_img):
            for r in range(image // chunk):
                at = pl.ds(k * image + r * chunk, chunk)
                valid = mask[pl.ds(k * step + r * chunk, chunk)]
                raw = third[at, lanes(cb)]
                pre = raw * row(7, cb) + (row(8, cb) + img[at, lanes(cb)].astype(F32))
                h = 0.5 * pre
                t = jnp.tanh(h)
                value = h + h * t
                trunk[at, lanes(cb)] = (value * valid).astype(LOW)
                up = merged[at, lanes(cb)] * ((1.0 + value) + t * (1.0 - value))
                merged[at, lanes(cb)] = up
                one = one + column_sum(up)
                two = two + column_sum(up * raw)
        put_stats(wide_msg, (1, 0), wide_blocks, cb, one, two)

    def both_halves(body, k, point):
        repeat(wide_blocks // 2, body)
        swap(k).start()
        travel(point)
        repeat(wide_blocks // 2, lambda i: body(i + wide_blocks // 2))

    both_halves(normalize_c, 4, None)
    wide_start(1)

    swap(1).wait_recv()
    swap(4).wait_recv()

    def heads_gradient(i):
        own = trunk[:, pl.ds(pl.multiple_of(core * half + i * 512, 128), 512)]
        both = jnp.concatenate([own, sib_two[:, lanes(i, 512)]], axis=0)
        values = lax.dot_general(both, hg[...], TN, preferred_element_type=F32)
        for q in range(2):
            for b in range(p.heads // 256):
                part = values[q * 256 : q * 256 + 256, b * 256 : b * 256 + 256]
                put(HEADS, (2 * i + q) * p.heads + b * 256, part)

    def each(family, first_part, last_part, count, body):
        n = p.parts[family]
        for i in range(first_part, last_part):
            body(i + none)
            for done in range(i * n // count, (i + 1) * n // count):
                travel(p.first[family] + done)

    each(HEADS, 0, half // 512, half // 512, heads_gradient)
    wide_turn(1)

    def head_layer(nb):
        values = jnp.dot(trunk[...], wh[:, lanes(nb, 256)], preferred_element_type=F32)
        stage[:, lanes(nb, 256)] = values.astype(LOW)

    for i, point in enumerate((AFTER_HEADS_0, AFTER_HEADS_1, AFTER_HEADS_2)):
        head_layer(i)
        travel(point)
    swap(4).wait_send()
    wide_finish(1)

    def backward(blocks, gain, inverse):
        scale = gain * inverse
        coef[4, pl.ds(0, blocks)] = scale
        coef[5, pl.ds(0, blocks)] = -scale * total[pl.ds(0, blocks)] / count
        coef[6, pl.ds(0, blocks)] = -scale * total[pl.ds(blocks, blocks)] / count

    sum_up = total[pl.ds(0, wide_blocks)]
    sum_up_hat = (total[pl.ds(wide_blocks, wide_blocks)] - coef[0] * sum_up) * coef[1]
    shift_c_grad[...] = sum_up
    gain_c_grad[...] = sum_up_hat
    per_hat = -coef[7] * sum_up_hat / count
    coef[4] = coef[7]
    coef[5] = -coef[7] * sum_up / count - per_hat * coef[1] * coef[0]
    coef[6] = per_hat * coef[1]

    def third_gradient(i):
        cb = lax.rem(i + (1 - core) * (wide_blocks // 2), wide_blocks)
        for k in range(n_img):
            for r in range(image // chunk):
                at = pl.ds(k * image + r * chunk, chunk)
                valid = mask[pl.ds(k * step + r * chunk, chunk)]
                down = merged[at, lanes(cb)] * row(4, cb) + row(5, cb) + third[at, lanes(cb)] * row(6, cb)
                trunk[at, lanes(cb)] = (down * valid).astype(LOW)

    both_halves(third_gradient, 5, AFTER_THIRD_0)
    travel(AFTER_THIRD_1)

    def slope_of(pre):
        gate = logistic(pre)
        return gate * (1.0 + pre * (1.0 - gate))

    def third_back(nb):
        values = lax.dot_general(trunk[...], we[lanes(nb, 512), :], NT, preferred_element_type=F32)
        for h in range(4):
            cb = 4 * nb + h
            one = two = jnp.zeros((8, 128), F32)
            for k in range(n_img):
                at = pl.ds(k * image, image)
                hat = second[pl.ds(k * step, image), lanes(cb)]
                pre = hat * gain_b[pl.ds(cb, 1)] + shift_b[pl.ds(cb, 1)]
                up = values[k * image : (k + 1) * image, h * 128 : h * 128 + 128]
                up = up * slope_of(pre) * mask[pl.ds(k * step, image)]
                back[at, lanes(cb)] = up
                one = one + column_sum(up)
                two = two + column_sum(up * hat)
            put_stats(msg, (3,), mid_blocks, cb, one, two)

    third_back(none)
    sum_start(3, 1)
    travel(AFTER_BACK_B_1)
    swap(5).wait_recv()

    def expand_gradient(i):
        own = trunk[:, pl.ds(pl.multiple_of(core * half + i * 512, 128), 512)]
        both = jnp.concatenate([own, sib_one[:, lanes(i, 512)]], axis=0)
        values = jnp.dot(hid_b_t[...], both, preferred_element_type=F32)
        for q in range(2):
            put(EXPAND, (2 * i + q) * mid, values[:, q * 256 : q * 256 + 256])

    each(EXPAND, 0, half // 512, half // 512, expand_gradient)
    travel(AFTER_EXPAND_END)
    sum_finish(3, 1)
    shift_b_grad[...] = total[pl.ds(0, mid_blocks)]
    gain_b_grad[...] = total[pl.ds(mid_blocks, mid_blocks)]
    backward(mid_blocks, gain_b[...], coef[3, pl.ds(0, mid_blocks)])

    def second_gradient(cb):
        above, below = edges()
        for k in range(n_img):
            at = pl.ds(k * step, image)
            down = back[pl.ds(k * image, image), lanes(cb)] * row(4, cb) + row(5, cb)
            down = (down + second[at, lanes(cb)] * row(6, cb)) * mask[at]
            put_shifted(low_b, height + k * step, cb, down, above, below)

    repeat(mid_blocks, second_gradient)
    swap(6).start()
    own_quarter = pl.ds(pl.multiple_of(mid + core * (mid // 2), 128), mid // 2)
    low_b_all[pl.ds(0, rows)] = low_b[pl.ds(height, rows), own_quarter]
    travel(AFTER_SECOND)

    def second_back(nb):
        values = None
        for i in range(3):
            for j in range(3):
                term = lax.dot_general(
                    low_b[pl.ds((2 - j) * height, rows), pl.ds((2 - i) * mid, mid)],
                    ws[j, pl.ds(pl.multiple_of(i * mid + nb * 512, 256), 512), :],
                    NT,
                    preferred_element_type=F32,
                )
                values = term if values is None else values + term
        for h in range(4):
            cb = 4 * nb + h
            one = two = jnp.zeros((8, 128), F32)
            for k in range(n_img):
                at = pl.ds(k * image, image)
                hat = first[at, lanes(cb)]
                pre = hat * gain_a[pl.ds(cb, 1)] + shift_a[pl.ds(cb, 1)]
                up = values[k * step : k * step + image, h * 128 : h * 128 + 128]
                up = up * slope_of(pre) * mask[pl.ds(k * step, image)]
                back[at, lanes(cb)] = up
                one = one + column_sum(up)
                two = two + column_sum(up * hat)
            put_stats(msg, (4,), mid_blocks, cb, one, two)

    second_back(none)
    sum_start(4, 0)
    travel(AFTER_BACK_A_1)
    swap(2).wait_recv()
    swap(6).wait_recv()
    def spatial_gradient(i):
        j, k = i // 2, lax.rem(i, 2)
        values = lax.dot_general(
            hid_a[span16(j * height, p.depth), lanes(k, 768)], low_b_all[...], TN, preferred_element_type=F32
        )
        put(SPATIAL, i * 768, values)

    each(SPATIAL, 0, 5, 6, spatial_gradient)
    sum_finish(4, 0)
    shift_a_grad[...] = total[pl.ds(0, mid_blocks)]
    gain_a_grad[...] = total[pl.ds(mid_blocks, mid_blocks)]
    backward(mid_blocks, gain_a[...], coef[2, pl.ds(0, mid_blocks)])

    def first_gradient(cb):
        for k in range(n_img):
            at = pl.ds(k * image, image)
            down = back[at, lanes(cb)] * row(4, cb) + row(5, cb) + first[at, lanes(cb)] * row(6, cb)
            low_a[at, lanes(cb)] = (down * mask[pl.ds(k * step, image)]).astype(LOW)

    repeat(mid_blocks, first_gradient)
    swap(7).start()
    travel(AFTER_FIRST)
    swap(7).wait_recv()

    def reduce_gradient(i):
        values = jnp.dot(img_t[lanes(i, 512), :], low_a[...], preferred_element_type=F32)
        for q in range(2):
            for b in range(mid // 256):
                part = values[q * 256 : q * 256 + 256, b * 256 : b * 256 + 256]
                put(REDUCE, (2 * i + q) * mid + b * 256, part)

    each(REDUCE, 0, half // 512, half // 512, reduce_gradient)
    travel(AFTER_REDUCE_END)
    each(SPATIAL, 5, 6, 6, spatial_gradient)
    travel(AFTER_SPATIAL_END)

    def first_back(nb):
        values = lax.dot_general(low_a[pl.ds(0, cells)], wr[lanes(nb, 512), :], NT, preferred_element_type=F32)
        for h in range(4):
            for k in range(n_img):
                at = pl.ds(k * image, image)
                part = values[k * image : (k + 1) * image, h * 128 : h * 128 + 128]
                part = (part + merged[at, lanes(4 * nb + h)]) * mask[pl.ds(k * step, image)]
                img[at, lanes(4 * nb + h)] = part.astype(LOW)

    for i, point in enumerate((AFTER_LAST_0, AFTER_LAST_1, AFTER_LAST_2, None)):
        first_back(i + none)
        travel(point)

    travel(LAST)
    for segment in p.segments:
        send, recv = beside(segment)
        take(some_of(segment, segment[2]), recv)
        take(some_of(segment, segment[2] // 2), send)
    for k in (0, 1, 2, 5, 6, 7):
        swap(k).wait_send()


def run_block(plan, *arrays):
    p = plan
    cells, rows, mid, wide, half = p.cells, p.rows, p.mid, p.wide, p.half
    mid_blocks, wide_blocks = mid // 128, wide // 128
    anywhere = pl.BlockSpec(memory_space=pl.ANY)
    vmem = pl.BlockSpec(memory_space=pltpu.VMEM)
    smem = pl.BlockSpec(memory_space=pltpu.SMEM)
    shape = jax.ShapeDtypeStruct
    scratch = [
        pltpu.VMEM((wide, mid), LOW),
        pltpu.VMEM((3, 3 * mid, mid), LOW),
        pltpu.VMEM((mid, wide), LOW),
        pltpu.VMEM((wide, p.heads), LOW),
        pltpu.VMEM((2 * cells, p.heads), LOW),
        pltpu.VMEM((cells, wide), LOW),
        pltpu.VMEM((cells, half), LOW),
        pltpu.VMEM((cells, half), LOW),
        pltpu.VMEM((half, 2 * cells), LOW),
        pltpu.VMEM((cells, wide), F32),
        pltpu.VMEM((cells, wide), F32),
        pltpu.VMEM((cells, mid), F32),
        pltpu.VMEM((rows, mid), F32),
        pltpu.VMEM((cells, mid), F32),
        pltpu.VMEM((p.depth + 2 * p.height, 3 * mid), LOW),
        pltpu.VMEM((2 * cells, mid), LOW),
        pltpu.VMEM((mid, 2 * cells), LOW),
        pltpu.VMEM((rows + 2 * p.height, 3 * mid), LOW),
        pltpu.VMEM((p.depth, mid // 2), LOW),
        pltpu.VMEM((TASKS, cells, 256), LOW),
        pltpu.VMEM((rows, 128), F32),
        pltpu.VMEM((9, wide_blocks, 128), F32),
        pltpu.VMEM((5, 2 * mid_blocks, 128), F32),
        pltpu.VMEM((2, p.devices, 2 * mid_blocks, 128), F32),
        pltpu.VMEM((1, 128), F32),
        pltpu.VMEM((p.devices, 1, 128), F32),
        pltpu.VMEM((2, 2, 2 * wide_blocks, 128), F32),
        pltpu.VMEM((2, 2 * p.tasks + p.line, 2 * wide_blocks, 128), F32),
        pltpu.VMEM((2 * wide_blocks, 128), F32),
        pltpu.VMEM((2, p.total, 128), LOW),
        pltpu.VMEM((2, p.total, 128), LOW),
        pltpu.SemaphoreType.DMA((7,)),
        pltpu.SemaphoreType.DMA((9,)),
        pltpu.SemaphoreType.DMA((9,)),
        pltpu.SemaphoreType.DMA((8,)),
        pltpu.SemaphoreType.DMA((8,)),
        pltpu.SemaphoreType.DMA((len(p.segments), 2)),
        pltpu.SemaphoreType.DMA((len(p.segments), p.steps + 2)),
    ]
    return pl.pallas_call(
        functools.partial(block_kernel, plan),
        out_shape=(
            pltpu.VMEM((cells, p.heads), LOW),
            pltpu.VMEM((cells, wide), LOW),
            shape((2, 2, p.total, 128), LOW),
            *[pltpu.VMEM((mid_blocks, 128), F32)] * 4,
            *[pltpu.VMEM((wide_blocks, 128), F32)] * 2,
        ),
        in_specs=[anywhere, smem] + [anywhere] * 6 + [vmem] * 6,
        out_specs=[vmem] * 2 + [anywhere] + [vmem] * 6,
        scratch_shapes=scratch,
        compiler_params=pltpu.CompilerParams(
            collective_id=0, has_side_effects=True, vmem_limit_bytes=59 * 2**20
        ),
        name="block",
    )(*arrays)


def widen_kernel(plan, *refs):
    p = plan
    gathered, heads_in, images_in = refs[:3]
    small_in = refs[3:9]
    heads_out, images_out, out_reduce, out_spatial, out_expand, out_heads = refs[9:15]
    small_out = refs[15:21]
    low, reduce, spatial, expand, heads, load_sem, out_sem, pass_sem = refs[21:]
    passes = (
        pltpu.make_async_copy(heads_in, heads_out, pass_sem.at[0]),
        pltpu.make_async_copy(images_in, images_out, pass_sem.at[1]),
    )
    for one in passes:
        one.start()
    loads = []
    for s in range(4):
        for core in range(2):
            at = (core, slice(None), pl.ds(p.base[s], p.real[s]))
            loads.append(pltpu.make_async_copy(gathered.at[at], low.at[at], load_sem.at[s, core]))
    ahead = 3
    for one in loads[:ahead]:
        one.start()
    for src, dst in zip(small_in, small_out):
        dst[...] = src[...]
    where = (
        (heads, out_heads, p.half, p.heads, True),
        (expand, out_expand, p.mid, p.half, False),
        (spatial, out_spatial, 9 * p.mid, p.mid // 2, False),
        (reduce, out_reduce, p.half, p.mid, True),
    )
    copies = []
    per_tap = p.mid // 256
    for s, (wide, out, height, width, by_rows) in enumerate(where):
        for core in range(2):
            loads[2 * s + core].wait()
            for one in loads[2 * s + core + ahead :][:1]:
                one.start()
            size = 256
            row_at = core * height if by_rows else 0
            col_at = 0 if by_rows else core * width

            def one(i, s=s, wide=wide, out=out, row_at=row_at, col_at=col_at, core=core):
                rows = pl.ds(pl.multiple_of(row_at + i * size, size), size)
                for b in range(width // 256):
                    if s == EXPAND:
                        start = b * height + i * size
                    elif s == SPATIAL:
                        tap, sub = i // per_tap, lax.rem(i, per_tap)
                        start = (lax.rem(tap, 3) * 3 + tap // 3) * p.mid + sub * size
                    else:
                        start = i * width + b * size
                    src = pl.ds(pl.multiple_of(p.base[s] + start, size), size)
                    for part in range(2):
                        cols = pl.ds(col_at + b * 256 + part * 128, 128)
                        wide[rows, cols] = low[core, part, src, :].astype(F32)
                at = (rows, pl.ds(col_at, width))
                pltpu.make_async_copy(wide.at[at], out.at[at], out_sem.at[s, core]).start()

            repeat(height // size, one)
            at = (pl.ds(row_at, height), pl.ds(col_at, width))
            copies.append(pltpu.make_async_copy(wide.at[at], out.at[at], out_sem.at[s, core]))
    for one in copies + list(passes):
        one.wait()


def widen(plan, head_out, grad_images, gathered, *small):
    p = plan
    anywhere = pl.BlockSpec(memory_space=pl.ANY)
    vmem = pl.BlockSpec(memory_space=pltpu.VMEM)
    shape = jax.ShapeDtypeStruct
    full = ((p.wide, p.mid), (9 * p.mid, p.mid), (p.mid, p.wide), (p.wide, p.heads))
    return pl.pallas_call(
        functools.partial(widen_kernel, plan),
        out_shape=(
            shape(head_out.shape, LOW),
            shape(grad_images.shape, LOW),
            *(shape(one, F32) for one in full),
            *(shape(one.shape, F32) for one in small),
        ),
        in_specs=[anywhere] + [vmem] * 8,
        out_specs=[anywhere] * 6 + [vmem] * 6,
        scratch_shapes=[
            pltpu.VMEM(gathered.shape, LOW),
            *(pltpu.VMEM(one, F32) for one in full),
            pltpu.SemaphoreType.DMA((4, 2)),
            pltpu.SemaphoreType.DMA((4, 2)),
            pltpu.SemaphoreType.DMA((2,)),
        ],
        compiler_params=pltpu.CompilerParams(vmem_limit_bytes=48 * 2**20),
        name="widen",
    )(
        gathered,
        *(pltpu.with_memory_space_constraint(one, pltpu.VMEM) for one in (head_out, grad_images, *small)),
    )


def solution(mesh):
    cells_spec = P(("task", "dp"), None, None, None)

    def body(
        images,
        sizes,
        limits,
        head_grad,
        w_reduce,
        w_spatial,
        w_expand,
        w_heads,
        gain_a,
        shift_a,
        gain_b,
        shift_b,
        gain_c,
        shift_c,
    ):
        plan = Plan(mesh, images, w_reduce, w_heads)

        def flat(array):
            return array.transpose(0, 2, 1, 3).reshape(plan.cells, array.shape[3])

        def unflat(array):
            full = (plan.count, plan.span, plan.height, array.shape[1])
            return array.reshape(full).transpose(0, 2, 1, 3)

        outs = run_block(
            plan,
            flat(images),
            sizes,
            flat(limits),
            flat(head_grad),
            w_reduce,
            w_spatial.reshape(9, plan.mid, plan.mid),
            w_expand,
            w_heads,
            *(v.reshape(-1, 128) for v in (gain_a, shift_a, gain_b, shift_b, gain_c, shift_c)),
        )
        outs = widen(plan, *outs)
        return (
            unflat(outs[0]),
            unflat(outs[1]),
            outs[2],
            outs[3].reshape(w_spatial.shape),
            outs[4],
            outs[5],
            *(v.reshape(-1) for v in outs[6:]),
        )

    return jax.shard_map(
        body,
        mesh=mesh,
        in_specs=(cells_spec, P(("task", "dp"), None), cells_spec, cells_spec) + (P(),) * 10,
        out_specs=(cells_spec, cells_spec) + (P(),) * 10,
        check_vma=False,
    )
```

```python
import functools

import jax
import jax.numpy as jnp
from jax import lax
from jax.experimental import pallas as pl
from jax.experimental.pallas import tpu as pltpu
from jax.sharding import PartitionSpec as P

TASKS = 3
EPS = 1e-05
SOFT = 0.01
MESH = pl.DeviceIdType.MESH
F32 = jnp.float32
LOW = jnp.bfloat16
NT = (((1,), (1,)), ((), ()))
TN = (((0,), (0,)), ((), ()))
HEADS, EXPAND, SPATIAL, REDUCE = range(4)
PARTS = (4, 2, 6, 4)
ROUTES = (0, 0, 0, 0, 5, 0, 5, 0, 0, 0, 0, 3, 5, 4, 0, 3)
(
    AFTER_HEADS_0,
    AFTER_HEADS_1,
    AFTER_HEADS_2,
    AFTER_THIRD_0,
    AFTER_THIRD_1,
    AFTER_BACK_B_1,
    AFTER_EXPAND_END,
    AFTER_SECOND,
    AFTER_BACK_A_1,
    AFTER_FIRST,
    AFTER_REDUCE_END,
    AFTER_SPATIAL_END,
    AFTER_LAST_0,
    AFTER_LAST_1,
    AFTER_LAST_2,
    LAST,
) = range(100, 116)
AGENDA = {
    0: (0,),
    1: (10,),
    2: (20,),
    3: (30,),
    AFTER_THIRD_0: (1,),
    AFTER_BACK_B_1: (11, 21,),
    4: (40,),
    5: (50, 31,),
    AFTER_EXPAND_END: (2, 12,),
    AFTER_BACK_A_1: (22, 51, 32,),
    6: (60, 41,),
    7: (70, 3, 13,),
    8: (80,),
    9: (90, 23, 52,),
    10: (100, 33, 42,),
    12: (120, 71,),
    13: (130,),
    14: (140, 61,),
    15: (150, 4, 81,),
    11: (110, 24, 14,),
    AFTER_LAST_0: (91, 53,),
    AFTER_LAST_1: (34,),
    AFTER_LAST_2: (101,),
    LAST: (
        72, 43, 121, 141, 131, 62, 5, 25, 151, 15, 54, 82, 35, 73, 111, 44, 6, 92, 26, 102, 122, 152, 142, 16,
        132, 63, 55, 7, 83, 27, 36, 123, 153, 74, 17, 112, 8, 45, 93, 103, 28, 143, 37, 133, 64, 56, 18, 113,
        84, 124, 46, 154, 75, 94, 104, 38, 134, 144, 65, 114, 57, 85, 76, 135, 47, 125, 155, 66, 95, 105, 86, 145,
        58, 115, 77, 126, 156, 136, 67, 87, 116, 48, 96, 78, 127, 106, 137, 146, 157, 88, 97, 107, 147, 68, 158, 117,
        98, 108, 128, 148, 138, 118,
    ),
}


class Plan:
    def __init__(self, mesh, images, w_reduce, w_heads):
        self.tasks = mesh.shape["task"]
        self.dp = mesh.shape["dp"]
        self.line = self.dp // 2
        self.devices = self.tasks * self.dp
        assert self.tasks == 4 and self.dp % 2 == 0
        assert self.devices & (self.devices - 1) == 0
        self.count, self.height, self.span, self.wide = images.shape
        assert self.height & (self.height - 1) == 0 and self.height % 16 == 0
        self.mid = w_reduce.shape[1]
        self.heads = w_heads.shape[1]
        assert self.mid == 512 and self.heads == 768 and self.wide == 2048
        self.image = self.height * self.span
        self.cells = self.count * self.image
        self.step = self.image + self.height
        self.rows = self.count * self.step - self.height
        self.both = 2 * self.count * self.step - self.height
        self.half = self.wide // 2
        self.depth = -(-self.both // 256) * 256
        assert self.line & (self.line - 1) == 0
        self.levels = self.line.bit_length() - 1
        self.steps = 2 + self.levels
        unit = 16 << self.steps
        self.real = (
            self.heads // 256 * self.half,
            self.half // 256 * self.mid,
            9 * self.mid,
            self.mid // 256 * self.half,
        )
        tuned = self.steps == 4 and all(real % (n * unit) == 0 for real, n in zip(self.real, PARTS))
        self.parts = PARTS if tuned else (1, 1, 1, 1)
        self.base, self.first, self.segments, at = [], [], [], 0
        for real, n in zip(self.real, self.parts):
            self.base.append(at)
            self.first.append(len(self.segments))
            size = -(-real // (n * unit)) * unit
            for _ in range(n):
                index = len(self.segments)
                self.segments.append((index, at, size, ROUTES[index] if tuned else 0))
                at += size
        self.total = at
        self.agenda = AGENDA
        if not tuned:
            self.stride = 2 * self.steps + 1
            self.agenda = {i: (self.stride * i,) for i in range(4)}
            self.agenda[LAST] = [self.stride * i + k for k in range(1, self.stride) for i in range(4)]
        else:
            self.stride = 10


def chunk_of(rows):
    for size in (128, 96, 64, 48, 32, 16):
        if rows % size == 0:
            return size
    raise ValueError(rows)


def column_sum(values):
    return jnp.sum(values.reshape(values.shape[0] // 8, 8, values.shape[1]), axis=0)


def fold(part):
    return jnp.sum(part, axis=0, keepdims=True)


def logistic(values):
    return 0.5 + 0.5 * jnp.tanh(0.5 * values)


def lanes(block, width=128):
    return pl.ds(pl.multiple_of(block * width, width), width)


def span16(start, size):
    return pl.ds(pl.multiple_of(start, 16), size)


def repeat(count, body):
    def step(i, carry):
        body(i)
        return carry

    lax.fori_loop(0, count, step, 0)


def block_kernel(
    plan,
    images,
    sizes,
    limits,
    head_grad,
    w_reduce,
    w_spatial,
    w_expand,
    w_heads,
    gain_a,
    shift_a,
    gain_b,
    shift_b,
    gain_c,
    shift_c,
    head_out,
    grad_images,
    gathered,
    terms,
    received,
    gain_a_grad,
    shift_a_grad,
    gain_b_grad,
    shift_b_grad,
    gain_c_grad,
    shift_c_grad,
    *scratch,
):
    (
        wr,
        ws,
        we,
        wh,
        hg,
        trunk,
        sib_one,
        sib_two,
        img_t,
        merged,
        third,
        first,
        second,
        back,
        hid_a,
        hid_b,
        hid_b_t,
        low_b,
        low_b_all,
        gsc,
        mask,
        coef,
        msg,
        slots,
        count_msg,
        count_slots,
        wide_msg,
        wide_slots,
        total,
        load_sem,
        sum_send,
        sum_recv,
        sib_send,
        sib_recv,
        ring_send,
        ring_recv,
    ) = scratch
    img, stage, low_a = grad_images, head_out, hid_b
    p = plan
    n_img, height, image, step = p.count, p.height, p.image, p.step
    cells, rows, mid, wide, half = p.cells, p.rows, p.mid, p.wide, p.half
    mid_blocks, wide_blocks = mid // 128, wide // 128
    chunk = chunk_of(image)
    task = lax.axis_index("task")
    dp = lax.axis_index("dp")
    core = lax.rem(dp, 2)
    level = dp // 2
    me = task * p.dp + dp
    none = dp // p.dp

    def place(at_task, at_dp):
        return {"task": at_task, "dp": at_dp}

    sibling = place(task, dp + 1 - 2 * core)

    def remote(src, dst, send, recv, device):
        return pltpu.make_async_remote_copy(
            src_ref=src, dst_ref=dst, send_sem=send, recv_sem=recv, device_id=device, device_id_type=MESH
        )

    def take(ref, sem):
        pltpu.make_async_copy(ref, ref, sem).wait()

    barrier = pltpu.get_barrier_semaphore()

    def greet(i):
        other = me ^ (p.devices - 1 - i)
        pl.semaphore_signal(
            barrier,
            inc=1,
            device_id=place(other // p.dp, lax.rem(other, p.dp)),
            device_id_type=MESH,
        )

    loads = {
        "images": (images, img),
        "reduce": (w_reduce, wr),
        "grad": (head_grad, hg.at[pl.ds(0, cells)]),
        "heads": (w_heads, wh),
        "limits": (limits, trunk),
        "expand": (w_expand, we),
    }
    order = list(loads)

    def load(key):
        pltpu.make_async_copy(*loads[key], load_sem.at[order.index(key)]).start()

    load("images")
    load("reduce")
    repeat(p.devices - 1, greet)
    for key in order[2:]:
        load(key)
    for row_tap in range(3):
        for col_tap in range(3):
            pltpu.make_async_copy(
                w_spatial.at[row_tap * 3 + col_tap],
                ws.at[col_tap, pl.ds(row_tap * mid, mid)],
                load_sem.at[len(order)],
            ).start()

    def loaded(key):
        pltpu.make_async_copy(*loads[key], load_sem.at[order.index(key)]).wait()

    mask[...] = jnp.zeros_like(mask)
    for k in range(n_img):
        at = lax.broadcasted_iota(jnp.int32, (image, 128), 0)
        inside = ((at & (height - 1)) < sizes[k, 0]) & ((at // height) < sizes[k, 1])
        mask[pl.ds(k * step, image)] = jnp.where(inside, 1.0, 0.0)
    zero_rows = jnp.zeros((height, 3 * mid), LOW)
    for k in range(2 * n_img + 1):
        hid_a[pl.ds(k * step, height)] = zero_rows
    beyond = p.depth - p.both
    hid_a[pl.ds(p.both + 2 * height, beyond)] = jnp.zeros((beyond, 3 * mid), LOW)
    low_b_all[pl.ds(p.both, beyond)] = jnp.zeros((beyond, mid // 2), LOW)
    for k in range(n_img + 1):
        low_b[pl.ds(k * step, height)] = zero_rows
    low_b_all[pl.ds(rows, height)] = jnp.zeros((height, mid // 2), LOW)

    def to_all(k, src, dst):
        def send(i):
            other = me ^ (p.devices - 1 - i)
            device = place(other // p.dp, lax.rem(other, p.dp))
            remote(src, dst.at[me], sum_send.at[k], sum_recv.at[k], device).start()

        repeat(p.devices - 1, send)

    def from_all(k, dst):
        some = dst.at[pl.ds(0, p.devices - 1)]
        take(some, sum_recv.at[k])
        take(some, sum_send.at[k])

    def sum_start(k, slot):
        slots[slot, me] = msg[k]
        to_all(k, msg.at[k], slots.at[slot])

    def sum_finish(k, slot):
        from_all(k, slots.at[slot])
        total[pl.ds(0, 2 * mid_blocks)] = jnp.sum(slots[slot], axis=0)

    plane = 2 * p.tasks
    spot = task * 2 + core

    def wide_start(k):
        wide_slots[k, spot] = wide_msg[k, 0]
        for i in range(plane - 1, 0, -1):
            other = spot ^ i
            remote(
                wide_msg.at[k, 0],
                wide_slots.at[k, spot],
                sum_send.at[5 + 2 * k],
                sum_recv.at[5 + 2 * k],
                place(other // 2, level * 2 + lax.rem(other, 2)),
            ).start()

    def wide_turn(k):
        some = wide_slots.at[k, pl.ds(0, plane - 1)]
        take(some, sum_recv.at[5 + 2 * k])
        take(some, sum_send.at[5 + 2 * k])
        partial = jnp.sum(wide_slots[k, pl.ds(0, plane)], axis=0)
        wide_msg[k, 1] = partial
        wide_slots[k, plane + level] = partial
        for i in range(p.line - 1, 0, -1):
            other = level ^ i
            remote(
                wide_msg.at[k, 1],
                wide_slots.at[k, plane + level],
                sum_send.at[6 + 2 * k],
                sum_recv.at[6 + 2 * k],
                place(task, other * 2 + core),
            ).start()

    def wide_finish(k):
        some = wide_slots.at[k, pl.ds(plane, p.line - 1)]
        take(some, sum_recv.at[6 + 2 * k])
        take(some, sum_send.at[6 + 2 * k])
        total[...] = jnp.sum(wide_slots[k, pl.ds(plane, p.line)], axis=0)

    low_bit, high_bit = lax.rem(task, 2), task // 2
    along_x = (low_bit, place(task + 1 - 2 * low_bit, dp))
    along_y = (high_bit, place(task + 2 - 4 * high_bit, dp))
    along_z = []
    for k in range(p.levels):
        bit = lax.rem(level // 2**k, 2)
        along_z.append((bit, place(task, dp + 2 ** (k + 1) - 2 ** (k + 2) * bit)))

    def route(kind, part):
        one, two = (along_x, along_y) if part == 0 else (along_y, along_x)
        return (
            [one, two, *along_z],
            [one, *along_z, two],
            [*along_z, one, two],
            [one, *along_z[:1], two, *along_z[1:]],
            [*along_z[:1], one, *along_z[1:], two],
            [*along_z[:1], one, two, *along_z[1:]],
        )[kind]

    def held(segment, part, k):
        _, at, size, kind = segment
        for j, (bit, _) in enumerate(route(kind, part)[:k]):
            at = at + bit * (size >> (j + 1))
        return at

    def inbox(segment, k):
        _, at, size, _ = segment
        return at + size - (size >> k)

    def put(family, row, values):
        low = values.astype(LOW)
        at = span16(p.base[family] + row, low.shape[0])
        terms[0, at, :] = low[:, :128]
        terms[1, at, :] = low[:, 128:]

    def add_received(segment, part, at, rows_here, k):
        starts = [inbox(segment, j) + at - held(segment, part, j + 1) for j in range(k)]
        size = chunk_of(rows_here)

        def one(i):
            here = span16(at + i * size, size)
            acc = terms[part, here, :].astype(F32)
            for start in starts:
                acc = acc + received[part, span16(start + i * size, size), :].astype(F32)
            terms[part, here, :] = acc.astype(LOW)

        repeat(rows_here // size, one)

    def some_of(segment, rows_here):
        return received.at[:, pl.ds(segment[1], rows_here)]

    def ring(segment, k):
        at = k - p.steps - 1 if k > p.steps else k
        return ring_send.at[segment[0], 0], ring_recv.at[segment[0], at]

    def settle(segment, k, arrived, sent):
        send, recv = ring(segment, k)
        take(some_of(segment, arrived), recv)
        take(some_of(segment, sent), send)

    def beside(segment):
        return ring_send.at[segment[0], 1], ring_recv.at[segment[0], p.steps + 1]

    def home(part, start, rows_here):
        return gathered.at[core, part, span16(start, rows_here)]

    def scatter(segment, k):
        _, _, size, kind = segment
        here = size >> (k + 1)
        if k:
            settle(segment, k - 1, 2 * here, 2 * here)
        for part in range(2):
            bit, partner = route(kind, part)[k]
            at = held(segment, part, k) + (1 - bit) * here
            if k:
                add_received(segment, part, at, here, k)
            remote(
                terms.at[part, span16(at, here)],
                received.at[part, pl.ds(inbox(segment, k), here)],
                *ring(segment, k),
                partner,
            ).start()

    def gather(segment, k):
        _, _, size, kind = segment
        here = size >> (k + 1)
        if k == p.steps - 1:
            settle(segment, k, here, here)
        else:
            settle(segment, p.steps + k + 1, here // 2, here if k == p.steps - 2 else here // 2)
        for part in range(2):
            partner = route(kind, part)[k][1]
            at = held(segment, part, k + 1)
            mine = ours = home(part, at, here)
            if k == p.steps - 1:
                add_received(segment, part, at, here, p.steps)
                mine = terms.at[part, span16(at, here)]
                pltpu.make_async_copy(mine, ours, ring_send.at[segment[0], 0]).start()
            remote(mine, ours, *ring(segment, p.steps + k), partner).start()
            if k == 0:
                remote(ours, ours, *beside(segment), sibling).start()

    shared = []

    def share(segment):
        index, at, size, kind = segment
        settle(segment, p.steps, size // 2, size // 2)
        take(some_of(segment, size // 2), ring_send.at[index, 1])
        for part in range(2):
            bit = route(kind, part)[0][0]
            ours = home(part, at + (1 - bit) * (size // 2), size // 2)
            remote(ours, ours, *beside(segment), sibling).start()
        rows_here = pl.ds(at, size)
        pltpu.make_async_copy(gathered.at[core, :, rows_here], received.at[:, rows_here], ring_send.at[index, 0]).start()
        for other in shared[-1:]:
            bring(other)
        shared.append(segment)

    def bring(segment):
        index, at, size, _ = segment
        send, recv = beside(segment)
        take(some_of(segment, size), recv)
        take(some_of(segment, size // 2), send)
        rows_here = pl.ds(at, size)
        pltpu.make_async_copy(gathered.at[1 - core, :, rows_here], terms.at[:, rows_here], ring_send.at[index, 0]).start()

    def travel(point):
        for todo in p.agenda.get(point, ()):
            segment, k = p.segments[todo // p.stride], todo % p.stride
            if k < p.steps:
                scatter(segment, k)
            elif k < 2 * p.steps:
                gather(segment, 2 * p.steps - 1 - k)
            else:
                share(segment)

    other_half = pl.ds(pl.multiple_of((1 - core) * half, 128), half)
    other_quarter = pl.ds(pl.multiple_of(mid + (1 - core) * (mid // 2), 128), mid // 2)
    swaps = (
        (images.at[:, other_half], sib_one),
        (head_grad, hg.at[pl.ds(cells, cells)]),
        (hid_a.at[pl.ds(height, rows)], hid_a.at[pl.ds(n_img * step + height, rows)]),
        (hid_b.at[pl.ds(0, cells)], hid_b.at[pl.ds(cells, cells)]),
        (trunk.at[:, other_half], sib_two),
        (trunk.at[:, other_half], sib_one),
        (low_b.at[pl.ds(height, rows), other_quarter], low_b_all.at[pl.ds(rows + height, rows)]),
        (low_a.at[pl.ds(0, cells)], low_a.at[pl.ds(cells, cells)]),
    )

    def swap(k):
        src, dst = swaps[k]
        return remote(src, dst, sib_send.at[k], sib_recv.at[k], sibling)

    def put_stats(ref, at, blocks, block, one, two):
        ref[(*at, pl.ds(block, 1))] = fold(one)
        ref[(*at, pl.ds(blocks + block, 1))] = fold(two)

    count_msg[...] = fold(column_sum(mask[...]))
    count_slots[me] = count_msg[...]
    loaded("images")
    loaded("reduce")

    def first_layer(nb):
        values = jnp.dot(img[...], wr[:, lanes(nb, 512)], preferred_element_type=F32)
        for h in range(4):
            one = two = jnp.zeros((8, 128), F32)
            for k in range(n_img):
                at = pl.ds(k * image, image)
                part = values[k * image : (k + 1) * image, h * 128 : h * 128 + 128]
                part = part * mask[pl.ds(k * step, image)]
                first[at, lanes(4 * nb + h)] = part
                one = one + column_sum(part)
                two = two + column_sum(part * part)
            put_stats(msg, (1,), mid_blocks, 4 * nb + h, one, two)

    first_layer(none)

    loaded("grad")
    loaded("heads")
    loaded("limits")
    head = p.heads // TASKS

    def merge(nb):
        at_wide = pl.ds(pl.multiple_of(nb * 256, 256), 256)
        for t in range(TASKS):
            at_head = pl.ds(t * head, head)
            values = lax.dot_general(
                hg[pl.ds(0, cells), at_head], wh[at_wide, at_head], NT, preferred_element_type=F32
            )
            gsc[t] = values.astype(LOW)

        def drop(i):
            at = span16(i * chunk, chunk)
            per = image // chunk
            valid = mask[span16(i // per * step + lax.rem(i, per) * chunk, chunk)]
            for h in range(2):
                grads = [gsc[t, at, pl.ds(h * 128, 128)].astype(F32) for t in range(TASKS)]
                signed, size, kept = 0.0, 0.0, 0.0
                for g in grads:
                    square = g * g + SOFT
                    signed = signed + g
                    size = size + square * lax.rsqrt(square)
                    kept = kept + jnp.tanh(g * 5.0) * g
                limit = trunk[at, lanes(2 * nb + h)].astype(F32)
                lean = jnp.tanh(2.5 + 2.5 * (signed / size) - 5.0 * limit)
                merged[at, lanes(2 * nb + h)] = (0.25 * valid) * (signed + lean * kept)

        repeat(cells // chunk, drop)

    blocks = wide // 256
    cuts = [0, blocks // 4, blocks * 5 // 8, blocks * 6 // 8, blocks]

    def merge_some(k):
        lax.fori_loop(cuts[k], cuts[k + 1], lambda i, carry: (merge(i), carry)[1], 0)

    merge_some(0)
    pl.semaphore_wait(barrier, p.devices - 1)
    to_all(0, count_msg, count_slots)
    sum_start(1, 1)
    swap(0).start()
    swap(1).start()
    merge_some(1)

    def turn_images(j):
        own = img[:, pl.ds(pl.multiple_of(core * half + j * 128, 128), 128)]
        both = jnp.concatenate([own, sib_one[:, lanes(j)]], axis=0)
        img_t[lanes(j), :] = both.T

    def center(blocks):
        mean = total[pl.ds(0, blocks)] / count
        spread = total[pl.ds(blocks, blocks)] / count - mean * mean + EPS
        coef[0, pl.ds(0, blocks)] = mean
        coef[1, pl.ds(0, blocks)] = lax.rsqrt(spread)

    def row(k, block):
        return coef[k, pl.ds(block, 1)]

    def edges():
        at = lax.broadcasted_iota(jnp.int32, (image, 128), 0) & (height - 1)
        return at != 0, at != height - 1

    def put_shifted(ref, start, block, values, above, below):
        at = pl.ds(start, image)
        up = jnp.where(above, pltpu.roll(values, 1, 0), 0.0)
        down = jnp.where(below, pltpu.roll(values, image - 1, 0), 0.0)
        for h, part in enumerate((up, values, down)):
            ref[at, pl.ds(pl.multiple_of(h * mid + block * 128, 128), 128)] = part.astype(LOW)

    from_all(0, count_slots)
    count = jnp.sum(count_slots[...], axis=0)
    sum_finish(1, 1)
    center(mid_blocks)
    coef[2, pl.ds(0, mid_blocks)] = coef[1, pl.ds(0, mid_blocks)]

    def normalize_a(cb):
        above, below = edges()
        gain, shift = gain_a[pl.ds(cb, 1)], shift_a[pl.ds(cb, 1)]
        for k in range(n_img):
            at = pl.ds(k * image, image)
            hat = (first[at, lanes(cb)] - row(0, cb)) * row(1, cb)
            first[at, lanes(cb)] = hat
            pre = hat * gain + shift
            hidden = pre * logistic(pre) * mask[pl.ds(k * step, image)]
            put_shifted(hid_a, height + k * step, cb, hidden, above, below)

    repeat(mid_blocks, normalize_a)
    swap(2).start()

    take(ws, load_sem.at[len(order)])

    def second_layer(nb):
        values = None
        for j in range(3):
            term = jnp.dot(
                hid_a[pl.ds(j * height, rows)], ws[j, :, lanes(nb, 512)], preferred_element_type=F32
            )
            values = term if values is None else values + term
        for h in range(4):
            part = values[:, h * 128 : h * 128 + 128] * mask[...]
            second[:, lanes(4 * nb + h)] = part
            put_stats(msg, (2,), mid_blocks, 4 * nb + h, column_sum(part), column_sum(part * part))

    second_layer(none)
    sum_start(2, 0)
    merge_some(2)
    swap(0).wait_recv()
    repeat(half // 128, turn_images)
    sum_finish(2, 0)
    center(mid_blocks)
    coef[3, pl.ds(0, mid_blocks)] = coef[1, pl.ds(0, mid_blocks)]

    def normalize_b(cb):
        gain, shift = gain_b[pl.ds(cb, 1)], shift_b[pl.ds(cb, 1)]
        for k in range(n_img):
            at = pl.ds(k * step, image)
            hat = (second[at, lanes(cb)] - row(0, cb)) * row(1, cb)
            second[at, lanes(cb)] = hat
            pre = hat * gain + shift
            hidden = pre * logistic(pre) * mask[at]
            hid_b[pl.ds(k * image, image), lanes(cb)] = hidden.astype(LOW)

    repeat(mid_blocks, normalize_b)
    swap(3).start()

    loaded("expand")

    def third_layer(nb):
        values = jnp.dot(hid_b[pl.ds(0, cells)], we[:, lanes(nb, 512)], preferred_element_type=F32)
        third[:, lanes(nb, 512)] = values
        for h in range(4):
            part = values[:, h * 128 : h * 128 + 128]
            put_stats(
                wide_msg, (0, 0), wide_blocks, 4 * nb + h, column_sum(part), column_sum(part * part)
            )

    repeat(wide // 512, third_layer)
    wide_start(0)
    merge_some(3)
    swap(3).wait()
    wide_turn(0)

    def turn_hidden(j):
        hid_b_t[lanes(j), :] = hid_b[:, lanes(j)].T

    repeat(mid_blocks, turn_hidden)
    wide_finish(0)
    center(wide_blocks)

    scale_c = gain_c[...] * coef[1]
    coef[7] = scale_c
    coef[8] = shift_c[...] - coef[0] * scale_c

    def normalize_c(i):
        cb = lax.rem(i + (1 - core) * (wide_blocks // 2), wide_blocks)
        one = two = jnp.zeros((8, 128), F32)
        for k in range(n_img):
            for r in range(image // chunk):
                at = pl.ds(k * image + r * chunk, chunk)
                valid = mask[pl.ds(k * step + r * chunk, chunk)]
                raw = third[at, lanes(cb)]
                pre = raw * row(7, cb) + (row(8, cb) + img[at, lanes(cb)].astype(F32))
                h = 0.5 * pre
                t = jnp.tanh(h)
                value = h + h * t
                trunk[at, lanes(cb)] = (value * valid).astype(LOW)
                up = merged[at, lanes(cb)] * ((1.0 + value) + t * (1.0 - value))
                merged[at, lanes(cb)] = up
                one = one + column_sum(up)
                two = two + column_sum(up * raw)
        put_stats(wide_msg, (1, 0), wide_blocks, cb, one, two)

    def both_halves(body, k, point):
        repeat(wide_blocks // 2, body)
        swap(k).start()
        travel(point)
        repeat(wide_blocks // 2, lambda i: body(i + wide_blocks // 2))

    both_halves(normalize_c, 4, None)
    wide_start(1)

    swap(1).wait_recv()
    swap(4).wait_recv()

    def heads_gradient(i):
        own = trunk[:, pl.ds(pl.multiple_of(core * half + i * 512, 128), 512)]
        both = jnp.concatenate([own, sib_two[:, lanes(i, 512)]], axis=0)
        values = lax.dot_general(both, hg[...], TN, preferred_element_type=F32)
        for q in range(2):
            for b in range(p.heads // 256):
                part = values[q * 256 : q * 256 + 256, b * 256 : b * 256 + 256]
                put(HEADS, (2 * i + q) * p.heads + b * 256, part)

    def each(family, first_part, last_part, count, body):
        n = p.parts[family]
        for i in range(first_part, last_part):
            body(i + none)
            for done in range(i * n // count, (i + 1) * n // count):
                travel(p.first[family] + done)

    each(HEADS, 0, half // 512, half // 512, heads_gradient)
    wide_turn(1)

    def head_layer(nb):
        values = jnp.dot(trunk[...], wh[:, lanes(nb, 256)], preferred_element_type=F32)
        stage[:, lanes(nb, 256)] = values.astype(LOW)

    for i, point in enumerate((AFTER_HEADS_0, AFTER_HEADS_1, AFTER_HEADS_2)):
        head_layer(i)
        travel(point)
    swap(4).wait_send()
    wide_finish(1)

    def backward(blocks, gain, inverse):
        scale = gain * inverse
        coef[4, pl.ds(0, blocks)] = scale
        coef[5, pl.ds(0, blocks)] = -scale * total[pl.ds(0, blocks)] / count
        coef[6, pl.ds(0, blocks)] = -scale * total[pl.ds(blocks, blocks)] / count

    sum_up = total[pl.ds(0, wide_blocks)]
    sum_up_hat = (total[pl.ds(wide_blocks, wide_blocks)] - coef[0] * sum_up) * coef[1]
    shift_c_grad[...] = sum_up
    gain_c_grad[...] = sum_up_hat
    per_hat = -coef[7] * sum_up_hat / count
    coef[4] = coef[7]
    coef[5] = -coef[7] * sum_up / count - per_hat * coef[1] * coef[0]
    coef[6] = per_hat * coef[1]

    def third_gradient(i):
        cb = lax.rem(i + (1 - core) * (wide_blocks // 2), wide_blocks)
        for k in range(n_img):
            for r in range(image // chunk):
                at = pl.ds(k * image + r * chunk, chunk)
                valid = mask[pl.ds(k * step + r * chunk, chunk)]
                down = merged[at, lanes(cb)] * row(4, cb) + row(5, cb) + third[at, lanes(cb)] * row(6, cb)
                trunk[at, lanes(cb)] = (down * valid).astype(LOW)

    both_halves(third_gradient, 5, AFTER_THIRD_0)
    travel(AFTER_THIRD_1)

    def slope_of(pre):
        gate = logistic(pre)
        return gate * (1.0 + pre * (1.0 - gate))

    def third_back(nb):
        values = lax.dot_general(trunk[...], we[lanes(nb, 512), :], NT, preferred_element_type=F32)
        for h in range(4):
            cb = 4 * nb + h
            one = two = jnp.zeros((8, 128), F32)
            for k in range(n_img):
                at = pl.ds(k * image, image)
                hat = second[pl.ds(k * step, image), lanes(cb)]
                pre = hat * gain_b[pl.ds(cb, 1)] + shift_b[pl.ds(cb, 1)]
                up = values[k * image : (k + 1) * image, h * 128 : h * 128 + 128]
                up = up * slope_of(pre) * mask[pl.ds(k * step, image)]
                back[at, lanes(cb)] = up
                one = one + column_sum(up)
                two = two + column_sum(up * hat)
            put_stats(msg, (3,), mid_blocks, cb, one, two)

    third_back(none)
    sum_start(3, 1)
    travel(AFTER_BACK_B_1)
    swap(5).wait_recv()

    def expand_gradient(i):
        own = trunk[:, pl.ds(pl.multiple_of(core * half + i * 512, 128), 512)]
        both = jnp.concatenate([own, sib_one[:, lanes(i, 512)]], axis=0)
        values = jnp.dot(hid_b_t[...], both, preferred_element_type=F32)
        for q in range(2):
            put(EXPAND, (2 * i + q) * mid, values[:, q * 256 : q * 256 + 256])

    each(EXPAND, 0, half // 512, half // 512, expand_gradient)
    travel(AFTER_EXPAND_END)
    sum_finish(3, 1)
    shift_b_grad[...] = total[pl.ds(0, mid_blocks)]
    gain_b_grad[...] = total[pl.ds(mid_blocks, mid_blocks)]
    backward(mid_blocks, gain_b[...], coef[3, pl.ds(0, mid_blocks)])

    def second_gradient(cb):
        above, below = edges()
        for k in range(n_img):
            at = pl.ds(k * step, image)
            down = back[pl.ds(k * image, image), lanes(cb)] * row(4, cb) + row(5, cb)
            down = (down + second[at, lanes(cb)] * row(6, cb)) * mask[at]
            put_shifted(low_b, height + k * step, cb, down, above, below)

    repeat(mid_blocks, second_gradient)
    swap(6).start()
    own_quarter = pl.ds(pl.multiple_of(mid + core * (mid // 2), 128), mid // 2)
    low_b_all[pl.ds(0, rows)] = low_b[pl.ds(height, rows), own_quarter]
    travel(AFTER_SECOND)

    def second_back(nb):
        values = None
        for i in range(3):
            for j in range(3):
                term = lax.dot_general(
                    low_b[pl.ds((2 - j) * height, rows), pl.ds((2 - i) * mid, mid)],
                    ws[j, pl.ds(pl.multiple_of(i * mid + nb * 512, 256), 512), :],
                    NT,
                    preferred_element_type=F32,
                )
                values = term if values is None else values + term
        for h in range(4):
            cb = 4 * nb + h
            one = two = jnp.zeros((8, 128), F32)
            for k in range(n_img):
                at = pl.ds(k * image, image)
                hat = first[at, lanes(cb)]
                pre = hat * gain_a[pl.ds(cb, 1)] + shift_a[pl.ds(cb, 1)]
                up = values[k * step : k * step + image, h * 128 : h * 128 + 128]
                up = up * slope_of(pre) * mask[pl.ds(k * step, image)]
                back[at, lanes(cb)] = up
                one = one + column_sum(up)
                two = two + column_sum(up * hat)
            put_stats(msg, (4,), mid_blocks, cb, one, two)

    second_back(none)
    sum_start(4, 0)
    travel(AFTER_BACK_A_1)
    swap(2).wait_recv()
    swap(6).wait_recv()
    def spatial_gradient(i):
        j, k = i // 2, lax.rem(i, 2)
        values = lax.dot_general(
            hid_a[span16(j * height, p.depth), lanes(k, 768)], low_b_all[...], TN, preferred_element_type=F32
        )
        put(SPATIAL, i * 768, values)

    each(SPATIAL, 0, 5, 6, spatial_gradient)
    sum_finish(4, 0)
    shift_a_grad[...] = total[pl.ds(0, mid_blocks)]
    gain_a_grad[...] = total[pl.ds(mid_blocks, mid_blocks)]
    backward(mid_blocks, gain_a[...], coef[2, pl.ds(0, mid_blocks)])

    def first_gradient(cb):
        for k in range(n_img):
            at = pl.ds(k * image, image)
            down = back[at, lanes(cb)] * row(4, cb) + row(5, cb) + first[at, lanes(cb)] * row(6, cb)
            low_a[at, lanes(cb)] = (down * mask[pl.ds(k * step, image)]).astype(LOW)

    repeat(mid_blocks, first_gradient)
    swap(7).start()
    travel(AFTER_FIRST)
    swap(7).wait_recv()

    def reduce_gradient(i):
        values = jnp.dot(img_t[lanes(i, 512), :], low_a[...], preferred_element_type=F32)
        for q in range(2):
            for b in range(mid // 256):
                part = values[q * 256 : q * 256 + 256, b * 256 : b * 256 + 256]
                put(REDUCE, (2 * i + q) * mid + b * 256, part)

    each(REDUCE, 0, half // 512, half // 512, reduce_gradient)
    travel(AFTER_REDUCE_END)
    each(SPATIAL, 5, 6, 6, spatial_gradient)
    travel(AFTER_SPATIAL_END)

    def first_back(nb):
        values = lax.dot_general(low_a[pl.ds(0, cells)], wr[lanes(nb, 512), :], NT, preferred_element_type=F32)
        for h in range(4):
            for k in range(n_img):
                at = pl.ds(k * image, image)
                part = values[k * image : (k + 1) * image, h * 128 : h * 128 + 128]
                part = (part + merged[at, lanes(4 * nb + h)]) * mask[pl.ds(k * step, image)]
                img[at, lanes(4 * nb + h)] = part.astype(LOW)

    for i, point in enumerate((AFTER_LAST_0, AFTER_LAST_1, AFTER_LAST_2, None)):
        first_back(i + none)
        travel(point)

    travel(LAST)
    bring(shared[-1])
    for index, at, size, _ in p.segments:
        take(gathered.at[:, :, pl.ds(at, size)], ring_send.at[index, 0])
    for k in (0, 1, 2, 5, 6, 7):
        swap(k).wait_send()


def run_block(plan, *arrays):
    p = plan
    cells, rows, mid, wide, half = p.cells, p.rows, p.mid, p.wide, p.half
    mid_blocks, wide_blocks = mid // 128, wide // 128
    anywhere = pl.BlockSpec(memory_space=pl.ANY)
    vmem = pl.BlockSpec(memory_space=pltpu.VMEM)
    smem = pl.BlockSpec(memory_space=pltpu.SMEM)
    shape = jax.ShapeDtypeStruct
    scratch = [
        pltpu.VMEM((wide, mid), LOW),
        pltpu.VMEM((3, 3 * mid, mid), LOW),
        pltpu.VMEM((mid, wide), LOW),
        pltpu.VMEM((wide, p.heads), LOW),
        pltpu.VMEM((2 * cells, p.heads), LOW),
        pltpu.VMEM((cells, wide), LOW),
        pltpu.VMEM((cells, half), LOW),
        pltpu.VMEM((cells, half), LOW),
        pltpu.VMEM((half, 2 * cells), LOW),
        pltpu.VMEM((cells, wide), F32),
        pltpu.VMEM((cells, wide), F32),
        pltpu.VMEM((cells, mid), F32),
        pltpu.VMEM((rows, mid), F32),
        pltpu.VMEM((cells, mid), F32),
        pltpu.VMEM((p.depth + 2 * p.height, 3 * mid), LOW),
        pltpu.VMEM((2 * cells, mid), LOW),
        pltpu.VMEM((mid, 2 * cells), LOW),
        pltpu.VMEM((rows + 2 * p.height, 3 * mid), LOW),
        pltpu.VMEM((p.depth, mid // 2), LOW),
        pltpu.VMEM((TASKS, cells, 256), LOW),
        pltpu.VMEM((rows, 128), F32),
        pltpu.VMEM((9, wide_blocks, 128), F32),
        pltpu.VMEM((5, 2 * mid_blocks, 128), F32),
        pltpu.VMEM((2, p.devices, 2 * mid_blocks, 128), F32),
        pltpu.VMEM((1, 128), F32),
        pltpu.VMEM((p.devices, 1, 128), F32),
        pltpu.VMEM((2, 2, 2 * wide_blocks, 128), F32),
        pltpu.VMEM((2, 2 * p.tasks + p.line, 2 * wide_blocks, 128), F32),
        pltpu.VMEM((2 * wide_blocks, 128), F32),
        pltpu.SemaphoreType.DMA((7,)),
        pltpu.SemaphoreType.DMA((9,)),
        pltpu.SemaphoreType.DMA((9,)),
        pltpu.SemaphoreType.DMA((8,)),
        pltpu.SemaphoreType.DMA((8,)),
        pltpu.SemaphoreType.DMA((len(p.segments), 2)),
        pltpu.SemaphoreType.DMA((len(p.segments), p.steps + 2)),
    ]
    return pl.pallas_call(
        functools.partial(block_kernel, plan),
        out_shape=(
            pltpu.VMEM((cells, p.heads), LOW),
            pltpu.VMEM((cells, wide), LOW),
            shape((2, 2, p.total, 128), LOW),
            *[pltpu.VMEM((2, p.total, 128), LOW)] * 2,
            *[pltpu.VMEM((mid_blocks, 128), F32)] * 4,
            *[pltpu.VMEM((wide_blocks, 128), F32)] * 2,
        ),
        in_specs=[anywhere, smem] + [anywhere] * 6 + [vmem] * 6,
        out_specs=[vmem] * 2 + [anywhere] + [vmem] * 8,
        scratch_shapes=scratch,
        compiler_params=pltpu.CompilerParams(
            collective_id=0, has_side_effects=True, vmem_limit_bytes=47 * 2**20
        ),
        name="block",
    )(*arrays)


def widen_kernel(plan, *refs):
    p = plan
    other, own, heads_in, images_in = refs[:4]
    small_in = refs[4:10]
    heads_out, images_out, out_reduce, out_spatial, out_expand, out_heads = refs[10:16]
    small_out = refs[16:22]
    reduce, spatial, expand, heads, out_sem, pass_sem = refs[22:]
    passes = (
        pltpu.make_async_copy(heads_in, heads_out, pass_sem.at[0]),
        pltpu.make_async_copy(images_in, images_out, pass_sem.at[1]),
    )
    for src, dst in zip(small_in, small_out):
        dst[...] = src[...]
    where = (
        (heads, out_heads, p.half, p.heads, True),
        (expand, out_expand, p.mid, p.half, False),
        (spatial, out_spatial, 9 * p.mid, p.mid // 2, False),
        (reduce, out_reduce, p.half, p.mid, True),
    )
    copies = []
    per_tap = p.mid // 256
    size = 256
    mine = lax.rem(lax.axis_index("dp"), 2)
    for s, (wide, out, height, width, by_rows) in enumerate(where):
        for low, core in ((own, mine), (other, 1 - mine)):
            row_at = core * height if by_rows else 0
            col_at = 0 if by_rows else core * width
            sem = out_sem.at[s, core]

            def one(i, s=s, wide=wide, out=out, low=low, row_at=row_at, col_at=col_at, sem=sem):
                rows = pl.ds(pl.multiple_of(row_at + i * size, size), size)
                for b in range(width // 256):
                    if s == EXPAND:
                        start = b * height + i * size
                    elif s == SPATIAL:
                        tap, sub = i // per_tap, lax.rem(i, per_tap)
                        start = (lax.rem(tap, 3) * 3 + tap // 3) * p.mid + sub * size
                    else:
                        start = i * width + b * size
                    src = pl.ds(pl.multiple_of(p.base[s] + start, size), size)
                    for part in range(2):
                        cols = pl.ds(pl.multiple_of(col_at + b * 256 + part * 128, 128), 128)
                        wide[rows, cols] = low[part, src, :].astype(F32)
                at = (rows, pl.ds(pl.multiple_of(col_at, 128), width))
                pltpu.make_async_copy(wide.at[at], out.at[at], sem).start()

            repeat(height // size, one)
            at = (pl.ds(pl.multiple_of(row_at, size), height), pl.ds(pl.multiple_of(col_at, 128), width))
            copies.append(pltpu.make_async_copy(wide.at[at], out.at[at], sem))
    for one in passes:
        one.start()
    for one in copies + list(passes):
        one.wait()


def widen(plan, head_out, grad_images, _, terms, received, *small):
    p = plan
    anywhere = pl.BlockSpec(memory_space=pl.ANY)
    vmem = pl.BlockSpec(memory_space=pltpu.VMEM)
    shape = jax.ShapeDtypeStruct
    full = ((p.wide, p.mid), (9 * p.mid, p.mid), (p.mid, p.wide), (p.wide, p.heads))
    held = (terms, received, head_out, grad_images, *small)
    return pl.pallas_call(
        functools.partial(widen_kernel, plan),
        out_shape=(
            shape(head_out.shape, LOW),
            shape(grad_images.shape, LOW),
            *(shape(one, F32) for one in full),
            *(shape(one.shape, F32) for one in small),
        ),
        in_specs=[vmem] * 10,
        out_specs=[anywhere] * 6 + [vmem] * 6,
        scratch_shapes=[
            *(pltpu.VMEM(one, F32) for one in full),
            pltpu.SemaphoreType.DMA((4, 2)),
            pltpu.SemaphoreType.DMA((2,)),
        ],
        compiler_params=pltpu.CompilerParams(vmem_limit_bytes=32 * 2**20),
        name="widen",
    )(*(pltpu.with_memory_space_constraint(one, pltpu.VMEM) for one in held))


def solution(mesh):
    cells_spec = P(("task", "dp"), None, None, None)

    def body(
        images,
        sizes,
        limits,
        head_grad,
        w_reduce,
        w_spatial,
        w_expand,
        w_heads,
        gain_a,
        shift_a,
        gain_b,
        shift_b,
        gain_c,
        shift_c,
    ):
        plan = Plan(mesh, images, w_reduce, w_heads)

        def flat(array):
            return array.transpose(0, 2, 1, 3).reshape(plan.cells, array.shape[3])

        def unflat(array):
            full = (plan.count, plan.span, plan.height, array.shape[1])
            return array.reshape(full).transpose(0, 2, 1, 3)

        outs = run_block(
            plan,
            flat(images),
            sizes,
            flat(limits),
            flat(head_grad),
            w_reduce,
            w_spatial.reshape(9, plan.mid, plan.mid),
            w_expand,
            w_heads,
            *(v.reshape(-1, 128) for v in (gain_a, shift_a, gain_b, shift_b, gain_c, shift_c)),
        )
        outs = widen(plan, *outs)
        return (
            unflat(outs[0]),
            unflat(outs[1]),
            outs[2],
            outs[3].reshape(w_spatial.shape),
            outs[4],
            outs[5],
            *(v.reshape(-1) for v in outs[6:]),
        )

    return jax.shard_map(
        body,
        mesh=mesh,
        in_specs=(cells_spec, P(("task", "dp"), None), cells_spec, cells_spec) + (P(),) * 10,
        out_specs=(cells_spec, cells_spec) + (P(),) * 10,
        check_vma=False,
    )
```

```python
import functools

import jax
import jax.numpy as jnp
from jax import lax
from jax.experimental import pallas as pl
from jax.experimental.pallas import tpu as pltpu
from jax.sharding import PartitionSpec as P

TASKS = 3
EPS = 1e-05
SOFT = 0.01
MESH = pl.DeviceIdType.MESH
F32 = jnp.float32
LOW = jnp.bfloat16
NT = (((1,), (1,)), ((), ()))
TN = (((0,), (0,)), ((), ()))
HEADS, EXPAND, SPATIAL, REDUCE = range(4)
PARTS = (4, 2, 6, 4)
ROUTES = (0, 0, 0, 0, 5, 0, 5, 0, 0, 0, 0, 4, 5, 0, 0, 3)
(
    AFTER_HEADS_0,
    AFTER_HEADS_1,
    AFTER_HEADS_2,
    AFTER_THIRD_0,
    AFTER_THIRD_1,
    AFTER_BACK_B_1,
    AFTER_EXPAND_END,
    AFTER_SECOND,
    AFTER_TAP_0,
    AFTER_TAP_1,
    AFTER_BACK_A_1,
    AFTER_FIRST,
    AFTER_REDUCE_END,
    AFTER_SPATIAL_END,
    AFTER_LAST_0,
    AFTER_LAST_1,
    AFTER_LAST_2,
    LAST,
) = range(100, 118)
AGENDA = {
    0: (0,),
    1: (10,),
    2: (20,),
    3: (30,),
    AFTER_THIRD_0: (1,),
    AFTER_BACK_B_1: (11, 21,),
    4: (40,),
    5: (50, 31,),
    AFTER_EXPAND_END: (2, 12,),
    AFTER_TAP_0: (22,),
    AFTER_BACK_A_1: (51, 32,),
    6: (60, 41,),
    7: (70, 3, 13,),
    8: (80, 23,),
    9: (90, 52, 33,),
    10: (100, 42,),
    11: (110,),
    12: (120, 71,),
    13: (130, 61, 4,),
    14: (140, 14,),
    15: (150, 81, 24,),
    AFTER_REDUCE_END: (53,),
    AFTER_LAST_0: (91, 34,),
    AFTER_LAST_2: (101,),
    LAST: (
        72, 43, 111, 131, 62, 121, 141, 5, 15, 25, 151, 54, 35, 82, 73, 92, 44, 102, 6, 112, 16, 132, 26, 63,
        122, 152, 142, 7, 55, 36, 17, 83, 27, 123, 74, 153, 93, 45, 8, 103, 37, 113, 133, 64, 143, 18, 56, 28,
        84, 124, 46, 75, 154, 94, 104, 38, 134, 114, 65, 144, 85, 57, 125, 76, 47, 155, 115, 66, 95, 105, 86, 135,
        145, 58, 126, 77, 156, 67, 87, 48, 127, 116, 96, 78, 106, 136, 146, 88, 117, 157, 97, 107, 137, 147, 68, 158,
        98, 128, 108, 138, 118, 148,
    ),
}


class Plan:
    def __init__(self, mesh, images, w_reduce, w_heads):
        self.tasks = mesh.shape["task"]
        self.dp = mesh.shape["dp"]
        self.line = self.dp // 2
        self.devices = self.tasks * self.dp
        assert self.tasks == 4 and self.dp % 2 == 0
        assert self.devices & (self.devices - 1) == 0
        self.count, self.height, self.span, self.wide = images.shape
        assert self.height & (self.height - 1) == 0 and self.height % 16 == 0
        self.mid = w_reduce.shape[1]
        self.heads = w_heads.shape[1]
        assert self.mid == 512 and self.heads == 768 and self.wide == 2048
        self.image = self.height * self.span
        self.cells = self.count * self.image
        self.step = self.image + self.height
        self.rows = self.count * self.step - self.height
        self.both = 2 * self.count * self.step - self.height
        self.half = self.wide // 2
        self.depth = -(-self.both // 256) * 256
        assert self.line & (self.line - 1) == 0
        self.levels = self.line.bit_length() - 1
        self.steps = 2 + self.levels
        unit = 16 << self.steps
        self.real = (
            self.heads // 256 * self.half,
            self.half // 256 * self.mid,
            9 * self.mid,
            self.mid // 256 * self.half,
        )
        tuned = self.steps == 4 and all(real % (n * unit) == 0 for real, n in zip(self.real, PARTS))
        self.parts = PARTS if tuned else (1, 1, 1, 1)
        self.base, self.first, self.segments, at = [], [], [], 0
        for real, n in zip(self.real, self.parts):
            self.base.append(at)
            self.first.append(len(self.segments))
            size = -(-real // (n * unit)) * unit
            for _ in range(n):
                index = len(self.segments)
                self.segments.append((index, at, size, ROUTES[index] if tuned else 0))
                at += size
        self.total = at
        self.agenda = AGENDA
        if not tuned:
            self.stride = 2 * self.steps + 1
            self.agenda = {i: (self.stride * i,) for i in range(4)}
            self.agenda[LAST] = [self.stride * i + k for k in range(1, self.stride) for i in range(4)]
        else:
            self.stride = 10


def chunk_of(rows):
    for size in (128, 96, 64, 48, 32, 16):
        if rows % size == 0:
            return size
    raise ValueError(rows)


def column_sum(values):
    return jnp.sum(values.reshape(values.shape[0] // 8, 8, values.shape[1]), axis=0)


def fold(part):
    return jnp.sum(part, axis=0, keepdims=True)


def logistic(values):
    return 0.5 + 0.5 * jnp.tanh(0.5 * values)


def lanes(block, width=128):
    return pl.ds(pl.multiple_of(block * width, width), width)


def span16(start, size):
    return pl.ds(pl.multiple_of(start, 16), size)


def repeat(count, body):
    def step(i, carry):
        body(i)
        return carry

    lax.fori_loop(0, count, step, 0)


def block_kernel(
    plan,
    images,
    sizes,
    limits,
    head_grad,
    w_reduce,
    w_spatial,
    w_expand,
    w_heads,
    gain_a,
    shift_a,
    gain_b,
    shift_b,
    gain_c,
    shift_c,
    head_out,
    grad_images,
    gathered,
    terms,
    received,
    gain_a_grad,
    shift_a_grad,
    gain_b_grad,
    shift_b_grad,
    gain_c_grad,
    shift_c_grad,
    *scratch,
):
    (
        wr,
        ws,
        we,
        wh,
        hg,
        trunk,
        sib_one,
        sib_two,
        img_t,
        merged,
        third,
        first,
        second,
        back,
        hid_a,
        hid_b,
        hid_b_t,
        low_b,
        low_b_all,
        gsc,
        mask,
        coef,
        msg,
        slots,
        count_msg,
        count_slots,
        wide_msg,
        wide_slots,
        total,
        load_sem,
        sum_send,
        sum_recv,
        sib_send,
        sib_recv,
        ring_send,
        ring_recv,
    ) = scratch
    img, stage, low_a = grad_images, head_out, hid_b
    p = plan
    n_img, height, image, step = p.count, p.height, p.image, p.step
    cells, rows, mid, wide, half = p.cells, p.rows, p.mid, p.wide, p.half
    mid_blocks, wide_blocks = mid // 128, wide // 128
    chunk = chunk_of(image)
    task = lax.axis_index("task")
    dp = lax.axis_index("dp")
    core = lax.rem(dp, 2)
    level = dp // 2
    me = task * p.dp + dp
    none = dp // p.dp

    def place(at_task, at_dp):
        return {"task": at_task, "dp": at_dp}

    sibling = place(task, dp + 1 - 2 * core)

    def remote(src, dst, send, recv, device):
        return pltpu.make_async_remote_copy(
            src_ref=src, dst_ref=dst, send_sem=send, recv_sem=recv, device_id=device, device_id_type=MESH
        )

    def take(ref, sem):
        pltpu.make_async_copy(ref, ref, sem).wait()

    barrier = pltpu.get_barrier_semaphore()

    def greet(i):
        other = me ^ (p.devices - 1 - i)
        pl.semaphore_signal(
            barrier,
            inc=1,
            device_id=place(other // p.dp, lax.rem(other, p.dp)),
            device_id_type=MESH,
        )

    loads = {
        "i0": (images.at[:, pl.ds(0, half)], img.at[:, pl.ds(0, half)]),
        "w0": (w_reduce.at[pl.ds(0, half)], wr.at[pl.ds(0, half)]),
        "i1": (images.at[:, pl.ds(half, half)], img.at[:, pl.ds(half, half)]),
        "w1": (w_reduce.at[pl.ds(half, half)], wr.at[pl.ds(half, half)]),
        "grad": (head_grad, hg.at[pl.ds(0, cells)]),
        "heads": (w_heads, wh),
        "limits": (limits, trunk),
        "expand": (w_expand, we),
    }
    order = list(loads)

    def load(key):
        pltpu.make_async_copy(*loads[key], load_sem.at[order.index(key)]).start()

    for key in order[:4]:
        load(key)
    repeat(p.devices - 1, greet)
    for key in order[4:]:
        load(key)
    for row_tap in range(3):
        for col_tap in range(3):
            pltpu.make_async_copy(
                w_spatial.at[row_tap * 3 + col_tap],
                ws.at[col_tap, pl.ds(row_tap * mid, mid)],
                load_sem.at[len(order)],
            ).start()

    def loaded(key):
        pltpu.make_async_copy(*loads[key], load_sem.at[order.index(key)]).wait()

    mask[...] = jnp.zeros_like(mask)
    for k in range(n_img):
        at = lax.broadcasted_iota(jnp.int32, (image, 128), 0)
        inside = ((at & (height - 1)) < sizes[k, 0]) & ((at // height) < sizes[k, 1])
        mask[pl.ds(k * step, image)] = jnp.where(inside, 1.0, 0.0)
    zero_rows = jnp.zeros((height, 3 * mid), LOW)
    for k in range(2 * n_img + 1):
        hid_a[pl.ds(k * step, height)] = zero_rows
    beyond = p.depth - p.both
    hid_a[pl.ds(p.both + 2 * height, beyond)] = jnp.zeros((beyond, 3 * mid), LOW)
    low_b_all[pl.ds(p.both, beyond)] = jnp.zeros((beyond, mid // 2), LOW)
    for k in range(n_img + 1):
        low_b[pl.ds(k * step, height)] = zero_rows
    low_b_all[pl.ds(rows, height)] = jnp.zeros((height, mid // 2), LOW)

    def to_all(k, src, dst):
        def send(i):
            other = me ^ (p.devices - 1 - i)
            device = place(other // p.dp, lax.rem(other, p.dp))
            remote(src, dst.at[me], sum_send.at[k], sum_recv.at[k], device).start()

        repeat(p.devices - 1, send)

    def from_all(k, dst):
        some = dst.at[pl.ds(0, p.devices - 1)]
        take(some, sum_recv.at[k])
        take(some, sum_send.at[k])

    def sum_start(k, slot):
        slots[slot, me] = msg[k]
        to_all(k, msg.at[k], slots.at[slot])

    def sum_finish(k, slot):
        from_all(k, slots.at[slot])
        total[pl.ds(0, 2 * mid_blocks)] = jnp.sum(slots[slot], axis=0)

    plane = 2 * p.tasks
    spot = task * 2 + core

    def wide_start(k):
        wide_slots[k, spot] = wide_msg[k, 0]
        for i in range(plane - 1, 0, -1):
            other = spot ^ i
            remote(
                wide_msg.at[k, 0],
                wide_slots.at[k, spot],
                sum_send.at[5 + 2 * k],
                sum_recv.at[5 + 2 * k],
                place(other // 2, level * 2 + lax.rem(other, 2)),
            ).start()

    def wide_turn(k):
        some = wide_slots.at[k, pl.ds(0, plane - 1)]
        take(some, sum_recv.at[5 + 2 * k])
        take(some, sum_send.at[5 + 2 * k])
        partial = jnp.sum(wide_slots[k, pl.ds(0, plane)], axis=0)
        wide_msg[k, 1] = partial
        wide_slots[k, plane + level] = partial
        for i in range(p.line - 1, 0, -1):
            other = level ^ i
            remote(
                wide_msg.at[k, 1],
                wide_slots.at[k, plane + level],
                sum_send.at[6 + 2 * k],
                sum_recv.at[6 + 2 * k],
                place(task, other * 2 + core),
            ).start()

    def wide_finish(k):
        some = wide_slots.at[k, pl.ds(plane, p.line - 1)]
        take(some, sum_recv.at[6 + 2 * k])
        take(some, sum_send.at[6 + 2 * k])
        total[...] = jnp.sum(wide_slots[k, pl.ds(plane, p.line)], axis=0)

    low_bit, high_bit = lax.rem(task, 2), task // 2
    along_x = (low_bit, place(task + 1 - 2 * low_bit, dp))
    along_y = (high_bit, place(task + 2 - 4 * high_bit, dp))
    along_z = []
    for k in range(p.levels):
        bit = lax.rem(level // 2**k, 2)
        along_z.append((bit, place(task, dp + 2 ** (k + 1) - 2 ** (k + 2) * bit)))

    def route(kind, part):
        one, two = (along_x, along_y) if part == 0 else (along_y, along_x)
        return (
            [one, two, *along_z],
            [one, *along_z, two],
            [*along_z, one, two],
            [one, *along_z[:1], two, *along_z[1:]],
            [*along_z[:1], one, *along_z[1:], two],
            [*along_z[:1], one, two, *along_z[1:]],
        )[kind]

    def held(segment, part, k):
        _, at, size, kind = segment
        for j, (bit, _) in enumerate(route(kind, part)[:k]):
            at = at + bit * (size >> (j + 1))
        return at

    def inbox(segment, k):
        _, at, size, _ = segment
        return at + size - (size >> k)

    def put(family, row, values):
        low = values.astype(LOW)
        at = span16(p.base[family] + row, low.shape[0])
        terms[0, at, :] = low[:, :128]
        terms[1, at, :] = low[:, 128:]

    def add_received(segment, part, at, rows_here, k):
        starts = [inbox(segment, j) + at - held(segment, part, j + 1) for j in range(k)]
        size = chunk_of(rows_here)

        def one(i):
            here = span16(at + i * size, size)
            acc = terms[part, here, :].astype(F32)
            for start in starts:
                acc = acc + received[part, span16(start + i * size, size), :].astype(F32)
            terms[part, here, :] = acc.astype(LOW)

        repeat(rows_here // size, one)

    def some_of(segment, rows_here):
        return received.at[:, pl.ds(segment[1], rows_here)]

    def ring(segment, k):
        at = k - p.steps - 1 if k > p.steps else k
        return ring_send.at[segment[0], 0], ring_recv.at[segment[0], at]

    def settle(segment, k, arrived, sent):
        send, recv = ring(segment, k)
        take(some_of(segment, arrived), recv)
        take(some_of(segment, sent), send)

    def beside(segment):
        return ring_send.at[segment[0], 1], ring_recv.at[segment[0], p.steps + 1]

    def home(part, start, rows_here):
        return gathered.at[core, part, span16(start, rows_here)]

    def scatter(segment, k):
        _, _, size, kind = segment
        here = size >> (k + 1)
        if k:
            settle(segment, k - 1, 2 * here, 2 * here)
        for part in range(2):
            bit, partner = route(kind, part)[k]
            at = held(segment, part, k) + (1 - bit) * here
            if k:
                add_received(segment, part, at, here, k)
            remote(
                terms.at[part, span16(at, here)],
                received.at[part, pl.ds(inbox(segment, k), here)],
                *ring(segment, k),
                partner,
            ).start()

    def gather(segment, k):
        _, _, size, kind = segment
        here = size >> (k + 1)
        if k == p.steps - 1:
            settle(segment, k, here, here)
        else:
            settle(segment, p.steps + k + 1, here // 2, here if k == p.steps - 2 else here // 2)
        for part in range(2):
            partner = route(kind, part)[k][1]
            at = held(segment, part, k + 1)
            mine = ours = home(part, at, here)
            if k == p.steps - 1:
                add_received(segment, part, at, here, p.steps)
                mine = terms.at[part, span16(at, here)]
                pltpu.make_async_copy(mine, ours, ring_send.at[segment[0], 0]).start()
            remote(mine, ours, *ring(segment, p.steps + k), partner).start()
            if k == 0:
                remote(ours, ours, *beside(segment), sibling).start()

    shared = []

    def share(segment):
        index, at, size, kind = segment
        settle(segment, p.steps, size // 2, size // 2)
        take(some_of(segment, size // 2), ring_send.at[index, 1])
        for part in range(2):
            bit = route(kind, part)[0][0]
            ours = home(part, at + (1 - bit) * (size // 2), size // 2)
            remote(ours, ours, *beside(segment), sibling).start()
        rows_here = pl.ds(at, size)
        pltpu.make_async_copy(gathered.at[core, :, rows_here], received.at[:, rows_here], ring_send.at[index, 0]).start()
        for other in shared[-1:]:
            bring(other)
        shared.append(segment)

    def bring(segment):
        index, at, size, _ = segment
        send, recv = beside(segment)
        take(some_of(segment, size), recv)
        take(some_of(segment, size // 2), send)
        rows_here = pl.ds(at, size)
        pltpu.make_async_copy(gathered.at[1 - core, :, rows_here], terms.at[:, rows_here], ring_send.at[index, 0]).start()

    def travel(point):
        for todo in p.agenda.get(point, ()):
            segment, k = p.segments[todo // p.stride], todo % p.stride
            if k < p.steps:
                scatter(segment, k)
            elif k < 2 * p.steps:
                gather(segment, 2 * p.steps - 1 - k)
            else:
                share(segment)

    other_half = pl.ds(pl.multiple_of((1 - core) * half, 128), half)
    other_quarter = pl.ds(pl.multiple_of(mid + (1 - core) * (mid // 2), 128), mid // 2)
    swaps = (
        (images.at[:, other_half], sib_one),
        (head_grad, hg.at[pl.ds(cells, cells)]),
        (hid_a.at[pl.ds(height, rows)], hid_a.at[pl.ds(n_img * step + height, rows)]),
        (hid_b.at[pl.ds(0, cells)], hid_b.at[pl.ds(cells, cells)]),
        (trunk.at[:, other_half], sib_two),
        (trunk.at[:, other_half], sib_one),
        (low_b.at[pl.ds(height, rows), other_quarter], low_b_all.at[pl.ds(rows + height, rows)]),
        (low_a.at[pl.ds(0, cells)], low_a.at[pl.ds(cells, cells)]),
    )

    def swap(k):
        src, dst = swaps[k]
        return remote(src, dst, sib_send.at[k], sib_recv.at[k], sibling)

    def put_stats(ref, at, blocks, block, one, two):
        ref[(*at, pl.ds(block, 1))] = fold(one)
        ref[(*at, pl.ds(blocks + block, 1))] = fold(two)

    count_msg[...] = fold(column_sum(mask[...]))
    count_slots[me] = count_msg[...]
    loaded("i0")
    loaded("w0")

    def first_layer(nb):
        front, rear = pl.ds(0, half), pl.ds(half, half)
        values = jnp.dot(img[:, front], wr[front, lanes(nb, 512)], preferred_element_type=F32)
        loaded("i1")
        loaded("w1")
        values = values + jnp.dot(img[:, rear], wr[rear, lanes(nb, 512)], preferred_element_type=F32)
        for h in range(4):
            one = two = jnp.zeros((8, 128), F32)
            for k in range(n_img):
                at = pl.ds(k * image, image)
                part = values[k * image : (k + 1) * image, h * 128 : h * 128 + 128]
                part = part * mask[pl.ds(k * step, image)]
                first[at, lanes(4 * nb + h)] = part
                one = one + column_sum(part)
                two = two + column_sum(part * part)
            put_stats(msg, (1,), mid_blocks, 4 * nb + h, one, two)

    first_layer(none)

    loaded("grad")
    loaded("heads")
    loaded("limits")
    head = p.heads // TASKS

    def merge(nb):
        at_wide = pl.ds(pl.multiple_of(nb * 256, 256), 256)
        for t in range(TASKS):
            at_head = pl.ds(t * head, head)
            values = lax.dot_general(
                hg[pl.ds(0, cells), at_head], wh[at_wide, at_head], NT, preferred_element_type=F32
            )
            gsc[t] = values.astype(LOW)

        def drop(i):
            at = span16(i * chunk, chunk)
            per = image // chunk
            valid = mask[span16(i // per * step + lax.rem(i, per) * chunk, chunk)]
            for h in range(2):
                grads = [gsc[t, at, pl.ds(h * 128, 128)].astype(F32) for t in range(TASKS)]
                signed, size, kept = 0.0, 0.0, 0.0
                for g in grads:
                    square = g * g + SOFT
                    signed = signed + g
                    size = size + square * lax.rsqrt(square)
                    kept = kept + jnp.tanh(g * 5.0) * g
                limit = trunk[at, lanes(2 * nb + h)].astype(F32)
                lean = jnp.tanh(2.5 + 2.5 * (signed / size) - 5.0 * limit)
                merged[at, lanes(2 * nb + h)] = (0.25 * valid) * (signed + lean * kept)

        repeat(cells // chunk, drop)

    blocks = wide // 256
    cuts = [0, blocks // 8, blocks * 5 // 8, blocks * 6 // 8, blocks]

    def merge_some(k):
        lax.fori_loop(cuts[k], cuts[k + 1], lambda i, carry: (merge(i), carry)[1], 0)

    merge_some(0)
    pl.semaphore_wait(barrier, p.devices - 1)
    to_all(0, count_msg, count_slots)
    sum_start(1, 1)
    swap(0).start()
    swap(1).start()
    merge_some(1)

    def turn_images(j):
        own = img[:, pl.ds(pl.multiple_of(core * half + j * 128, 128), 128)]
        both = jnp.concatenate([own, sib_one[:, lanes(j)]], axis=0)
        img_t[lanes(j), :] = both.T

    def center(blocks):
        mean = total[pl.ds(0, blocks)] / count
        spread = total[pl.ds(blocks, blocks)] / count - mean * mean + EPS
        coef[0, pl.ds(0, blocks)] = mean
        coef[1, pl.ds(0, blocks)] = lax.rsqrt(spread)

    def row(k, block):
        return coef[k, pl.ds(block, 1)]

    def edges():
        at = lax.broadcasted_iota(jnp.int32, (image, 128), 0) & (height - 1)
        return at != 0, at != height - 1

    def put_shifted(ref, start, block, values, above, below):
        at = pl.ds(start, image)
        up = jnp.where(above, pltpu.roll(values, 1, 0), 0.0)
        down = jnp.where(below, pltpu.roll(values, image - 1, 0), 0.0)
        for h, part in enumerate((up, values, down)):
            ref[at, pl.ds(pl.multiple_of(h * mid + block * 128, 128), 128)] = part.astype(LOW)

    from_all(0, count_slots)
    count = jnp.sum(count_slots[...], axis=0)
    sum_finish(1, 1)
    center(mid_blocks)
    coef[2, pl.ds(0, mid_blocks)] = coef[1, pl.ds(0, mid_blocks)]

    def normalize_a(cb):
        above, below = edges()
        gain, shift = gain_a[pl.ds(cb, 1)], shift_a[pl.ds(cb, 1)]
        for k in range(n_img):
            at = pl.ds(k * image, image)
            hat = (first[at, lanes(cb)] - row(0, cb)) * row(1, cb)
            first[at, lanes(cb)] = hat
            pre = hat * gain + shift
            hidden = pre * logistic(pre) * mask[pl.ds(k * step, image)]
            put_shifted(hid_a, height + k * step, cb, hidden, above, below)

    repeat(mid_blocks, normalize_a)
    swap(2).start()

    take(ws, load_sem.at[len(order)])

    def second_layer(nb):
        values = None
        for j in range(3):
            term = jnp.dot(
                hid_a[pl.ds(j * height, rows)], ws[j, :, lanes(nb, 512)], preferred_element_type=F32
            )
            values = term if values is None else values + term
        for h in range(4):
            part = values[:, h * 128 : h * 128 + 128] * mask[...]
            second[:, lanes(4 * nb + h)] = part
            put_stats(msg, (2,), mid_blocks, 4 * nb + h, column_sum(part), column_sum(part * part))

    second_layer(none)
    sum_start(2, 0)
    merge_some(2)
    swap(0).wait_recv()
    repeat(half // 128, turn_images)
    sum_finish(2, 0)
    center(mid_blocks)
    coef[3, pl.ds(0, mid_blocks)] = coef[1, pl.ds(0, mid_blocks)]

    def normalize_b(cb):
        gain, shift = gain_b[pl.ds(cb, 1)], shift_b[pl.ds(cb, 1)]
        for k in range(n_img):
            at = pl.ds(k * step, image)
            hat = (second[at, lanes(cb)] - row(0, cb)) * row(1, cb)
            second[at, lanes(cb)] = hat
            pre = hat * gain + shift
            hidden = pre * logistic(pre) * mask[at]
            hid_b[pl.ds(k * image, image), lanes(cb)] = hidden.astype(LOW)

    repeat(mid_blocks, normalize_b)
    swap(3).start()

    loaded("expand")

    def third_layer(nb):
        values = jnp.dot(hid_b[pl.ds(0, cells)], we[:, lanes(nb, 512)], preferred_element_type=F32)
        third[:, lanes(nb, 512)] = values
        for h in range(4):
            part = values[:, h * 128 : h * 128 + 128]
            put_stats(
                wide_msg, (0, 0), wide_blocks, 4 * nb + h, column_sum(part), column_sum(part * part)
            )

    repeat(wide // 512, third_layer)
    wide_start(0)
    merge_some(3)
    swap(3).wait()
    wide_turn(0)

    def turn_hidden(j):
        hid_b_t[lanes(j), :] = hid_b[:, lanes(j)].T

    repeat(mid_blocks, turn_hidden)
    wide_finish(0)
    center(wide_blocks)

    scale_c = gain_c[...] * coef[1]
    coef[7] = scale_c
    coef[8] = shift_c[...] - coef[0] * scale_c

    def normalize_c(i):
        cb = lax.rem(i + (1 - core) * (wide_blocks // 2), wide_blocks)
        one = two = jnp.zeros((8, 128), F32)
        for k in range(n_img):
            for r in range(image // chunk):
                at = pl.ds(k * image + r * chunk, chunk)
                valid = mask[pl.ds(k * step + r * chunk, chunk)]
                raw = third[at, lanes(cb)]
                pre = raw * row(7, cb) + (row(8, cb) + img[at, lanes(cb)].astype(F32))
                h = 0.5 * pre
                t = jnp.tanh(h)
                value = h + h * t
                trunk[at, lanes(cb)] = (value * valid).astype(LOW)
                up = merged[at, lanes(cb)] * ((1.0 + value) + t * (1.0 - value))
                merged[at, lanes(cb)] = up
                one = one + column_sum(up)
                two = two + column_sum(up * raw)
        put_stats(wide_msg, (1, 0), wide_blocks, cb, one, two)

    def both_halves(body, k, point):
        repeat(wide_blocks // 2, body)
        swap(k).start()
        travel(point)
        repeat(wide_blocks // 2, lambda i: body(i + wide_blocks // 2))

    both_halves(normalize_c, 4, None)
    wide_start(1)

    swap(1).wait_recv()
    swap(4).wait_recv()

    def heads_gradient(i):
        own = trunk[:, pl.ds(pl.multiple_of(core * half + i * 512, 128), 512)]
        both = jnp.concatenate([own, sib_two[:, lanes(i, 512)]], axis=0)
        values = lax.dot_general(both, hg[...], TN, preferred_element_type=F32)
        for q in range(2):
            for b in range(p.heads // 256):
                part = values[q * 256 : q * 256 + 256, b * 256 : b * 256 + 256]
                put(HEADS, (2 * i + q) * p.heads + b * 256, part)

    def each(family, first_part, last_part, count, body):
        n = p.parts[family]
        for i in range(first_part, last_part):
            body(i + none)
            for done in range(i * n // count, (i + 1) * n // count):
                travel(p.first[family] + done)

    each(HEADS, 0, half // 512, half // 512, heads_gradient)
    wide_turn(1)

    def head_layer(nb):
        values = jnp.dot(trunk[...], wh[:, lanes(nb, 256)], preferred_element_type=F32)
        stage[:, lanes(nb, 256)] = values.astype(LOW)

    for i, point in enumerate((AFTER_HEADS_0, AFTER_HEADS_1, AFTER_HEADS_2)):
        head_layer(i)
        travel(point)
    swap(4).wait_send()
    wide_finish(1)

    def backward(blocks, gain, inverse):
        scale = gain * inverse
        coef[4, pl.ds(0, blocks)] = scale
        coef[5, pl.ds(0, blocks)] = -scale * total[pl.ds(0, blocks)] / count
        coef[6, pl.ds(0, blocks)] = -scale * total[pl.ds(blocks, blocks)] / count

    sum_up = total[pl.ds(0, wide_blocks)]
    sum_up_hat = (total[pl.ds(wide_blocks, wide_blocks)] - coef[0] * sum_up) * coef[1]
    shift_c_grad[...] = sum_up
    gain_c_grad[...] = sum_up_hat
    per_hat = -coef[7] * sum_up_hat / count
    coef[4] = coef[7]
    coef[5] = -coef[7] * sum_up / count - per_hat * coef[1] * coef[0]
    coef[6] = per_hat * coef[1]

    def third_gradient(i):
        cb = lax.rem(i + (1 - core) * (wide_blocks // 2), wide_blocks)
        for k in range(n_img):
            for r in range(image // chunk):
                at = pl.ds(k * image + r * chunk, chunk)
                valid = mask[pl.ds(k * step + r * chunk, chunk)]
                down = merged[at, lanes(cb)] * row(4, cb) + row(5, cb) + third[at, lanes(cb)] * row(6, cb)
                trunk[at, lanes(cb)] = (down * valid).astype(LOW)

    both_halves(third_gradient, 5, AFTER_THIRD_0)
    travel(AFTER_THIRD_1)

    def slope_of(pre):
        gate = logistic(pre)
        return gate * (1.0 + pre * (1.0 - gate))

    def third_back(nb):
        values = lax.dot_general(trunk[...], we[lanes(nb, 512), :], NT, preferred_element_type=F32)
        for h in range(4):
            cb = 4 * nb + h
            one = two = jnp.zeros((8, 128), F32)
            for k in range(n_img):
                at = pl.ds(k * image, image)
                hat = second[pl.ds(k * step, image), lanes(cb)]
                pre = hat * gain_b[pl.ds(cb, 1)] + shift_b[pl.ds(cb, 1)]
                up = values[k * image : (k + 1) * image, h * 128 : h * 128 + 128]
                up = up * slope_of(pre) * mask[pl.ds(k * step, image)]
                back[at, lanes(cb)] = up
                one = one + column_sum(up)
                two = two + column_sum(up * hat)
            put_stats(msg, (3,), mid_blocks, cb, one, two)

    third_back(none)
    sum_start(3, 1)
    travel(AFTER_BACK_B_1)
    swap(5).wait_recv()

    def expand_gradient(i):
        own = trunk[:, pl.ds(pl.multiple_of(core * half + i * 512, 128), 512)]
        both = jnp.concatenate([own, sib_one[:, lanes(i, 512)]], axis=0)
        values = jnp.dot(hid_b_t[...], both, preferred_element_type=F32)
        for q in range(2):
            put(EXPAND, (2 * i + q) * mid, values[:, q * 256 : q * 256 + 256])

    each(EXPAND, 0, half // 512, half // 512, expand_gradient)
    travel(AFTER_EXPAND_END)
    sum_finish(3, 1)
    shift_b_grad[...] = total[pl.ds(0, mid_blocks)]
    gain_b_grad[...] = total[pl.ds(mid_blocks, mid_blocks)]
    backward(mid_blocks, gain_b[...], coef[3, pl.ds(0, mid_blocks)])

    def second_gradient(cb):
        above, below = edges()
        for k in range(n_img):
            at = pl.ds(k * step, image)
            down = back[pl.ds(k * image, image), lanes(cb)] * row(4, cb) + row(5, cb)
            down = (down + second[at, lanes(cb)] * row(6, cb)) * mask[at]
            put_shifted(low_b, height + k * step, cb, down, above, below)

    repeat(mid_blocks, second_gradient)
    swap(6).start()
    own_quarter = pl.ds(pl.multiple_of(mid + core * (mid // 2), 128), mid // 2)
    low_b_all[pl.ds(0, rows)] = low_b[pl.ds(height, rows), own_quarter]
    travel(AFTER_SECOND)

    def second_back(nb):
        values = None
        for i in range(3):
            for j in range(3):
                term = lax.dot_general(
                    low_b[pl.ds((2 - j) * height, rows), pl.ds((2 - i) * mid, mid)],
                    ws[j, pl.ds(pl.multiple_of(i * mid + nb * 512, 256), 512), :],
                    NT,
                    preferred_element_type=F32,
                )
                values = term if values is None else values + term
            travel((AFTER_TAP_0, AFTER_TAP_1, None)[i])
        for h in range(4):
            cb = 4 * nb + h
            one = two = jnp.zeros((8, 128), F32)
            for k in range(n_img):
                at = pl.ds(k * image, image)
                hat = first[at, lanes(cb)]
                pre = hat * gain_a[pl.ds(cb, 1)] + shift_a[pl.ds(cb, 1)]
                up = values[k * step : k * step + image, h * 128 : h * 128 + 128]
                up = up * slope_of(pre) * mask[pl.ds(k * step, image)]
                back[at, lanes(cb)] = up
                one = one + column_sum(up)
                two = two + column_sum(up * hat)
            put_stats(msg, (4,), mid_blocks, cb, one, two)

    second_back(none)
    sum_start(4, 0)
    travel(AFTER_BACK_A_1)
    swap(2).wait_recv()
    swap(6).wait_recv()
    def spatial_gradient(i):
        j, k = i // 2, lax.rem(i, 2)
        values = lax.dot_general(
            hid_a[span16(j * height, p.depth), lanes(k, 768)], low_b_all[...], TN, preferred_element_type=F32
        )
        put(SPATIAL, i * 768, values)

    each(SPATIAL, 0, 6, 6, spatial_gradient)
    sum_finish(4, 0)
    shift_a_grad[...] = total[pl.ds(0, mid_blocks)]
    gain_a_grad[...] = total[pl.ds(mid_blocks, mid_blocks)]
    backward(mid_blocks, gain_a[...], coef[2, pl.ds(0, mid_blocks)])

    def first_gradient(cb):
        for k in range(n_img):
            at = pl.ds(k * image, image)
            down = back[at, lanes(cb)] * row(4, cb) + row(5, cb) + first[at, lanes(cb)] * row(6, cb)
            low_a[at, lanes(cb)] = (down * mask[pl.ds(k * step, image)]).astype(LOW)

    repeat(mid_blocks, first_gradient)
    swap(7).start()
    travel(AFTER_FIRST)
    swap(7).wait_recv()

    def reduce_gradient(i):
        values = jnp.dot(img_t[lanes(i, 512), :], low_a[...], preferred_element_type=F32)
        for q in range(2):
            for b in range(mid // 256):
                part = values[q * 256 : q * 256 + 256, b * 256 : b * 256 + 256]
                put(REDUCE, (2 * i + q) * mid + b * 256, part)

    each(REDUCE, 0, half // 512, half // 512, reduce_gradient)
    travel(AFTER_REDUCE_END)
    each(SPATIAL, 6, 6, 6, spatial_gradient)
    travel(AFTER_SPATIAL_END)

    def first_back(nb):
        values = lax.dot_general(low_a[pl.ds(0, cells)], wr[lanes(nb, 512), :], NT, preferred_element_type=F32)
        for h in range(4):
            for k in range(n_img):
                at = pl.ds(k * image, image)
                part = values[k * image : (k + 1) * image, h * 128 : h * 128 + 128]
                part = (part + merged[at, lanes(4 * nb + h)]) * mask[pl.ds(k * step, image)]
                img[at, lanes(4 * nb + h)] = part.astype(LOW)

    for i, point in enumerate((AFTER_LAST_0, AFTER_LAST_1, AFTER_LAST_2, None)):
        first_back(i + none)
        travel(point)

    travel(LAST)
    bring(shared[-1])
    for index, at, size, _ in p.segments:
        take(gathered.at[:, :, pl.ds(at, size)], ring_send.at[index, 0])
    for k in (0, 1, 2, 5, 6, 7):
        swap(k).wait_send()


def run_block(plan, *arrays):
    p = plan
    cells, rows, mid, wide, half = p.cells, p.rows, p.mid, p.wide, p.half
    mid_blocks, wide_blocks = mid // 128, wide // 128
    anywhere = pl.BlockSpec(memory_space=pl.ANY)
    vmem = pl.BlockSpec(memory_space=pltpu.VMEM)
    smem = pl.BlockSpec(memory_space=pltpu.SMEM)
    shape = jax.ShapeDtypeStruct
    scratch = [
        pltpu.VMEM((wide, mid), LOW),
        pltpu.VMEM((3, 3 * mid, mid), LOW),
        pltpu.VMEM((mid, wide), LOW),
        pltpu.VMEM((wide, p.heads), LOW),
        pltpu.VMEM((2 * cells, p.heads), LOW),
        pltpu.VMEM((cells, wide), LOW),
        pltpu.VMEM((cells, half), LOW),
        pltpu.VMEM((cells, half), LOW),
        pltpu.VMEM((half, 2 * cells), LOW),
        pltpu.VMEM((cells, wide), F32),
        pltpu.VMEM((cells, wide), F32),
        pltpu.VMEM((cells, mid), F32),
        pltpu.VMEM((rows, mid), F32),
        pltpu.VMEM((cells, mid), F32),
        pltpu.VMEM((p.depth + 2 * p.height, 3 * mid), LOW),
        pltpu.VMEM((2 * cells, mid), LOW),
        pltpu.VMEM((mid, 2 * cells), LOW),
        pltpu.VMEM((rows + 2 * p.height, 3 * mid), LOW),
        pltpu.VMEM((p.depth, mid // 2), LOW),
        pltpu.VMEM((TASKS, cells, 256), LOW),
        pltpu.VMEM((rows, 128), F32),
        pltpu.VMEM((9, wide_blocks, 128), F32),
        pltpu.VMEM((5, 2 * mid_blocks, 128), F32),
        pltpu.VMEM((2, p.devices, 2 * mid_blocks, 128), F32),
        pltpu.VMEM((1, 128), F32),
        pltpu.VMEM((p.devices, 1, 128), F32),
        pltpu.VMEM((2, 2, 2 * wide_blocks, 128), F32),
        pltpu.VMEM((2, 2 * p.tasks + p.line, 2 * wide_blocks, 128), F32),
        pltpu.VMEM((2 * wide_blocks, 128), F32),
        pltpu.SemaphoreType.DMA((9,)),
        pltpu.SemaphoreType.DMA((9,)),
        pltpu.SemaphoreType.DMA((9,)),
        pltpu.SemaphoreType.DMA((8,)),
        pltpu.SemaphoreType.DMA((8,)),
        pltpu.SemaphoreType.DMA((len(p.segments), 2)),
        pltpu.SemaphoreType.DMA((len(p.segments), p.steps + 2)),
    ]
    return pl.pallas_call(
        functools.partial(block_kernel, plan),
        out_shape=(
            pltpu.VMEM((cells, p.heads), LOW),
            pltpu.VMEM((cells, wide), LOW),
            shape((2, 2, p.total, 128), LOW),
            *[pltpu.VMEM((2, p.total, 128), LOW)] * 2,
            *[pltpu.VMEM((mid_blocks, 128), F32)] * 4,
            *[pltpu.VMEM((wide_blocks, 128), F32)] * 2,
        ),
        in_specs=[anywhere, smem] + [anywhere] * 6 + [vmem] * 6,
        out_specs=[vmem] * 2 + [anywhere] + [vmem] * 8,
        scratch_shapes=scratch,
        compiler_params=pltpu.CompilerParams(
            collective_id=0, has_side_effects=True, vmem_limit_bytes=95 * 2**19
        ),
        name="block",
    )(*arrays)


def widen_kernel(plan, *refs):
    p = plan
    other, own, heads_in, images_in = refs[:4]
    small_in = refs[4:10]
    heads_out, images_out, out_reduce, out_spatial, out_expand, out_heads = refs[10:16]
    small_out = refs[16:22]
    reduce, spatial, expand, heads, out_sem, pass_sem = refs[22:]
    passes = (
        pltpu.make_async_copy(heads_in, heads_out, pass_sem.at[0]),
        pltpu.make_async_copy(images_in, images_out, pass_sem.at[1]),
    )
    for one in passes:
        one.start()
    for src, dst in zip(small_in, small_out):
        dst[...] = src[...]
    where = (
        (heads, out_heads, p.half, p.heads, True),
        (expand, out_expand, p.mid, p.half, False),
        (spatial, out_spatial, 9 * p.mid, p.mid // 2, False),
        (reduce, out_reduce, p.half, p.mid, True),
    )
    copies = []
    per_tap = p.mid // 256
    size = 256
    mine = lax.rem(lax.axis_index("dp"), 2)
    for s, (wide, out, height, width, by_rows) in enumerate(where):
        for low, core in ((own, mine), (other, 1 - mine)):
            row_at = core * height if by_rows else 0
            col_at = 0 if by_rows else core * width
            sem = out_sem.at[s, core]

            def one(i, s=s, wide=wide, out=out, low=low, row_at=row_at, col_at=col_at, sem=sem):
                rows = pl.ds(pl.multiple_of(row_at + i * size, size), size)
                for b in range(width // 256):
                    if s == EXPAND:
                        start = b * height + i * size
                    elif s == SPATIAL:
                        tap, sub = i // per_tap, lax.rem(i, per_tap)
                        start = (lax.rem(tap, 3) * 3 + tap // 3) * p.mid + sub * size
                    else:
                        start = i * width + b * size
                    src = pl.ds(pl.multiple_of(p.base[s] + start, size), size)
                    for part in range(2):
                        cols = pl.ds(pl.multiple_of(col_at + b * 256 + part * 128, 128), 128)
                        wide[rows, cols] = low[part, src, :].astype(F32)
                at = (rows, pl.ds(pl.multiple_of(col_at, 128), width))
                pltpu.make_async_copy(wide.at[at], out.at[at], sem).start()

            repeat(height // size, one)
            at = (pl.ds(pl.multiple_of(row_at, size), height), pl.ds(pl.multiple_of(col_at, 128), width))
            copies.append(pltpu.make_async_copy(wide.at[at], out.at[at], sem))
    for one in copies + list(passes):
        one.wait()


def widen(plan, head_out, grad_images, _, terms, received, *small):
    p = plan
    anywhere = pl.BlockSpec(memory_space=pl.ANY)
    vmem = pl.BlockSpec(memory_space=pltpu.VMEM)
    shape = jax.ShapeDtypeStruct
    full = ((p.wide, p.mid), (9 * p.mid, p.mid), (p.mid, p.wide), (p.wide, p.heads))
    held = (terms, received, head_out, grad_images, *small)
    return pl.pallas_call(
        functools.partial(widen_kernel, plan),
        out_shape=(
            shape(head_out.shape, LOW),
            shape(grad_images.shape, LOW),
            *(shape(one, F32) for one in full),
            *(shape(one.shape, F32) for one in small),
        ),
        in_specs=[vmem] * 10,
        out_specs=[anywhere] * 6 + [vmem] * 6,
        scratch_shapes=[
            *(pltpu.VMEM(one, F32) for one in full),
            pltpu.SemaphoreType.DMA((4, 2)),
            pltpu.SemaphoreType.DMA((2,)),
        ],
        compiler_params=pltpu.CompilerParams(vmem_limit_bytes=32 * 2**20),
        name="widen",
    )(*(pltpu.with_memory_space_constraint(one, pltpu.VMEM) for one in held))


def solution(mesh):
    cells_spec = P(("task", "dp"), None, None, None)

    def body(
        images,
        sizes,
        limits,
        head_grad,
        w_reduce,
        w_spatial,
        w_expand,
        w_heads,
        gain_a,
        shift_a,
        gain_b,
        shift_b,
        gain_c,
        shift_c,
    ):
        plan = Plan(mesh, images, w_reduce, w_heads)

        def flat(array):
            return array.transpose(0, 2, 1, 3).reshape(plan.cells, array.shape[3])

        def unflat(array):
            full = (plan.count, plan.span, plan.height, array.shape[1])
            return array.reshape(full).transpose(0, 2, 1, 3)

        outs = run_block(
            plan,
            flat(images),
            sizes,
            flat(limits),
            flat(head_grad),
            w_reduce,
            w_spatial.reshape(9, plan.mid, plan.mid),
            w_expand,
            w_heads,
            *(v.reshape(-1, 128) for v in (gain_a, shift_a, gain_b, shift_b, gain_c, shift_c)),
        )
        outs = widen(plan, *outs)
        return (
            unflat(outs[0]),
            unflat(outs[1]),
            outs[2],
            outs[3].reshape(w_spatial.shape),
            outs[4],
            outs[5],
            *(v.reshape(-1) for v in outs[6:]),
        )

    return jax.shard_map(
        body,
        mesh=mesh,
        in_specs=(cells_spec, P(("task", "dp"), None), cells_spec, cells_spec) + (P(),) * 10,
        out_specs=(cells_spec, cells_spec) + (P(),) * 10,
        check_vma=False,
    )
```
